512 devices in a mesh: brow: 32 (over y, x_lo, core), bcol: 16 (over z, x_hi).
Axes of the slice: x: 4 (x_hi: 2, x_lo: 2; x = x_hi * 2 + x_lo), y: 8, z: 8, core: 2. Of those that a mesh axis runs over, the one named last changes fastest.
Arguments:
- upper_store: bfloat16 [12288, 12288], P('brow', 'bcol'), may hold values from -0.21875 to 0.21875
- block_mask: int32 [96, 96], P('brow', 'bcol'), may hold values from 0 to 1, as said below
Outputs:
- product: bfloat16 [12288, 12288], P('brow', 'bcol')
The draws below stay inside these ranges and needn't reach their ends.
Inputs may be any that keep to these rules, and one draw needn't show every extreme that they name: block_mask is 1 on every diagonal block and 0 on every block below the diagonal.
All inputs are finite; a program needn't handle non-finite values.
Results may differ from the reference program's by a relative error of at most 0.001.
Values may be sent and summed in bfloat16 or wider, within the bound.
A program may use at most 64 MiB of HBM per device.

```python
import jax
import jax.numpy as jnp

BLOCK = 128
PB = 6
NBLK = 96
ORDER = 12288
N_BCOL = 16


def draw_block_mask(key, part):
    key = jax.random.fold_in(key, 11)
    row_ids = jnp.arange(NBLK, dtype=jnp.int32)[:, None]
    col_ids = jnp.arange(NBLK, dtype=jnp.int32)[None, :]
    offset = col_ids - row_ids
    distance = jnp.minimum(jnp.abs(offset), NBLK - jnp.abs(offset))
    limit = 1000 - 1800 * distance // NBLK
    rolled = jax.random.randint(key, (NBLK, NBLK), 0, 1000)
    kept = (rolled < limit) | (offset == 0)
    return jnp.where((offset >= 0) & kept, 1, 0).astype(jnp.int32)


def block_levels(own_key, extent, split, least, largest):
    def one(position, parts):
        heights = jax.random.uniform(jax.random.fold_in(jax.random.fold_in(own_key, 6), position), (parts,), jnp.float32, least / len(split), largest / len(split))
        return jnp.repeat(jnp.exp(heights), extent[position] // parts).reshape((-1,) + (1,) * (len(extent) - position - 1))

    level = one(*split[0])
    for cut in split[1:]:
        level = level * one(*cut)
    return level


def bell_draw(own_key, dims, scale, reach, split=(), kind=jnp.bfloat16):
    array = jax.random.normal(own_key, dims, jnp.float32) * scale
    if len(split) > 0:
        array = block_levels(own_key, dims, split, -0.22, 0.18) * array
    return jnp.clip(array, min=-reach, max=reach).astype(kind)


def setup_inputs(seed: int = 0) -> dict:
    seeds = jax.random.split(jax.random.key(seed), 3)
    upper_store = bell_draw(seeds[0], (ORDER, ORDER), (PB * BLOCK) ** -0.5, 0.21875, ((0, 32), (1, 16)))
    block_mask = draw_block_mask(jax.random.fold_in(seeds[2], 71), 0)
    return dict(upper_store=upper_store, block_mask=block_mask)


def reference(upper_store, block_mask):
    panels = N_BCOL
    width = PB * BLOCK
    nblocks = PB * panels
    keep_flags = block_mask.astype(jnp.bfloat16)
    masked = upper_store.reshape(nblocks, BLOCK, nblocks, BLOCK) * keep_flags[:, None, :, None]
    masked = masked.reshape(panels, width, panels, width)
    row_tiles = []
    for panel_row in range(panels):
        total = jnp.zeros((width, panels, width), jnp.float32)
        for step_index in range(2):
            columns = ((jnp.arange(panels) + step_index) % panels).astype(jnp.int32)
            partners = ((jnp.arange(panels) + panel_row) % panels).astype(jnp.int32)
            left_tiles = masked[panel_row][:, columns, :].astype(jnp.float32)
            right_tiles = masked[partners, :, columns, :].astype(jnp.float32)
            total = total + jnp.einsum('ick,cjk->icj', left_tiles, right_tiles)
        row_tiles.append(total.reshape(width, panels * width).astype(jnp.bfloat16))
    return jnp.concatenate(row_tiles, axis=0)
```

```python
import jax
import jax.numpy as jnp
from jax import lax
from jax.experimental import pallas as pl
from jax.experimental.pallas import tpu as pltpu
from jax.sharding import PartitionSpec as P

CHUNKS = 6
SLOTS = 44
SIB = 32
PLAN = (
    ((1, 12, 14, 16, 17, 29, 31, 194, 240, 256), 8, (83894272, 83894529, 83894786, 83895043, 83895300, 83895557, 101717272, 117450258, 102632219, 106697241, 117450772, 105647642, 101717789, 117451029, 117451543, 70193435, 117450515, 71178011, 117451286, 103681052)),
    ((2, 3, 15, 17, 18, 30, 31, 33, 195, 225, 227, 243, 257), 12, (68163584, 79828996, 82843905, 68163842, 68164099, 117514252, 117516308, 68225044, 117514766, 117516822, 67114757, 68162060, 117515280, 105714201, 69010969, 68162574, 68225558, 117517079, 103746842, 33554441, 69076762, 117516051, 68225815, 33554442, 117514509, 117515537, 103683352, 33554438, 117515023, 71176986, 33554439, 33554440, 117515794, 33554443, 117516565)),
    ((3, 13, 18, 19, 32, 34, 48, 49, 50, 51, 130, 226, 258), 9, (79894529, 67312131, 81860868, 81992197, 117580559, 68228367, 67175936, 101844761, 33554440, 117580045, 117580302, 33554438, 67176450, 33554443, 33554442, 33554439, 117581073, 117581844, 117579788, 33554441, 117581330, 105649176, 117582358, 117580816, 117582101, 117581587, 117582615)),
    ((2, 4, 20, 21, 26, 29, 33, 35, 37, 53, 54, 227, 229, 259), 8, (81926144, 68294661, 81926401, 67241986, 81926659, 67242500, 106698265, 100731162, 109647640, 33554440, 117647123, 117646609, 72159257, 33554439, 33554442, 33554438, 117645581, 117646352, 117646866, 33554443, 117647894, 117647637, 117645324, 33554441, 117645838, 117647380, 117646095, 117648151)),
    ((5, 12, 20, 21, 36, 52, 64, 66, 68, 82, 83, 228, 260), 8, (81991680, 68491265, 68425733, 81991939, 67307522, 117711374, 106631704, 67308036, 117711631, 72092696, 101911065, 101975578, 33554439, 117712402, 101975835, 68359182, 33554440, 33554442, 68359439, 117713687, 33554443, 117712659, 117710860, 117713430, 117711888, 117711117, 33554438, 117713173, 117712916, 117712145, 33554441)),
    ((6, 20, 22, 23, 37, 39, 65, 69, 71, 83, 84, 85, 131, 229, 261), 6, (68425986, 82057728, 67372801, 117776653, 82057987, 67373572, 68424461, 117776910, 67373829, 101911320, 68424718, 33554438, 117778966, 102041113, 33554441, 33554440, 117778195, 117776396, 33554442, 117778452, 117777167, 33554439, 117777681, 117777424, 117777938, 117778709, 117779223, 33554443)),
    ((7, 22, 23, 38, 40, 56, 70, 87, 98, 102, 114, 166, 196, 230, 262), 7, (68622339, 68622852, 67438080, 69540609, 102107416, 67438594, 117841932, 82124293, 68489740, 102107673, 33554439, 33554438, 117842703, 33554442, 68490511, 33554441, 117843474, 117842446, 33554443, 117843217, 117844502, 33554440, 117842189, 117844245, 117842960, 117844759, 117843731, 117843988)),
    ((8, 9, 22, 23, 28, 29, 39, 41, 71, 73, 101, 103, 112, 117, 118, 119, 167, 199, 231, 263), 8, (68556801, 82188292, 68557058, 67503616, 105713177, 67504387, 117907725, 67504901, 68555533, 33554442, 117909267, 117907982, 33554438, 102041624, 73143321, 117907468, 33554440, 117908496, 117909524, 33554441, 117908239, 107681562, 33554443, 117910038, 117908753, 117909010, 117909781, 33554439, 117910295)),
    ((9, 12, 24, 25, 38, 40, 57, 72, 119, 134, 136, 168, 184, 198, 232, 264), 12, (83367939, 67704836, 70785029, 78125312, 82254337, 68623106, 69671173, 102237977, 67569152, 33554439, 78126337, 33554442, 33554440, 78126594, 67569923, 117974546, 117974803, 33554443, 78126852, 105647896, 117973518, 117974032, 117975317, 73078040, 117975831, 117975574, 33554438, 117973775, 117973261, 117973004, 117975060, 33554441, 117974289)),
    ((8, 10, 11, 43, 59, 73, 88, 89, 137, 153, 201, 216, 233, 251, 265), 11, (82319360, 68687876, 75043077, 81205504, 67634945, 83106305, 67635202, 69605379, 101124632, 81336578, 67635973, 33554441, 81336836, 33554439, 33554442, 70720515, 118038540, 68686348, 118040853, 33554443, 118041367, 118039825, 33554438, 118039054, 118040596, 118038797, 118039311, 118041110, 118040082, 33554440, 118040339, 118039568)),
    ((11, 26, 27, 42, 58, 106, 164, 168, 170, 196, 202, 217, 219, 234, 236, 266), 10, (67835905, 74059523, 82188802, 67700995, 74059780, 67836165, 83564544, 67701252, 78256897, 102303512, 102370073, 83564805, 107614726, 33554439, 82385154, 118104076, 33554440, 33554442, 118104847, 118105361, 118106903, 118105618, 33554443, 33554441, 118106646, 118104333, 118106132, 118106389, 118104590, 118105104, 118105875)),
    ((10, 12, 13, 31, 43, 45, 165, 167, 171, 185, 186, 187, 218, 235, 250, 267), 14, (67765760, 68622593, 68818947, 83236867, 70916100, 82057474, 68884482, 67766017, 69868037, 101254936, 70851584, 82451457, 101255961, 70982660, 33554438, 33554441, 73076483, 118171411, 33554442, 33554440, 118170897, 33554439, 118169869, 118170126, 118171154, 118171925, 118172439, 118170640, 118172182, 118169612, 33554443, 118170383, 118171668)),
    ((13, 28, 29, 74, 192, 200, 202, 204, 215, 221, 236, 252, 268), 15, (67377152, 67966976, 67639299, 69933060, 70064641, 68491522, 67967490, 71112961, 67115522, 67832067, 102500376, 118235148, 71113220, 69146885, 68882956, 72092929, 118235919, 33554438, 111807769, 72093700, 33554442, 118237204, 118235405, 33554441, 118237718, 68883727, 33554439, 33554443, 118235662, 118236176, 33554440, 118237975, 118236690, 118237461, 118236947, 118236433)),
    ((12, 15, 28, 29, 30, 61, 193, 197, 205, 207, 214, 220, 235, 237, 241, 269), 14, (69474304, 83105793, 69015553, 67246082, 68950020, 69016322, 71110403, 68950277, 67896832, 70916612, 101385752, 67897603, 82189061, 102499865, 72158233, 101386266, 71110917, 118301712, 118302740, 70983168, 33554439, 102434587, 118301198, 118302226, 33554441, 33554438, 118301969, 33554442, 33554440, 118301455, 118302997, 118300941, 118303511, 118300684, 118303254, 33554443, 118302483)),
    ((15, 30, 31, 224, 238, 252, 254, 255, 270), 9, (69081088, 69015809, 71111939, 69081602, 71112196, 70127106, 118366734, 67116032, 70126849, 118367248, 102631449, 102565656, 68229376, 70127363, 82909701, 102697990, 118366220, 69014542, 70127620, 118366991, 33554440, 118368276, 69015056, 70128134, 118367505, 33554441, 118366477, 118368790, 118368019, 33554443, 118368533, 33554442, 33554439, 118367762, 118369047)),
    ((17, 30, 31, 222, 239, 240, 242, 255, 271), 14, (68027904, 69081348, 71047173, 69144066, 67180547, 69867780, 81795585, 69144323, 105715225, 69144837, 101716760, 104731930, 69077274, 101519899, 69143809, 67177752, 70192922, 103747612, 118432270, 69011993, 118432013, 69079821, 118433041, 69080849, 118431756, 118432784, 118432527)),
    ((0, 1, 15, 30, 208, 272), 4, (100667928, 100668441, 100668698, 118499605, 104730139, 118499091, 118498834, 104729628, 118499862, 118499348, 118500119, 104730909, 72160283)),
    ((1, 2, 14, 32, 47, 49, 51, 209, 241, 243, 273), 10, (67177472, 68098049, 67115011, 67177986, 80746756, 81861379, 67178500, 67116293, 67178757, 118565141, 103679768, 33554440, 118564884, 33554438, 71240984, 33554441, 33554439, 33554442, 118564627, 33554443, 104665625, 118565398, 118565655, 72225560, 118564370)),
    ((2, 3, 19, 35, 48, 50, 54, 146, 210, 229, 242, 274), 8, (80812032, 67179522, 69277953, 83040259, 67180036, 82909185, 81861632, 67180293, 100797208, 33554441, 33554442, 118629906, 118630163, 118630934, 33554439, 33554440, 118630677, 118631191, 118630420, 33554438, 33554443)),
    ((4, 5, 21, 28, 66, 81, 83, 85, 211, 243, 275), 7, (67246337, 80877570, 68290819, 68291076, 82974976, 82975237, 118696727, 102434328, 118696470, 33554442, 33554443, 33554441, 33554440, 118695956, 33554438, 118696213, 74125848, 118695699, 33554439, 118695442)),
    ((4, 5, 21, 26, 28, 65, 84, 131, 212, 244, 276), 9, (80943106, 67377412, 67442693, 83040512, 68491779, 100927513, 83040769, 106695706, 33554443, 118761235, 100862744, 118761749, 33554440, 108663067, 118761492, 33554438, 33554439, 33554442, 118762006, 118762263, 33554441, 118760978)),
    ((4, 5, 6, 7, 12, 20, 40, 87, 113, 213, 245, 277), 8, (67377664, 67377921, 83106050, 81008900, 68422405, 100861720, 83106563, 101910810, 106632217, 33554439, 118826514, 33554442, 33554438, 118827285, 118826771, 118827028, 33554440, 33554441, 118827799, 33554443, 118827542)),
    ((6, 7, 23, 54, 73, 112, 117, 118, 212, 246, 278), 6, (83171329, 67573762, 67442944, 81074436, 83171587, 101058328, 83171845, 33554441, 33554438, 101058585, 33554442, 118892050, 118892307, 118892564, 118892821, 33554440, 118893335, 33554439, 33554443, 118893078)),
    ((6, 8, 11, 24, 25, 55, 57, 89, 119, 147, 183, 198, 247, 279), 9, (81008641, 67508227, 67508484, 70654213, 68552192, 106630425, 100993304, 83237634, 100993562, 33554442, 101124123, 118958357, 33554439, 118957586, 33554438, 118958614, 118958871, 33554441, 118957843, 33554443, 118958100, 33554440)),
    ((8, 9, 25, 28, 43, 56, 73, 88, 216, 248, 280), 8, (70850561, 68753412, 83302403, 101190168, 70720002, 83302661, 33554442, 68617728, 33554439, 119023636, 33554443, 106696985, 33554438, 119023122, 119024407, 119024150, 119023893, 33554440, 119023379, 33554441)),
    ((10, 24, 26, 57, 59, 106, 169, 183, 185, 217, 219, 233, 281), 12, (67639553, 78190593, 76091396, 69802240, 81139971, 68684292, 70785536, 83368192, 102173208, 83368450, 70786051, 68684549, 80288773, 82385410, 119089172, 33554439, 80289027, 119088915, 33554440, 119089429, 119088658, 33554442, 33554443, 119089943, 119089686, 33554438, 33554441)),
    ((10, 11, 27, 42, 58, 167, 180, 186, 218, 235, 250, 282), 14, (83237120, 67770369, 70719491, 67311621, 70982146, 70523139, 68426501, 82384896, 33554438, 75107842, 33554440, 79305473, 71899650, 68749828, 119155479, 33554443, 33554441, 79305732, 101320984, 70851843, 68750085, 119154708, 119154451, 33554442, 119154965, 119155222, 33554439, 119154194)),
    ((11, 12, 13, 19, 28, 31, 203, 215, 221, 251, 283), 13, (82057217, 68814336, 72030464, 83630338, 67770629, 68814850, 83499267, 69933828, 68815107, 82123779, 69605637, 101320728, 70916868, 33554440, 69868289, 119219730, 119221015, 73076248, 119219987, 119220758, 33554441, 33554443, 33554439, 33554438, 119220501, 33554442, 119220244)),
    ((12, 13, 29, 44, 60, 205, 208, 214, 220, 236, 237, 246, 284), 15, (68360192, 69539841, 82122755, 68426240, 73141762, 82253828, 67574277, 71178241, 67967745, 68880386, 69146628, 101452312, 82516482, 73142019, 68688133, 101452569, 68880643, 73142276, 33554440, 33554442, 119285523, 68881157, 33554438, 33554443, 119285266, 33554439, 119285780, 119286037, 119286551, 119286294, 33554441)),
    ((1, 13, 14, 15, 30, 91, 253, 255, 285), 14, (67967232, 69998593, 67901442, 67574018, 67311876, 67115264, 71047429, 72158465, 83237379, 68946436, 104664344, 101517081, 33554440, 67897112, 104664603, 112858650, 119350802, 119351059, 33554441, 71111449, 78319642, 119352087, 67897371, 33554439, 119351316, 33554438, 33554442, 119351573, 119351830, 33554443)),
    ((0, 1, 14, 15, 31, 62, 240, 242, 254, 286), 13, (71175425, 68032513, 68098308, 69011458, 71175939, 82123269, 67180800, 69011715, 71176196, 68164354, 68164608, 69278977, 101516824, 102699033, 68164869, 83696901, 104732170, 101517338, 33554440, 33554441, 68028953, 70065667, 33554438, 33554443, 119416852, 33554439, 119417366, 119416595, 119416338, 119417623, 119417109)),
    ((12, 14, 15, 28, 30, 287), 14, (68032770, 69998850, 68098563, 71176704, 69077508, 67115781, 67181057, 68099076, 119480846, 70128654, 68028430, 119481103, 68028687, 70192642, 119481617, 68029201, 102435352, 119480332, 119480589, 101387033, 72093977, 119481360, 73078553)),
    ((34, 35, 44, 45, 47), 5, (100797720, 100799513, 68227864, 100798490, 68228634, 107744795, 107745820, 105780765, 70126109)),
    ((18, 30, 51, 52, 59, 61), 6, (100864792, 100733721, 109776666, 100863004, 105714461, 100863774, 108795419, 74256411)),
    ((35, 41, 45), 7, (69212161, 70391810, 67243779, 70326274, 70392325, 70457856, 69212676, 70327045, 107746585, 107746842, 110694424, 100800283)),
    ((51, 52, 62), 9, (69212418, 70392576, 75634945, 70260995, 70326532, 69344005, 101847832, 67308824, 100864538, 100865307, 107812121, 100863516, 100865821)),
    ((13, 59, 69), 3, (100930330, 105648664, 100930587, 110761241)),
    ((6, 28, 52, 59, 86), 5, (109776409, 100992795, 107680536, 100865050, 77206553, 110761500, 100996893, 76222492)),
    ((9, 27, 103), 5, (109581592, 67635480, 101061658, 107680025, 75110169)),
    ((8, 61, 86, 120), 3, (100996632, 101124889, 101127962, 107811099)),
    ((42, 44, 102, 137), 7, (101060888, 101193497, 68491032, 110695708, 107745562, 109710619, 76156700, 75175706)),
    ((25, 60, 120), 7, (69343236, 77139201, 77139715, 70589186, 77140229, 109644825, 83433472, 109778458, 101127448)),
    ((11, 15, 27, 63), 11, (70457344, 82188549, 70457601, 70785792, 76156418, 76156932, 104728600, 69737217, 101321498, 74061594, 103683609, 69737475, 102369051, 73077018)),
    ((12, 27, 60, 153, 154), 12, (70981637, 70719746, 71833857, 70851332, 101386776, 71834115, 82451968, 70720256, 73079553, 101256473, 75173635, 101257754, 109778716, 68686617, 107679771)),
    ((29, 31, 45, 125), 9, (74189824, 82712577, 70588418, 74190595, 69212930, 74190852, 69736965, 102500120, 104731673, 106761498, 74191642, 112989211)),
    ((12, 30, 61, 62, 92, 157, 188), 15, (71112704, 70850818, 73208069, 69343491, 69999105, 69343748, 108794904, 69213184, 71113475, 70982404, 74255896, 101386010, 104663068, 73272860, 101389851, 74257436, 111875609, 115086877, 105714974, 80547869)),
    ((0, 1, 14, 17, 31, 32, 42, 47, 48, 60, 160, 224, 241, 302), 6, (72223744, 71243777, 70588675, 72224772, 72225029, 72224258, 70326786, 72224515, 120463886, 71111694, 105780232, 120463629, 120465428, 105780489, 120464143, 120466199, 120464400, 33554439, 120465942, 120464914, 33554443, 120465685, 120464657, 120465171, 33554438, 120463372, 33554442)),
    ((0, 1, 15, 31, 62, 63, 92, 126, 303), 12, (70125570, 77600773, 70125827, 68229121, 71241218, 71241475, 105843737, 70261504, 71241732, 71173657, 69213444, 106828056, 104729116, 72290332, 120529679, 111875098, 120529422, 120528908, 73273881, 120529936, 112006683, 120529165, 73274908, 120530193)),
    ((35, 47, 51, 60, 62), 8, (101847576, 108794138, 100799769, 104795163, 107811612, 72225307, 70125083, 73272604)),
    ((34, 35, 46, 63), 4, (101782552, 100800025, 106763290, 105843996, 101783323)),
    ((34, 35, 51, 62, 63, 93), 6, (100797976, 109907993, 100798746, 77338137, 100799003, 106828573, 101848092, 71173917, 106827550)),
    ((34, 42), 10, (70260736, 70653956, 82123013, 69408769, 76683267, 70392834, 69278720, 110694936, 69409794, 69279235, 110695193, 100797466, 68227610)),
    ((26, 58, 68), 8, (69277697, 69540354, 69409280, 69409539, 70589444, 69410053, 100929818, 110758936, 78189080, 108662553)),
    ((41, 44, 46, 52, 62), 5, (106763545, 104663322, 100865564, 108729368, 110693915)),
    ((23, 51, 61), 4, (101848600, 67309592, 102107929, 108795674)),
    ((9, 24, 26, 43), 5, (109712409, 109647128, 108727323, 102172698, 75173401, 108597020)),
    ((8, 25, 42, 58, 60, 103), 8, (109580568, 109710363, 102237722, 109777693, 101062425, 111744798, 102238492, 75238685, 77205790)),
    ((11, 24, 26, 43, 45, 136), 8, (107746329, 102172440, 108728347, 101191194, 106630172, 76158491, 68621338, 102304029, 73207321)),
    ((11, 13, 27, 91), 13, (77204994, 70522880, 83630595, 79304961, 72751364, 101321240, 70786565, 104665114, 72095258, 102369819, 75109915, 112857625, 74061336, 78318617)),
    ((11, 13, 26, 43, 45, 62, 154), 13, (73013249, 69540098, 69474563, 69278211, 69540868, 108728600, 102303770, 83302917, 106762267, 82517504, 106631196, 101258009, 104664094, 76158744, 104662557, 104663583)),
    ((15, 29, 125), 12, (75239171, 82516224, 69934085, 70786305, 70261253, 102501145, 103683864, 69802500, 72159513, 79436546, 75239428, 73144089, 112004890, 79435034)),
    ((12, 13, 14, 17, 29, 45, 46, 53, 58, 59, 63, 241, 317), 12, (82581505, 70064130, 69278468, 121448725, 79502080, 73275651, 121447183, 121448982, 72094991, 67963157, 70654469, 106631961, 67963414, 69671685, 121446669, 33554439, 106632730, 121446926, 121447697, 121448468, 33554443, 106761240, 121448211, 33554440, 121447440, 106762011, 33554441, 121449239, 121446412, 33554438, 121447954, 33554442)),
    ((0, 1, 15, 16, 28, 30, 31, 42, 44, 47, 50, 63, 94, 318), 15, (72292356, 70195205, 72161792, 71244033, 69409027, 73272320, 70588931, 82778629, 71244293, 121512205, 70065154, 105845003, 121512719, 73273348, 121512976, 121513490, 70192146, 106695960, 69076498, 70982912, 70261761, 121514261, 33554440, 70393347, 70983428, 73275147, 33554438, 121514004, 121514518, 33554441, 33554442, 121512462, 121511948, 121513747, 121513233, 121514775, 33554439)),
    ((17, 46, 47, 48, 62, 160, 319), 11, (69867522, 73274627, 71174917, 70195456, 72289794, 106763032, 70393089, 70196228, 104662809, 72224024, 70327297, 121577998, 104663834, 121578255, 121578512, 121577741, 121578769, 121577484)),
    ((69, 78, 79, 92), 4, (100931352, 110891289, 107876379, 105777946, 74323738)),
    ((85, 93, 94), 3, (100995352, 68425496, 109907481, 109909786)),
    ((68, 74, 77), 4, (111808536, 100928538, 100928795, 68358682, 109843481)),
    ((91, 93), 2, (111873560, 109907737)),
    ((69, 74, 75, 76, 91), 9, (67374594, 72685573, 67374851, 72554756, 72423681, 100930072, 109842713, 71440896, 70523397, 71441153, 111807514, 100931101, 112858140, 111810331)),
    ((78, 86), 6, (71571456, 71309317, 69474817, 72489219, 71572740, 100995864, 69475074, 105711641, 100996378)),
    ((74, 103), 2, (101061144, 111808025, 111808794)),
    ((86, 91, 92, 120), 4, (111874840, 100996122, 111875865, 112858395, 78319387, 101126684)),
    ((43, 136, 137), 2, (101192472, 109712153, 109712666, 101190683, 101191964)),
    ((26, 119, 153), 5, (102109720, 67570712, 102241817, 109646874, 67702809)),
    ((77, 93), 8, (71440388, 71571968, 67901697, 71702786, 105646616, 71703045, 78253827, 106694681, 76289560)),
    ((27, 78, 92, 108, 140), 12, (72620036, 73078785, 77270530, 71572229, 83696132, 73079301, 107678745, 72882435, 109775128, 83565056, 72948483, 107677467, 106629404, 105712410, 75108889)),
    ((0, 2, 4, 8, 12, 31, 36, 58, 61, 74, 77, 92, 93, 230, 244, 332), 11, (73209859, 71571717, 82581761, 72685829, 82450948, 106694937, 76286976, 106694426, 106629144, 76287490, 33554442, 72948738, 33554439, 33554441, 77337881, 33554440, 122429709, 122431765, 33554438, 122430480, 122429452, 33554443, 122430994, 122432022, 122430223, 122429966, 122430737, 122431508, 122432279, 122431251)),
    ((1, 3, 7, 13, 15, 16, 29, 33, 45, 60, 62, 69, 75, 79, 93, 94, 95, 101, 229, 246, 333), 13, (73144321, 71440642, 71964676, 73210112, 73144578, 75304450, 82582019, 72423427, 73079044, 73210373, 106695448, 72091907, 77338392, 106759961, 122495245, 122497558, 73143053, 107811354, 33554439, 122494988, 122495502, 33554441, 122496530, 122496273, 33554442, 76353816, 122496016, 122497815, 33554440, 122496787, 33554443, 33554438, 122497301, 122495759, 122497044)),
    ((17, 32, 46, 48, 63, 64, 79, 95, 126, 160, 334), 13, (73340928, 73275393, 73734147, 82778116, 73341185, 75438339, 72030725, 72292864, 71637250, 73341444, 74322181, 122560524, 73208332, 74321153, 72686338, 122561552, 73209360, 74321410, 71310084, 122561809, 106825752, 74321667, 122561038, 106826521, 107876870, 122561295, 122560781, 122563351, 73209617, 107877127, 122562580, 33554442, 33554440, 122562837, 33554441, 33554443, 122562066, 122562323, 122563094)),
    ((47, 49, 62, 63, 78, 94, 95, 335), 13, (72222208, 75372546, 72222465, 75373059, 72555010, 73338884, 107812376, 73337856, 71309829, 122626574, 73274382, 73338113, 72424197, 107941147, 73338627, 75371291, 122626060, 122627345, 122626831, 106759705, 122627088, 105711130, 76354073, 122626317)),
    ((93, 94, 95), 3, (110892056, 106825498, 108925209)),
    ((68, 77, 79, 94), 4, (108859160, 101913369, 109909274, 106893595)),
    ((69, 93, 95), 5, (110891800, 100930841, 106826010, 74387226, 75371802)),
    ((68, 79, 86), 4, (101914137, 106892826, 67375129, 100995608)),
    ((75, 85, 92), 4, (111810072, 101979418, 67440410, 100995099, 68425243, 110891033)),
    ((68, 76, 78, 94), 8, (75700224, 67439873, 67440130, 72620547, 71374853, 72620804, 101914392, 106760474, 108860443, 110827289)),
    ((58, 91), 9, (72554496, 69670916, 71636993, 71768578, 71637507, 69541125, 111873304, 79303448, 111744537, 77205529)),
    ((102,), 2, (101060632, 68490776)),
    ((75, 153), 3, (101257496, 68687640, 111809817)),
    ((75, 76, 92, 136, 154), 5, (102176536, 110692889, 67704345, 106629914, 110825243, 110826524)),
    ((59, 92, 93, 123), 6, (110760728, 76221720, 106695194, 108660507, 110890265, 73074457)),
    ((4, 8, 11, 21, 23, 27, 31, 42, 43, 57, 59, 61, 75, 76, 77, 89, 90, 92, 122, 347), 12, (71505922, 69016068, 70916352, 72751105, 71572482, 71768835, 110824728, 108859417, 123412749, 33554440, 108727579, 123414034, 82517765, 123414291, 110825754, 33554438, 123413263, 33554441, 123414548, 123412492, 123415062, 33554442, 123413006, 78254872, 123413520, 123414805, 33554443, 123413777, 123415319, 33554439)),
    ((0, 3, 7, 20, 24, 28, 60, 62, 74, 76, 77, 90, 93, 246, 348), 15, (71768065, 72095746, 72620292, 70064388, 75110656, 70195714, 71309573, 71768325, 73013505, 77336323, 108858648, 72091416, 72031235, 123478542, 105646105, 72948229, 33554441, 33554443, 77336066, 33554439, 123478799, 73075204, 123479056, 33554438, 123480598, 33554442, 123479827, 123478285, 123478028, 76288792, 123479570, 123480855, 33554440, 123479313, 123480084, 123480341)),
    ((44, 45, 49, 53, 57, 59, 61, 63, 76, 77, 78, 79, 85, 94, 95, 349), 17, (76352769, 72357890, 72096003, 70392068, 72161285, 82254080, 72096257, 72488961, 71964930, 71506179, 73013764, 109842200, 123544849, 77272344, 71375106, 109842969, 73139712, 123545363, 33554440, 72091161, 109844250, 123545106, 72092442, 75303961, 33554439, 123546134, 74192657, 123545877, 123544592, 75305242, 123543821, 123545620, 33554438, 123543564, 123546391, 33554441, 123544335, 33554442, 123544078, 33554443)),
    ((45, 47, 48, 50, 61, 62, 63, 78, 79, 80, 82, 110, 126, 350), 16, (72161537, 74389506, 72292608, 75370500, 75369472, 73205762, 72686083, 123611413, 105711384, 82647809, 75369986, 72423939, 73341700, 72290069, 83761665, 75370243, 71375365, 73341957, 123609100, 71174421, 72358149, 33554438, 123610128, 123611156, 33554440, 108795161, 33554442, 33554443, 123610385, 123611927, 74256153, 123610899, 123609614, 33554441, 123610642, 33554439, 123611670, 123609871, 123609357)),
    ((78, 79, 81, 83, 94, 351), 13, (74323968, 82843653, 81861125, 72293121, 72226818, 75372036, 108859928, 72489475, 72227077, 74320920, 83827458, 123675664, 108860185, 72223248, 72358401, 123674636, 105712154, 123674893, 74323472, 123675150, 123675407, 106760731, 106760988, 123675921)),
    ((111,), 2, (107873816, 76419608, 109974297)),
    ((110, 126, 127), 3, (107809049, 112005656, 110039066)),
    ((103, 109), 2, (111940120, 101061401)),
    ((), 0, ()),
    ((), 0, ()),
    ((78, 110, 120, 125), 4, (105711896, 112005145, 101127706, 107808283)),
    ((), 6, (74520577, 79960066, 69736453, 67505152, 81074690, 67505923, 72816644, 67505409)),
    ((120,), 7, (77993987, 74586116, 70785285, 71702528, 73537793, 101127192, 69605890)),
    ((153,), 1, (110626584,)),
    ((122, 138), 2, (108594713, 109644056, 108595226, 108595483, 108595996)),
    ((10, 42, 58, 107, 108, 109, 122, 123, 170, 187, 228, 230, 234, 246, 251, 362), 8, (107678232, 101321754, 124396303, 75044111, 107743257, 124396560, 75044368, 68751898, 78385176, 33554441, 79369752, 33554439, 33554438, 124397074, 33554443, 33554440, 124398359, 33554442, 78386201, 124397588, 124396046, 124397331, 124395532, 124397845, 124398102, 124396817, 124395789)),
    ((7, 19, 37, 38, 43, 75, 106, 108, 109, 122, 125, 228, 229, 231, 235, 252, 363), 8, (74913792, 79367939, 75110912, 74914306, 79367425, 75111170, 75176196, 108595736, 79368453, 74057473, 33554440, 33554438, 33554442, 74058501, 33554441, 124461068, 112004121, 33554443, 124463381, 124461325, 33554439, 124463638, 124463124, 124462867, 124461582, 124461839, 124463895, 124462096, 124462610, 124462353)),
    ((32, 34, 40, 44, 57, 93, 106, 109, 124, 125, 172, 238, 364), 11, (74258432, 76158976, 74061828, 74123266, 74782978, 78384899, 74258691, 72030977, 78385413, 74259205, 124526604, 82451713, 108791832, 124527375, 75174412, 108792089, 124527632, 33554442, 33554440, 75175183, 78384642, 33554439, 75175440, 33554438, 124528660, 33554441, 124528917, 33554443, 124529174, 124528403, 124529431, 124526861, 124527118, 124527889, 124528146)),
    ((33, 35, 39, 45, 48, 77, 79, 94, 97, 101, 108, 125, 126, 157, 189, 236, 239, 253, 365), 12, (73537536, 75307008, 78385921, 74062082, 75175938, 75438595, 75241475, 77402116, 74189316, 77402373, 107677208, 107677977, 107678491, 124594710, 77401345, 33554439, 33554443, 74189573, 112004378, 33554442, 124592654, 124593682, 124594967, 124594196, 124592397, 124594453, 33554441, 33554440, 124593939, 124592911, 124592140, 124593425, 124593168, 33554438)),
    ((64, 78, 95, 96, 111, 113, 126, 127, 142, 238, 366), 13, (77402881, 75438083, 75372805, 83695874, 77403652, 73734912, 82713346, 76419333, 107940888, 73270808, 74521088, 76418305, 75371032, 73472259, 76419076, 124658961, 33554443, 109974536, 124657933, 108922905, 33554438, 109974793, 124658190, 124657676, 124658447, 124659732, 33554439, 124659218, 124659989, 124660246, 124658704, 124659475, 124660503, 75306769, 33554442)),
    ((79, 82, 94, 110, 126, 127, 225, 255, 367), 10, (75435522, 76420869, 73406464, 82713092, 73406721, 74319874, 110038041, 74521345, 74320131, 112006170, 74521600, 75435779, 124723212, 109909016, 75436036, 124723469, 124724240, 124724497, 124723726, 124723983)),
    ((119, 124, 126, 127), 6, (101125912, 112987161, 68556056, 108923418, 111022363, 77469210, 78452507)),
    ((102, 110, 111, 159), 6, (102044440, 110957082, 107874075, 108989468, 75435291, 112136217, 76418074)),
    ((103, 125), 2, (101062168, 112989721)),
    ((), 0, ()),
    ((124,), 2, (112988184, 80418328)),
    ((108, 119, 124), 5, (101126170, 113971736, 75171352, 112923673, 68556314)),
    ((119, 120), 2, (101126937, 102110232, 102111002)),
    ((107, 136), 10, (71899136, 74848258, 78059522, 74455043, 67570945, 74783236, 74848773, 80156677, 102176025, 67637017, 112921624, 112922138)),
    ((123, 124), 9, (74848513, 69801987, 73734660, 73865218, 113972249, 71769088, 108661274, 108660760, 69671429, 79433241)),
    ((9, 55, 105, 106, 107, 122, 170, 215, 217, 230, 244, 251, 377), 2, (125379857, 76027665, 33554439, 33554442, 125380885, 125381142, 33554438, 125378572, 33554440, 125380114, 33554441, 125380371, 125378829, 33554443, 125379086, 125381399, 125380628, 125379600, 125379343)),
    ((20, 26, 38, 52, 58, 75, 90, 92, 107, 120, 123, 125, 186, 228, 246, 250, 252, 378), 10, (74127364, 75040513, 73996544, 108791320, 73996802, 110890009, 107611674, 73997059, 73074201, 107612187, 73997317, 33554438, 79434264, 33554442, 125444108, 125444622, 33554441, 33554440, 125446164, 33554443, 78320153, 33554439, 125445907, 125445393, 125446421, 125446678, 125445650, 125444365, 125445136, 125444879, 125446935)),
    ((40, 43, 53, 55, 57, 59, 91, 107, 108, 109, 117, 124, 125, 238, 379), 8, (74979330, 74979844, 75105792, 73014017, 75106563, 110956056, 125510929, 33554440, 75107077, 112922649, 33554439, 74058265, 33554441, 112004634, 33554442, 125511186, 125510672, 33554443, 125511957, 33554438, 125512214, 125509901, 125510415, 125511700, 125509644, 125511443, 125510158, 125512471)),
    ((33, 45, 48, 54, 56, 60, 94, 108, 109, 122, 125, 126, 139, 188, 189, 235, 236, 380), 10, (74782720, 79432961, 75307265, 74979586, 79433475, 74717188, 75307524, 74455296, 75171842, 75307781, 125575951, 76223759, 75172099, 79433989, 125577236, 33554438, 107743512, 33554440, 33554441, 33554443, 112988935, 125576465, 125576208, 125575180, 125577493, 125576722, 125576979, 125578007, 125575694, 33554442, 125577750, 125575437)),
    ((77, 81, 85, 91, 92, 93, 95, 109, 110, 124, 126, 127, 173, 237, 239, 381), 14, (75110400, 75237121, 74192898, 73734404, 74127616, 74258945, 74193155, 74586372, 76224773, 75176450, 71047683, 108726041, 69999362, 75373316, 125641230, 107742744, 108726810, 108727067, 125642258, 125640973, 33554439, 77401112, 125641487, 33554440, 125641744, 125642515, 125643286, 125643029, 125640716, 33554441, 33554438, 33554442, 125642001, 125642772, 33554443, 125643543)),
    ((79, 80, 82, 94, 95, 110, 112, 125, 127, 142, 158, 240, 254, 255, 382), 16, (78451457, 82647043, 77466624, 74390018, 75438848, 77466881, 70195972, 107809561, 73472000, 77467138, 75439108, 125707280, 75302914, 77467652, 74455813, 75439365, 125706252, 125708822, 73271830, 74387478, 33554443, 107877400, 125706766, 125707794, 72222744, 107877658, 125707023, 111022598, 72223002, 125709079, 33554441, 125708051, 33554440, 76355088, 33554442, 33554439, 108792347, 125706509, 125708308, 125708565, 125707537)),
    ((78, 109, 110, 111, 113, 126, 142, 383), 13, (74389760, 77469445, 74324226, 76421379, 83761409, 125772302, 110957848, 83827202, 74455556, 110956314, 75367936, 73472516, 76418840, 108860697, 125772559, 108856859, 125772816, 125773073, 108857884, 78386458, 125771788, 125772045, 108858141)),
    ((140, 142, 143), 3, (114037017, 112071704, 112070171, 112072474, 76417818)),
    ((158, 159), 3, (114103064, 112135962, 113121049, 78582041)),
    ((35, 139, 143), 4, (112071450, 100799257, 109709848, 76416794)),
    ((85, 158), 3, (100994072, 114102809, 68424216)),
    ((140, 141), 1, (114036760, 114038041)),
    ((157, 158), 2, (114103577, 114102040, 81532184)),
    ((137, 139), 2, (101192984, 109709593)),
    ((), 0, ()),
    ((38, 56, 121, 137, 152, 153, 168, 184, 217, 232, 244, 248, 392), 11, (76748800, 74914051, 79173636, 80091137, 70851074, 79108356, 72947717, 71834368, 71834629, 110627608, 33554443, 101193226, 126363154, 126364439, 126361612, 126362897, 33554441, 33554438, 126362383, 33554439, 126363925, 126363668, 126361869, 126362126, 126363411, 126364182, 126362640, 33554440)),
    ((3, 25, 41, 55, 73, 105, 138, 153, 154, 169, 186, 201, 233, 393), 11, (78125056, 71833601, 76024324, 77076485, 82319618, 75896835, 69736709, 78125825, 79174146, 126428176, 77075984, 33554438, 76024067, 33554440, 101258264, 126427405, 33554439, 33554442, 77137944, 33554443, 126427148, 33554441, 126429975, 126428690, 126429461, 126428947, 126429204, 126427662, 126427919, 126429718, 126428433)),
    ((40, 42, 55, 56, 57, 59, 72, 108, 130, 134, 139, 154, 155, 230, 234, 394), 7, (77142017, 77207557, 76088832, 73996291, 76089346, 112923160, 76089860, 110757401, 78384152, 110758682, 33554438, 126493198, 77141006, 33554443, 33554439, 126493712, 77141520, 33554440, 126493969, 126494483, 126492684, 126494997, 126494740, 33554442, 126495254, 33554441, 126495511, 126494226, 126492941, 126493455)),
    ((33, 37, 41, 43, 56, 75, 90, 124, 125, 140, 141, 154, 157, 188, 235, 247, 395), 9, (75634692, 77207813, 76154368, 75897091, 76154625, 108792601, 33554440, 76154882, 33554438, 33554442, 78450969, 110692120, 33554443, 126560533, 126558734, 33554439, 79435545, 33554441, 126558477, 126560019, 126558991, 126559762, 126560790, 126561047, 126560276, 126558220, 126559505, 126559248)),
    ((66, 68, 74, 76, 92, 93, 141, 154, 156, 157, 234, 236, 396), 10, (80481280, 76355584, 72030211, 75765764, 76220418, 76355845, 77404417, 76220932, 110888728, 80481537, 75503877, 110889497, 80481794, 33554440, 126624527, 33554438, 33554442, 126623756, 77271564, 80482051, 126624270, 126625041, 126625298, 33554439, 126626583, 126624784, 33554441, 33554443, 126626326, 126625555, 126624013, 126625812, 126626069)),
    ((50, 65, 67, 77, 79, 81, 93, 111, 126, 140, 143, 156, 158, 159, 173, 189, 231, 237, 397), 9, (77404160, 77273089, 77338626, 75766019, 77208065, 77338884, 79499268, 109774360, 126689549, 77404677, 109775641, 79498754, 79499011, 110823450, 33554441, 76286211, 33554443, 126691348, 126690320, 126689292, 126691605, 33554439, 126689806, 126690577, 126691862, 126690063, 33554440, 126690834, 33554438, 33554442, 126691091, 126692119)),
    ((96, 110, 111, 113, 127, 128, 130, 143, 158, 159, 238, 398), 16, (77535232, 77469698, 79500547, 77535489, 76879874, 77469956, 78452997, 76487424, 78515457, 76749060, 126757655, 74320663, 78515971, 110954520, 111023385, 76618241, 78516485, 126756113, 75368729, 76484377, 75504386, 112072202, 126755085, 75436311, 111020570, 77403921, 79566362, 126756370, 126755856, 33554438, 33554440, 126756884, 126757398, 126755599, 126756627, 126757141, 33554441, 126755342, 33554439, 126754828, 33554443)),
    ((97, 111, 142, 158, 159, 254, 255, 399), 11, (77532160, 77470210, 75503618, 75635201, 77470467, 76417540, 114103832, 77532417, 75504133, 77533188, 110955289, 111019546, 78580762, 126820364, 77533445, 126821649, 79564824, 79565338, 126821135, 80549657, 109905435, 126820621, 126821392, 126820878)),
    ((158, 159), 2, (113119000, 111020825)),
    ((142, 157, 158), 4, (115086104, 80547096, 113054490, 110954265, 110954779)),
    ((51,), 1, (101848344,)),
    ((136, 142), 3, (102175256, 112070681, 79500825)),
    ((), 0, ()),
    ((142, 157), 3, (114102553, 113054744, 81532697)),
    ((153, 157), 3, (115085848, 110627097, 110627354, 80546840)),
    ((), 0, ()),
    ((104, 136, 137, 150, 155, 169, 184, 201, 214, 216, 248, 408), 3, (109579032, 110757913, 127412758, 33554440, 33554441, 33554443, 127411987, 110758426, 127412501, 33554442, 127411730, 127412244, 33554439, 33554438, 127413015)),
    ((34, 40, 41, 51, 53, 89, 137, 138, 139, 154, 185, 230, 249, 409), 11, (69933313, 81270786, 81271043, 76945667, 72882181, 76027909, 67701760, 71899396, 76945924, 109643544, 73930753, 33554438, 127475981, 79174400, 127476495, 127477009, 127477266, 127477780, 33554441, 33554439, 127477523, 127478294, 33554440, 33554442, 127476752, 127476238, 127478037, 127475724, 127478551, 33554443)),
    ((36, 37, 52, 56, 58, 86, 90, 138, 139, 141, 152, 155, 186, 235, 247, 252, 410), 12, (70981889, 76224513, 76093442, 80287747, 69933568, 77137408, 80288005, 79239427, 127541774, 109710105, 72947972, 79239685, 78189582, 109644568, 33554439, 127543059, 109840154, 33554438, 33554441, 33554440, 33554443, 127541517, 33554442, 127541260, 127543316, 127543573, 127543830, 127542288, 127542545, 127542031, 127544087, 127542802)),
    ((75, 85, 89, 91, 93, 140, 141, 156, 157, 234, 236, 251, 253, 411), 7, (76159232, 77076738, 76159493, 77203201, 77076996, 113052952, 33554438, 77203715, 127607310, 78255118, 33554439, 33554442, 127607053, 127609109, 80483096, 127608595, 33554440, 127608338, 33554441, 33554443, 127608081, 127607567, 127607824, 127609366, 127606796, 127609623, 127608852)),
    ((50, 64, 76, 77, 80, 82, 84, 90, 92, 122, 140, 141, 157, 173, 231, 412), 7, (77268480, 77268737, 76356098, 77269508, 109840408, 80483352, 109840921, 77404931, 33554439, 127673103, 33554438, 33554442, 127675159, 127674388, 78320911, 127672332, 77269765, 33554441, 127672846, 33554443, 127673617, 127674902, 33554440, 127674645, 127674131, 127672589, 127673360, 127673874)),
    ((109, 110, 113, 123, 125, 127, 140, 141, 142, 143, 145, 156, 158, 159, 253, 413), 15, (76945408, 76290049, 78452738, 75831299, 76290308, 76880133, 77334016, 76617729, 114037272, 127739667, 74254099, 79498264, 76285464, 127738896, 127740438, 74254870, 78386704, 109774617, 77334787, 127739153, 127740181, 70065412, 78386961, 77335301, 33554440, 127738639, 113053978, 33554443, 127738382, 110823707, 33554442, 76286746, 127738125, 127739410, 127740695, 80484122, 127737868, 33554438, 33554439, 127739924, 33554441)),
    ((112, 126, 127, 142, 143, 144, 159, 190, 237, 254, 255, 414), 14, (76421122, 75831555, 76486660, 75700480, 79564290, 76486917, 79563776, 75569153, 77535748, 127806231, 75369239, 76484887, 79564033, 76617985, 127803404, 111087130, 76552195, 79565061, 127803661, 76417050, 33554439, 112071963, 76618499, 127803918, 77532955, 127805717, 33554440, 113120521, 127804432, 76417307, 33554438, 77399552, 33554442, 127804946, 109905944, 127805460, 127804689, 109906457, 127804175, 127805974, 33554443, 127805203)),
    ((142, 143, 158, 415), 12, (79565569, 76487168, 79565826, 74520836, 112069656, 77465859, 76421636, 75569413, 127868940, 79499800, 76416524, 75569667, 78516748, 110955034, 76552453, 127869197, 127869454, 127869968, 127870225, 109905689, 127869711)),
    ((47, 175), 5, (105781016, 71242008, 70126360, 112069145, 80614937)),
    ((174, 190, 191), 3, (116200728, 114232858, 112002841)),
    ((175,), 1, (114168344, 114169625)),
    ((191,), 1, (114232600,)),
    ((170, 171), 1, (101322520, 101324313)),
    ((172, 174, 188), 3, (112003609, 101389336, 111872794)),
    ((103,), 1, (101061912,)),
    ((119, 187), 3, (101125656, 101387545, 68817689, 101387290)),
    ((8, 137, 171), 4, (101192216, 109579289, 101324570, 78252826, 76023320, 109578011, 109579549, 109579806, 109580319, 111807004)),
    ((25, 52, 56, 86, 154, 170, 183, 185, 186, 201, 252, 425), 4, (109645080, 77075224, 102307595, 33554441, 128526356, 33554439, 128526099, 33554442, 33554438, 128526870, 33554440, 128527127, 128525842, 128526613)),
    ((10, 12, 66, 68, 70, 74, 84, 88, 91, 155, 168, 171, 186, 187, 202, 251, 426), 13, (74062336, 81467394, 77862915, 81336321, 79108099, 80288257, 78187269, 112854552, 112854809, 67768581, 79239940, 112855578, 82582788, 79240192, 33554443, 108598043, 79240450, 128591892, 128592406, 128590864, 33554438, 33554440, 128590093, 33554439, 33554441, 128589836, 128590607, 74059035, 128592149, 128592663, 128590350, 33554442, 128591121, 128591635, 128591378)),
    ((29, 45, 47, 58, 67, 71, 86, 122, 156, 165, 172, 173, 188, 189, 235, 427), 10, (79960322, 77863172, 82450688, 79304704, 78125573, 82451201, 79305217, 33554441, 80353795, 78126084, 33554442, 112920088, 67834392, 78252034, 128657171, 33554438, 128658199, 128656400, 33554439, 128655629, 128657685, 128655886, 33554440, 128657428, 128656143, 128656914, 128657942, 33554443, 128655372, 128656657)),
    ((98, 106, 108, 109, 127, 138, 157, 174, 184, 188, 189, 234, 428), 10, (78317827, 79501313, 78318084, 78453248, 79501570, 77928965, 128722707, 74188563, 112986136, 128721679, 112002585, 33554440, 128722193, 80612377, 128720908, 33554441, 79369487, 128723478, 81596953, 128721936, 128722450, 33554443, 128721422, 79370001, 128723735, 33554438, 33554439, 128722964, 128723221, 33554442, 128721165)),
    ((47, 60, 97, 101, 107, 109, 111, 112, 123, 126, 139, 142, 157, 161, 165, 172, 175, 190, 205, 237, 429), 11, (79435778, 81595906, 79436035, 81596163, 79501824, 79173892, 81596420, 79436293, 128788243, 75302675, 115086360, 79502337, 109906713, 81596677, 111871514, 80547352, 33554441, 33554440, 128788500, 79501081, 77334552, 33554443, 128788757, 33554438, 128787729, 128787472, 128786701, 128786444, 128786958, 128787215, 128789014, 33554442, 128787986, 128789271, 33554439)),
    ((128, 130, 142, 147, 158, 159, 160, 175, 190, 191, 206, 430), 12, (79566850, 80549891, 79632388, 78977029, 80612609, 77928708, 78584069, 78387456, 80612866, 78715138, 80613123, 77666561, 80613380, 113184521, 128852237, 128851980, 80613637, 113051416, 128852751, 33554439, 33554440, 80614665, 113051673, 128853265, 128853522, 128854550, 128854293, 128853779, 128853008, 33554442, 33554438, 33554443, 128854036, 128852494, 128854807)),
    ((113, 129, 143, 174, 190, 191, 431), 10, (79629569, 77731840, 80614402, 78514435, 79629312, 77732101, 77601028, 79630597, 79629826, 115215896, 112003865, 128917773, 79630340, 82646040, 128918030, 114233114, 128917516, 128918287, 128918544, 128918801)),
    ((189, 190, 191), 2, (112985880, 112986649, 115215386, 115216156, 115217435)),
    ((174, 190), 3, (116199960, 115151897, 79496728)),
    ((191,), 2, (113116952, 81662744)),
    ((), 0, ()),
    ((187, 190), 2, (116200985, 102371864)),
    ((174,), 1, (115152664,)),
    ((), 0, ()),
    ((136, 170), 3, (111741208, 68752664, 102176281)),
    ((136, 137, 153, 173), 4, (101191704, 110626331, 109578266, 111938073)),
    ((154, 170, 188), 5, (112920856, 67835160, 110692633, 111741467, 68752923, 111740444, 111740957, 110693146)),
    ((26, 29, 58, 68, 71, 86, 170, 171, 187, 218, 235, 442), 8, (102373131, 67834123, 33554438, 110759193, 111805976, 78189337, 33554439, 33554441, 33554440, 111806234, 33554442, 129640982, 109646619, 109647388, 129640211, 129640468, 129640725, 75107611, 129639954, 75108380, 129641239)),
    ((106, 107, 117, 119, 123, 138, 171, 172, 185, 188, 189, 219, 234, 443), 10, (78911488, 78256128, 83499012, 79301381, 78059777, 78256385, 81401858, 78060032, 78256644, 129704719, 74057999, 79300867, 82516995, 129704205, 129705490, 33554441, 129705233, 101390091, 33554439, 33554438, 33554440, 129704976, 129706518, 129706261, 129706004, 129706775, 33554442, 129703948, 129704462, 129705747)),
    ((44, 60, 112, 114, 116, 120, 122, 124, 139, 172, 173, 176, 189, 444), 13, (82515969, 77928450, 79239171, 81467649, 79366917, 78321664, 70064900, 111937560, 129769741, 79502596, 129770255, 80418063, 79366146, 111937817, 80417549, 111938330, 33554440, 33554438, 129770769, 80418577, 33554439, 33554441, 33554443, 129770512, 129769484, 109777947, 129771026, 33554442, 75238939, 129771283, 129772311, 129772054, 129769998, 129771797, 129771540)),
    ((61, 141, 142, 145, 147, 149, 155, 157, 159, 172, 173, 174, 177, 188, 191, 213, 445), 11, (78649345, 78387202, 78649604, 129837333, 76351765, 79431168, 129836048, 80483856, 79431939, 115149850, 129835277, 79432453, 129835020, 115150108, 129836562, 108794395, 111871768, 78382618, 129835534, 33554441, 111872025, 78382876, 129835791, 33554439, 33554442, 33554443, 112921117, 129837847, 129836305, 33554440, 74255387, 129837590, 129837076, 129836819, 33554438)),
    ((129, 142, 143, 144, 158, 159, 174, 178, 191, 206, 222, 446), 14, (78518273, 78583810, 81074181, 81661185, 78518530, 78911748, 78714880, 79632643, 81661956, 129902355, 77465363, 78581011, 112003096, 79764225, 77666307, 79632900, 129901070, 129902612, 77465620, 78581268, 80548878, 78649856, 129900556, 33554438, 78650371, 81662213, 129900813, 33554439, 33554442, 115217673, 129901841, 33554440, 33554443, 129901584, 129902869, 129903126, 129902098, 129903383, 129901327)),
    ((174, 175, 190, 447), 12, (80615424, 78780417, 81663492, 79563011, 81663749, 129966349, 80614157, 77797377, 78584323, 78513933, 115152408, 79562754, 78650114, 129966092, 113051929, 77666818, 129967377, 113052186, 129966606, 129966863, 78513676, 129967120, 78514961)),
    ((205, 206, 207), 3, (101455384, 116263961, 116265754, 80611098, 116266779, 80612123)),
    ((190, 206, 221, 222), 3, (116200219, 101518361, 114101016, 101520154)),
    ((1, 207), 2, (116266009, 100668952)),
    ((2,), 1, (100730648,)),
    ((102, 171, 205), 3, (101060120, 114035226, 101323801)),
    ((206, 222, 223), 3, (114099736, 116330266, 114099995, 101521177)),
    ((136,), 2, (102175512, 67636504)),
    ((119,), 1, (101126424,)),
    ((205,), 2, (114034968, 67900696)),
    ((25, 154, 170, 204), 5, (101258520, 101259033, 111740698, 110630684, 113969947, 109645597, 76091676)),
    ((171, 205), 4, (101454872, 80480280, 101455641, 111806746, 67769626, 80481049)),
    ((116, 117, 120, 188, 201, 204, 205, 219, 221, 459), 2, (102437639, 33554442, 130754580, 130754837, 130754323, 33554440, 33554438, 130754066, 130755351, 130755094, 33554441, 33554443)),
    ((128, 132, 140, 155, 156, 157, 189, 196, 200, 202, 218, 221, 460), 11, (67898368, 81598468, 81205253, 80414465, 83630850, 80550146, 67899139, 130818060, 67898625, 80288517, 115083544, 81468160, 115083801, 130819602, 130820116, 33554440, 83565314, 81468419, 130818317, 130820630, 130818574, 130819088, 33554442, 33554441, 130818831, 33554438, 33554443, 130819345, 33554439, 130819859, 130820887, 130820373)),
    ((45, 129, 131, 133, 143, 145, 149, 150, 173, 174, 190, 193, 197, 204, 206, 207, 221, 222, 461), 14, (80353282, 79697924, 80222211, 79960580, 83631104, 80353541, 112003352, 81597720, 81402368, 101518874, 81402625, 81528858, 68949018, 33554441, 130886166, 113969177, 82583041, 33554440, 33554442, 130885909, 130885652, 33554438, 130884110, 130885138, 130884881, 130885395, 130884367, 33554439, 130883853, 130886423, 33554443, 130883596, 130884624)),
    ((160, 162, 172, 174, 175, 191, 192, 207, 222, 223, 462), 12, (80025600, 82709761, 81664002, 82710018, 80681476, 79763461, 80026369, 82710275, 80546051, 113116696, 80677912, 79698176, 82710532, 130949389, 81597197, 130951188, 78514196, 82710789, 130949646, 115149337, 81662488, 115281673, 82711817, 130949903, 130950931, 130950160, 33554438, 33554442, 130950674, 130950417, 33554440, 130949132, 130951959, 130951445, 130951702, 33554439, 33554443)),
    ((161, 163, 175, 206, 222, 223, 463), 11, (81664256, 81727492, 79829250, 80611587, 101520408, 79698433, 81726978, 116330009, 114100762, 81726721, 79698693, 131014668, 80812293, 81659929, 131015696, 83760153, 131015953, 116330779, 131015439, 131014925, 131015182)),
    ((17, 221, 223), 5, (102502936, 101717529, 116329754, 83759898, 81659674)),
    ((18, 207), 2, (101778968, 115282201)),
    ((19, 223), 3, (101845016, 115214617, 83760409)),
    ((20,), 1, (101910552,)),
    ((21, 23), 2, (101976601, 102106904)),
    ((22, 102, 190), 3, (116201240, 102042137, 79498008, 102044698)),
    ((25, 221), 4, (101519640, 68949784, 81529624, 110630169)),
    ((9, 204), 3, (102438680, 108596249, 67899672)),
    ((153,), 3, (102241304, 77072408, 67702296, 101256985, 68687129)),
    ((9, 170), 4, (102306584, 67767576, 109581337, 75042329, 109581850, 75042842)),
    ((187, 205, 221), 5, (112855064, 67833368, 68817944, 115082777, 114034202, 114034459)),
    ((170, 188, 204, 222), 5, (102306840, 112920345, 115148314, 113968667, 67767832, 113969436)),
    ((45, 133, 145, 149, 150, 173, 204, 205, 214, 218, 221, 476), 3, (102503175, 33554441, 131868692, 33554440, 33554442, 131868178, 67964167, 33554443, 33554438, 131868435, 131868949, 131869206, 131869463)),
    ((172, 173, 177, 181, 189, 191, 204, 205, 206, 219, 222, 223, 477), 14, (80746496, 81528577, 80484355, 82647300, 81139717, 80550402, 80484612, 81402112, 79763712, 82582275, 131932686, 113969688, 82516739, 131932943, 33554439, 68883992, 131933200, 33554440, 67899416, 131934485, 131933971, 131934999, 131933457, 131934742, 131932172, 33554442, 33554438, 131932429, 33554441, 33554443, 131933714, 131934228)),
    ((175, 176, 178, 190, 191, 206, 207, 208, 210, 223, 238, 254, 478), 14, (80680962, 81729538, 68098816, 81594113, 80615684, 80025861, 81467904, 79763969, 82647555, 81729797, 114100248, 115280921, 131997965, 82711065, 132000278, 79563286, 80678934, 80610841, 131998736, 132000535, 79563543, 80679191, 81594627, 117315339, 131999507, 33554438, 33554442, 131998222, 82648068, 131999250, 131998993, 33554440, 132000021, 33554441, 131997708, 131998479, 131999764, 33554439)),
    ((206, 207, 209, 222, 479), 10, (82712832, 80681218, 80026115, 83760644, 132064272, 115148824, 80877827, 81660677, 82712080, 80611856, 80747009, 80681733, 132063758, 80611342, 132063244, 132063501, 132064015, 115149593, 132064529)),
    ((15, 238, 239), 3, (116263705, 101584152, 101582618, 68032281, 70128410)),
    ((2, 17, 18, 95, 238), 3, (116197144, 100731417, 107942170, 100732699, 100733468)),
    ((3,), 1, (100795928, 100796185, 100796698)),
    ((2, 4), 2, (100861464, 100731674, 100862233)),
    ((5, 11, 27), 4, (107679000, 75109144, 107615257, 100927002, 100927771)),
    ((6, 27, 28, 30, 51, 238), 6, (100864281, 107681048, 105715482, 116197403, 68294425, 116197917, 107679516, 100993822)),
    ((7, 10, 13, 42), 6, (101059096, 109711641, 107613722, 75043866, 105649947, 77141785)),
    ((8, 28, 93), 4, (107681304, 109906969, 101123866, 77337113)),
    ((9, 137), 2, (109580824, 67634712, 101192729)),
    ((10, 25, 26), 3, (109646360, 68748824, 101255193, 109645338)),
    ((11, 43, 76, 108, 171, 255), 8, (117312280, 101323289, 109842458, 107615004, 101323547, 77272602, 109711902, 111938845, 79368989)),
    ((28, 59, 60, 91, 187, 188, 221, 238), 10, (101389080, 108792857, 107680794, 101519131, 76223001, 102372636, 116196893, 67833628, 109775902, 112858911, 78319903, 77206046)),
    ((61, 76, 77, 170, 205, 221, 255), 8, (110826265, 102503707, 117311260, 107810072, 75240216, 101322781, 101454622, 76287257, 109843738)),
    ((94, 126, 161, 175, 177, 180, 193, 213, 221, 222, 225, 229, 235, 253, 255, 493), 7, (101519385, 112006424, 75303192, 33554439, 68949529, 101520666, 33554443, 132983575, 77467416, 33554441, 132982804, 132983318, 33554440, 132982547, 101520924, 33554442, 33554438, 132983061, 109908763, 132982290)),
    ((44, 110, 111, 192, 194, 206, 222, 223, 224, 239, 252, 254, 255, 494), 15, (83695616, 81860609, 83826689, 68029954, 81795073, 68030468, 83826949, 68029440, 82123522, 83696387, 133046541, 117314073, 68030211, 82124036, 133046798, 81659417, 82517248, 68030725, 133047055, 117378311, 109975066, 82775065, 68031239, 133047312, 133047826, 109973019, 33554443, 101586185, 133047569, 133048854, 33554442, 107744536, 133048597, 33554438, 33554440, 133048340, 75174680, 133046284, 74320410, 133048083, 133049111)),
    ((62, 78, 197, 207, 208, 238, 254, 255, 495), 11, (83823616, 83761154, 83630084, 81795333, 82708225, 82708739, 82909445, 101649945, 83696644, 108860952, 83824387, 107812634, 133112334, 133112848, 133112591, 133111820, 101650459, 133113105, 133112077)),
    ((1, 95, 255), 5, (108926744, 100668185, 101650202, 83757338, 69080346)),
    ((14, 18, 239), 5, (101779224, 117379353, 104666906, 70127898, 67963674)),
    ((19, 255), 4, (117311000, 68095000, 69079576, 101844505, 101845786)),
    ((18, 20), 3, (101779736, 101910041, 67179800, 101910298)),
    ((9, 13, 21), 4, (101976089, 108596506, 76026650, 101976347, 105648920)),
    ((22,), 1, (102041368, 102041881, 102042394)),
    ((11, 23, 26, 29), 6, (108661785, 102500634, 102107163, 107615512, 72159002, 73143578)),
    ((24, 59), 3, (102172952, 102173465, 109777178, 77207322)),
    ((8, 25), 3, (109580056, 110629401, 110629914, 68683802)),
    ((41,), 1, (110693400,)),
    ((27, 187), 3, (101388312, 108664089, 68818456)),
    ((10, 75, 204), 6, (101254680, 75043352, 108599065, 74058776, 102437915, 74060057, 110824474, 78254618)),
    ((27, 58, 204, 205, 239), 7, (108663833, 101586456, 82709016, 101453339, 74124825, 101454364, 111744282, 77205274)),
    ((30, 75, 110, 238, 239), 6, (102568472, 116197659, 69014811, 117379100, 107808793, 102566685, 110825498, 77403161)),
    ((94, 127, 207, 208, 210, 222, 223, 234, 236, 238, 239, 240, 242, 255, 510), 10, (117378584, 68031512, 134097430, 81660438, 82776086, 134096402, 82708504, 102634504, 108922649, 33554443, 102635018, 108924186, 33554438, 134097687, 76483865, 33554439, 134096916, 134097173, 77468441, 134096659, 33554441)),
    ((95, 127, 238, 239, 241, 253, 254, 511), 16, (82778370, 82450437, 82974720, 134160396, 102568728, 82582529, 83757058, 82844163, 102569753, 83757572, 68095233, 134160910, 82643737, 82707980, 82778884, 68096261, 111023130, 134161167, 68030988, 134160653, 108925979, 134161681, 74386971, 134161424, 76484122)),
)

LEFT, RIGHT0, RIGHT1 = CHUNKS, 2 * CHUNKS, 3 * CHUNKS
SIZE = 384 // CHUNKS
MAX_SENDS = max(len(p[2]) for p in PLAN)
MAX_FROM = max(1, max(len(p[0]) for p in PLAN))
MESH = pl.DeviceIdType.MESH


def nt_dot(left, right):
    return lax.dot_general(left, right, (((1,), (1,)), ((), ())), preferred_element_type=jnp.float32)


def choose(index, low, high, leaf):
    if all(PLAN[i] == PLAN[low] for i in range(low, high)):
        leaf(PLAN[low])
        return
    middle = (low + high) // 2

    @pl.when(index < middle)
    def _():
        choose(index, low, middle, leaf)

    @pl.when(index >= middle)
    def _():
        choose(index, middle, high, leaf)


def kernel(upper_ref, mask_ref, out_ref, buf, acc, table, origin, count, in_sem, send_sem, recv_sem):
    brow, column = lax.axis_index("brow"), lax.axis_index("bcol")
    row, half = brow // 2, brow % 2
    own = buf.at[pl.ds(0, 384)]
    load = pltpu.make_async_copy(upper_ref, own, in_sem)
    load.start()

    def leaf(plan):
        origins, targets, sends = plan
        count[0] = len(origins)
        count[1] = targets
        count[2] = len(sends)
        for i, v in enumerate(origins):
            origin[i] = v
        for i, v in enumerate(sends):
            table[i] = v

    choose(row * 16 + column, 0, 256, leaf)
    sends = count[2]
    barrier = pltpu.get_barrier_semaphore()

    @pl.loop(0, count[0])
    def _(i):
        v = origin[i]
        chip, flip = v % 256, v // 256
        there = (chip // 16) * 2 + (half + flip) % 2
        pl.semaphore_signal(barrier, inc=1, device_id=(there, chip % 16), device_id_type=MESH)

    load.wait()
    for i in range(3):
        for j in range(6):
            keep = mask_ref[i, j].astype(jnp.float32)
            at = (pl.ds(i * 128, 128), pl.ds(j * 128, 128))
            buf[at] = (buf[at].astype(jnp.float32) * keep).astype(jnp.bfloat16)

    @pl.when(count[1] > 0)
    def _():
        pl.semaphore_wait(barrier, count[1])

    def slot(index):
        return buf.at[pl.ds(pl.multiple_of(index * SIZE, SIZE), SIZE)]

    def copy(v, i):
        chip = (v // 65536) % 256
        there = (chip // 16) * 2 + (half + (v // 2**24) % 2) % 2
        return pltpu.make_async_remote_copy(
            src_ref=slot(v % 256),
            dst_ref=slot((v // 256) % 256),
            send_sem=send_sem.at[i],
            recv_sem=recv_sem.at[(v // 256) % 256],
            device_id=(there, chip % 16),
            device_id_type=MESH,
        )

    def arrived(index):
        pltpu.make_async_copy(slot(index), slot(index), recv_sem.at[index]).wait()

    @pl.loop(0, sends)
    def _(i):
        v = table[i]

        @pl.when((v // 2**25) % 2 == 1)
        def _():
            arrived(v % 256)

        @pl.when((v // 2**26) % 2 == 1)
        def _():
            copy(v, i).start()

    has0 = (row == 0) | ((column >= row) & (row + column >= 16))
    has1 = (column < 15) & ((row <= 1) | ((column + 1 >= row) & (row + column >= 16)))
    here = pl.ds(pl.multiple_of(half * 384, 128), 384)
    other = pl.ds(pl.multiple_of(384 - half * 384, 128), 384)
    acc[...] = jnp.zeros_like(acc)

    def rows(index):
        return buf[pl.ds(pl.multiple_of(index * SIZE, SIZE), 384), :]

    @pl.when(has0)
    def _():
        @pl.loop(0, CHUNKS)
        def _(j):
            arrived(SIB + j)

        right = jnp.where(row + column == 0, 0, RIGHT0)
        acc[:, here] = nt_dot(rows(0), rows(right))
        acc[:, other] = nt_dot(rows(0), rows(SIB))

    @pl.when(has1)
    def _():
        @pl.loop(0, CHUNKS)
        def _(j):
            arrived(SIB + CHUNKS + j)

        left = jnp.where(column == 0, RIGHT1, LEFT)
        acc[:, here] += nt_dot(rows(left), rows(RIGHT1))
        acc[:, other] += nt_dot(rows(left), rows(SIB + CHUNKS))

    out_ref[...] = acc[...].astype(jnp.bfloat16)

    @pl.loop(0, sends)
    def _(i):
        v = table[i]

        @pl.when((v // 2**26) % 2 == 1)
        def _():
            copy(v, i).wait_send()


def per_device(upper_store, block_mask):
    return pl.pallas_call(
        kernel,
        out_shape=jax.ShapeDtypeStruct((384, 768), jnp.bfloat16),
        in_specs=[pl.BlockSpec(memory_space=pl.ANY), pl.BlockSpec(memory_space=pltpu.SMEM)],
        out_specs=pl.BlockSpec(memory_space=pltpu.VMEM),
        scratch_shapes=[
            pltpu.VMEM((SLOTS * SIZE, 768), jnp.bfloat16),
            pltpu.VMEM((384, 768), jnp.float32),
            pltpu.SMEM((MAX_SENDS,), jnp.int32),
            pltpu.SMEM((MAX_FROM,), jnp.int32),
            pltpu.SMEM((3,), jnp.int32),
            pltpu.SemaphoreType.DMA,
            pltpu.SemaphoreType.DMA((MAX_SENDS,)),
            pltpu.SemaphoreType.DMA((SLOTS,)),
        ],
        compiler_params=pltpu.CompilerParams(
            collective_id=0, has_side_effects=True, vmem_limit_bytes=48 * 2**20
        ),
        name="cannon_steps",
    )(upper_store, block_mask)


def solution(mesh):
    spec = P("brow", "bcol")
    return jax.shard_map(per_device, mesh=mesh, in_specs=(spec, spec), out_specs=spec, check_vma=False)
```

```python
import jax
import jax.numpy as jnp
from jax import lax
from jax.experimental import pallas as pl
from jax.experimental.pallas import tpu as pltpu
from jax.sharding import PartitionSpec as P

CHUNKS = 6
SLOTS = 45
SIB = 33
PLAN = (
    ((1, 14, 16, 17, 31, 48, 224, 256), 5, (83894528, 83894785, 83895042, 83895299, 83895556, 83895813, 101717528, 103681305, 117451285, 101719578, 71178010, 117450514, 117450771, 117451028, 101583131, 117451542, 117451799, 103683612)),
    ((2, 3, 15, 16, 17, 18, 31, 33, 225, 257), 10, (70260738, 81795329, 68163584, 117516050, 82909458, 68163844, 67114243, 67114757, 117517335, 68225815, 117516307, 117514765, 68162317, 117516564, 68225044, 33554441, 117515279, 33554438, 33554443, 103682840, 117514508, 68162060, 33554440, 33554439, 33554442, 117515793, 68163345, 104731929, 70192921, 117515022, 117515536, 117516821, 117517078)),
    ((3, 18, 19, 32, 34, 48, 50, 51, 52, 96, 194, 226, 258), 8, (69277697, 81860613, 81860868, 68229122, 67311619, 67175936, 101845016, 101845274, 33554439, 101845785, 117580558, 68360718, 33554440, 33554443, 33554438, 117580815, 68228367, 117581329, 68228881, 117582100, 33554442, 117581072, 117581843, 117582357, 117582614, 117580301, 117581586, 33554441, 117582871, 117580044)),
    ((2, 17, 18, 19, 20, 33, 35, 37, 49, 51, 53, 131, 195, 227, 243, 259), 8, (79828994, 70391813, 81926147, 81926404, 68294657, 67241472, 101914649, 67179289, 100731160, 101910554, 100731931, 117646865, 68294417, 117646608, 68294160, 117648150, 33554440, 33554442, 117645837, 68293389, 117646351, 117647893, 33554438, 117646094, 117647636, 117648407, 117645580, 33554443, 117647122, 33554439, 117647379, 33554441)),
    ((5, 12, 20, 21, 36, 66, 68, 84, 130, 132, 228, 244, 260), 9, (33554442, 79894528, 117711887, 69409029, 81991681, 81991939, 68360450, 68425988, 68622351, 33554438, 117711630, 68359182, 33554441, 101976600, 33554439, 101976345, 105647131, 72949531, 117711373, 117711116, 68358668, 101975578, 117712401, 68359953, 33554443, 33554440, 117712658, 117712144, 117713943, 117713686, 117713172, 117712915, 117713429)),
    ((20, 21, 22, 23, 37, 39, 53, 65, 69, 71, 85, 87, 197, 229, 231, 261), 8, (82057217, 82057474, 83105797, 68425731, 67373572, 67372544, 101911321, 102107928, 117777423, 68424975, 102042394, 33554440, 117776652, 68424204, 33554442, 102042139, 117777166, 68424718, 33554438, 33554439, 117777680, 33554443, 117777937, 68425489, 33554441, 117778708, 117778965, 117779222, 117776909, 117779479, 117778194, 117778451)),
    ((7, 21, 22, 23, 25, 36, 38, 40, 54, 70, 98, 102, 166, 246, 262), 6, (69671170, 82122756, 68491265, 68556805, 68557059, 82253824, 102106904, 117842702, 68490254, 33554442, 117843473, 68491025, 117842445, 68489997, 117843216, 68490768, 33554443, 117844758, 117844244, 117843987, 33554438, 117844501, 117843730, 33554440, 117845015, 33554441, 33554439, 117842959, 117842188)),
    ((8, 22, 24, 27, 39, 69, 73, 99, 103, 119, 151, 167, 183, 231, 263), 9, (70654464, 83237634, 68557571, 68753921, 67504644, 67504901, 104471320, 74125336, 113645833, 117908495, 70654735, 117909009, 68556561, 33554440, 117909523, 117910037, 117908752, 68556304, 33554443, 117909780, 117910294, 117908238, 117909266, 117907724, 33554438, 117910551, 117907981, 33554439, 33554442)),
    ((9, 11, 23, 24, 25, 40, 72, 88, 89, 136, 164, 166, 232, 264), 11, (72882436, 67569923, 78125056, 82319361, 68688386, 68688645, 82188549, 76025346, 102237721, 33554441, 33554442, 117974545, 68622097, 107614744, 67765784, 117973517, 33554438, 117975316, 117975573, 33554443, 117974802, 117973260, 117976087, 117973774, 117975059, 117975830, 117974031, 117974288, 33554439, 33554440)),
    ((11, 24, 25, 26, 27, 41, 43, 73, 89, 105, 197, 199, 201, 233, 265), 12, (68687876, 69671936, 69736709, 70850561, 68688128, 75042563, 83433474, 67635459, 102173464, 102172953, 33554438, 115809306, 68750106, 33554440, 33554442, 114891291, 68749595, 118039567, 68687119, 33554443, 118039053, 68686605, 118040081, 68687633, 118039824, 118040338, 118040852, 118038796, 118041623, 118041366, 118040595, 118041109, 118039310, 33554441, 33554439)),
    ((8, 11, 12, 25, 26, 27, 29, 42, 168, 170, 184, 198, 202, 230, 234, 266), 11, (83237377, 82057733, 68753408, 82450435, 68753669, 74059266, 67835906, 68884740, 74059780, 105647640, 102370073, 102369306, 33554439, 118104846, 68885006, 101451803, 118104589, 68752141, 33554442, 118104332, 68751884, 118105617, 33554441, 118105874, 118106645, 118105103, 33554440, 118106388, 118106131, 118105360, 118106902, 33554443, 118107159, 33554438)),
    ((10, 13, 26, 28, 29, 43, 45, 165, 169, 171, 180, 187, 188, 213, 221, 235, 250, 267), 10, (82188291, 68491521, 67639296, 73076226, 70981637, 73076740, 68818945, 67766788, 101255192, 118170125, 68817677, 118172181, 33554440, 33554442, 118170382, 68817934, 33554439, 118170896, 118169868, 68817420, 33554438, 101520665, 118172438, 118171667, 118170639, 118172695, 33554443, 118171153, 118171410, 118171924, 33554441)),
    ((10, 14, 27, 29, 42, 44, 76, 192, 204, 206, 218, 232, 236, 250, 268), 14, (67377920, 82516229, 72093443, 67770370, 68032516, 71047429, 68950020, 67967489, 67967744, 72092929, 69016066, 102500120, 104537114, 70127130, 102501145, 118235661, 68883213, 118235404, 69016332, 33554438, 33554440, 118236689, 68884241, 33554441, 118237717, 33554439, 118237974, 80480790, 118236175, 68883727, 33554443, 118235918, 118236946, 118238231, 33554442, 118237460, 118237203, 118236432)),
    ((11, 12, 15, 28, 29, 30, 31, 45, 61, 111, 193, 201, 205, 207, 220, 237, 253, 269), 11, (71110403, 68884481, 71047172, 69146629, 69015554, 69015808, 115808793, 71047705, 68880409, 105713688, 68946456, 103750940, 69011740, 33554443, 33554439, 101386010, 118301197, 68948749, 101385755, 118302225, 118301711, 68949263, 118302996, 33554442, 118303510, 118301454, 33554441, 118301968, 118303767, 118300940, 33554438, 33554440, 118302739, 118303253, 118302482)),
    ((0, 12, 15, 30, 31, 46, 224, 236, 238, 240, 254, 255, 270), 11, (68098565, 67901954, 70127363, 69081348, 67115265, 70126592, 68098818, 69146881, 104798744, 118366733, 72093720, 69014285, 100670474, 118366476, 103682566, 69143558, 118367504, 118368532, 82708500, 118367761, 118366990, 118369046, 118369303, 82709271, 118368789, 82708757, 33554440, 33554443, 118367247, 33554441, 118368275, 118368018, 33554439)),
    ((14, 17, 29, 30, 239, 254, 255, 271), 13, (68229379, 67180545, 69144837, 68028932, 69081600, 69081858, 69144580, 69144066, 104666906, 67963674, 100733209, 104471580, 69011996, 70065436, 105712920, 105714205, 118432526, 101517339, 118432783, 118432269, 83756813, 118433040, 69080592, 118432012, 118433297)),
    ((0, 1, 28, 30, 208, 240, 272), 10, (100667928, 115677466, 83434010, 73142554, 100668953, 118500118, 67178518, 111221275, 71175451, 118499347, 105454876, 71175708, 102632222, 104729629, 118499090, 118499861, 118500375, 118499604)),
    ((1, 2, 15, 19, 31, 49, 51, 224, 241, 273), 10, (67312384, 81861122, 67115012, 80746499, 68098309, 67177729, 67178243, 100730904, 102767897, 67115801, 69144345, 100734217, 100734474, 33554439, 33554440, 118564883, 33554443, 103683866, 33554438, 118565397, 118565911, 118565140, 118565654, 118564626)),
    ((2, 3, 48, 50, 82, 210, 242, 274), 6, (81795076, 82909187, 67179008, 67311873, 67180293, 67179522, 100796184, 33554440, 33554441, 33554438, 33554443, 33554442, 118631447, 33554439, 118630162, 67308562, 118630676, 118631190, 118630419, 118630933)),
    ((2, 3, 4, 5, 23, 49, 83, 211, 243, 245, 275), 6, (80877568, 67246082, 67246341, 67246595, 82974724, 82974977, 101779224, 100861977, 33554443, 118696212, 33554440, 33554439, 33554442, 101782554, 33554441, 118696469, 118695698, 118695955, 33554438, 118696983, 118696726)),
    ((4, 5, 52, 80, 212, 242, 244, 276), 8, (70326273, 80943108, 67312130, 83040259, 67442949, 83171328, 100927768, 100862489, 33554442, 118761491, 67439891, 118762005, 33554441, 118761234, 33554440, 33554438, 118761748, 33554439, 118762519, 118762262, 33554443)),
    ((5, 6, 11, 53, 55, 113, 117, 245, 277), 9, (82975234, 81008641, 67377156, 67377411, 67377664, 83106565, 100992792, 105519129, 73075993, 118827284, 118826770, 67505170, 118828055, 33554443, 118827541, 118827798, 33554442, 33554438, 33554439, 118827027, 33554441, 33554440)),
    ((5, 6, 7, 26, 39, 54, 114, 118, 246, 278), 10, (70588672, 70720002, 67443205, 67443460, 83171841, 83172099, 100993816, 100993305, 101058843, 117120026, 75107354, 71900186, 33554442, 33554440, 33554443, 33554439, 33554438, 33554441, 118892306, 67570706, 118892563, 67570963, 118893591, 118892820, 118893334, 118893077)),
    ((4, 8, 9, 24, 89, 135, 147, 183, 215, 245, 247, 279), 8, (67442693, 70653956, 69670915, 67508225, 83236866, 83237120, 33554439, 101913880, 33554438, 33554443, 118957842, 67636242, 33554440, 33554441, 118958099, 118958356, 118958613, 67637013, 118959127, 118958870, 33554442)),
    ((8, 9, 56, 150, 152, 214, 244, 248, 280), 8, (83171586, 83302404, 67704837, 67705091, 68617985, 68617728, 116857112, 80222232, 67635736, 101124122, 101189145, 101124891, 33554438, 33554441, 33554439, 119023378, 67701778, 119024149, 33554440, 119023892, 67702292, 119023635, 119024663, 119024406, 33554443, 33554442)),
    ((7, 9, 10, 26, 27, 185, 217, 247, 249, 251, 281), 12, (83106049, 83106307, 80287749, 70785027, 70785282, 67639552, 83367940, 71899392, 82385154, 108597784, 67700248, 101255961, 101058330, 119089685, 67768085, 33554443, 119089942, 67768342, 33554441, 119089171, 33554440, 119089428, 33554442, 119088914, 119090199, 33554438, 33554439)),
    ((10, 11, 27, 56, 58, 90, 186, 250, 282), 11, (68557312, 82384898, 82254081, 67705349, 75108356, 69867523, 67705603, 73144581, 68749828, 101320472, 108664073, 33554443, 119155478, 67833878, 119154707, 33554440, 119155221, 33554438, 119154964, 33554442, 119154450, 33554439, 119155735)),
    ((10, 12, 13, 28, 29, 59, 219, 249, 251, 283), 12, (67573764, 69868033, 73013504, 68815107, 81401861, 67770629, 67770882, 74124802, 101255705, 103422744, 71109912, 33554441, 33554440, 119220243, 119220500, 67898900, 102306842, 119221014, 67899414, 33554442, 33554439, 119219986, 119221271, 119220757, 33554438, 33554443)),
    ((12, 13, 29, 30, 60, 216, 220, 252, 284), 9, (68164101, 70523136, 67967234, 69933060, 82647041, 68880643, 73142019, 106697993, 101386776, 33554442, 33554443, 119285779, 33554439, 33554438, 33554440, 119286550, 119286293, 119286807, 119286036, 119285522)),
    ((12, 13, 14, 15, 30, 31, 77, 241, 253, 285), 12, (69539845, 69081090, 68098049, 68946179, 70064128, 67901441, 67901701, 67966980, 101325592, 71110168, 104664089, 67896857, 101386266, 33554439, 119351058, 33554442, 33554440, 33554441, 119351829, 102437403, 119351315, 119351572, 119352343, 119352086, 33554438, 33554443)),
    ((14, 15, 16, 29, 31, 46, 62, 240, 254, 286), 12, (68164353, 68164610, 71176453, 68164864, 68099076, 68099328, 67968003, 69011458, 69011201, 83696133, 106697752, 68945944, 103682073, 67963417, 101582362, 103683099, 68028443, 104732170, 33554439, 33554443, 119417879, 33554438, 119416594, 119417622, 83757590, 33554441, 119417108, 119417365, 33554440, 119416851)),
    ((13, 14, 15, 17, 46, 238, 287), 13, (67115525, 67180803, 70129665, 69077508, 70192128, 70192642, 103554328, 101517081, 71110936, 71111449, 119481873, 68229649, 116071962, 68029201, 69014042, 119481359, 119481102, 119481616, 119480588, 119480845)),
    ((17, 34, 45, 46, 47), 6, (105778968, 116464409, 67244057, 103881498, 67243034, 103881756, 72225820, 103683357, 107746587)),
    ((2, 52, 59, 61, 62), 4, (100730648, 107811353, 100865818, 100864795, 109776668, 107812381)),
    ((35, 47, 63), 8, (69212420, 69212672, 67243522, 70523393, 67244293, 67243779, 70457601, 104864536, 71375384, 73274904, 100800025, 104012570, 72226074)),
    ((4, 51, 62), 8, (73406464, 70260997, 81926657, 69343492, 70392066, 70457347, 100864024, 100862745, 100863258, 105715483)),
    ((42, 69, 102), 4, (101060632, 108337945, 76156185, 100930074)),
    ((29, 41, 51, 52, 56, 86), 7, (100865562, 103947033, 67309337, 106437144, 72159512, 100996892, 110694171, 109777693)),
    ((44, 59, 61, 103), 3, (101062168, 101062425, 107745562, 105649435, 107746844)),
    ((6, 9, 23, 59, 120), 5, (100993049, 102107416, 108596252, 101126938, 109776157, 101127963)),
    ((9, 41, 57, 117, 136), 4, (101191960, 110694682, 109582105, 67635993, 101060379, 101192476, 101189405)),
    ((59, 137, 154), 8, (69540611, 72816896, 69736965, 83433730, 75044868, 72948993, 101257752, 109776921, 101258778)),
    ((26, 27, 59, 91, 170), 11, (69474561, 70654211, 70719492, 82319616, 70981893, 78256130, 104341018, 75109146, 108662552, 101321753, 101451547, 72094491, 101320732, 101321501)),
    ((28, 61, 91, 154, 171), 13, (70719749, 70588932, 82451202, 79305728, 83564803, 73210625, 111873817, 106437400, 70983448, 74126872, 107809819, 101389852, 101258522)),
    ((31, 46, 61, 74), 11, (70326784, 70392322, 69605893, 83564548, 73145091, 74190081, 106763544, 111808281, 108795418, 108794907, 101452060, 101452573, 72095517)),
    ((15, 29, 46, 61, 76, 78, 124), 13, (70457861, 69212931, 70982404, 70850816, 73207298, 71112961, 71113219, 104602392, 72158232, 112988441, 80418585, 107810586, 101517596, 105711387, 101386526, 105715229)),
    ((0, 1, 12, 14, 17, 30, 31, 32, 50, 61, 62, 63, 78, 302), 11, (69212163, 71243777, 69998595, 72223744, 72225029, 72224772, 72224258, 120464399, 70065167, 71244047, 120463628, 71111180, 102631192, 71176984, 120463885, 120464656, 71112208, 120465684, 120465427, 69143827, 68028179, 120464142, 105779975, 71240967, 120465170, 120466455, 120465941, 33554440, 120464913, 120466198, 33554443, 33554438, 33554442, 33554441)),
    ((1, 13, 31, 62, 63, 126, 143, 303), 10, (69213186, 69343747, 71241732, 71241989, 71178241, 71240704, 104471064, 72289304, 104729369, 72290585, 112006682, 112006427, 120529164, 71176716, 114103068, 120529678, 71177230, 105714973, 71175965, 120529421, 120529935, 120530449, 120530192)),
    ((1, 35, 51, 60), 4, (100668440, 101847578, 108794139, 100800281)),
    ((20, 32, 44, 51), 6, (101910296, 100863513, 108271642, 75174426, 101782043, 104795676)),
    ((3, 35, 37, 44, 63), 6, (100797208, 100799513, 104405530, 74190362, 101848347, 105780764, 70126108)),
    ((34, 35, 45), 11, (70261248, 69540099, 69408772, 69409281, 72488962, 70326530, 67309829, 101782297, 100799768, 107092506, 73208090, 104795931)),
    ((28, 34, 85), 10, (75700226, 69278213, 69278465, 83040512, 70588419, 69540356, 101978904, 100797722, 107288857, 70983193, 73141273)),
    ((22, 43, 52, 86), 4, (100865304, 102041113, 100995867, 108728346)),
    ((7, 23, 42), 4, (102107672, 101058074, 110565913, 76156697, 102110491)),
    ((22, 42, 43), 5, (104995609, 75174169, 102041626, 105388568, 77141528)),
    ((25, 42, 58, 59, 60), 7, (106175258, 77205018, 102238488, 103095580, 75238684, 102238233, 113843227, 77205531, 110760477, 102369054)),
    ((9, 45, 50), 5, (103292184, 75042072, 107745817, 70983705, 108729370)),
    ((7, 15, 47, 60, 91), 8, (70785538, 79304709, 82385409, 70785796, 77204480, 79305219, 112858136, 108793369, 72030745, 104728090, 102369819, 104730652)),
    ((11, 12, 42, 43, 45, 52, 57, 60, 107), 14, (69278723, 69672193, 82320389, 70786304, 69802244, 83499266, 110696217, 103423256, 73077016, 103160859, 73207835, 112922906, 102435359, 104666140, 104665117, 106761248, 102434334)),
    ((12, 13, 45), 10, (70786049, 70261509, 70916354, 82516997, 79435779, 75238400, 75239428, 105649688, 70982936, 105648409, 102499867, 106696218)),
    ((13, 15, 27, 29, 31, 45, 46, 59, 62, 63, 79, 109, 157, 235, 317), 13, (69933824, 69999108, 69999362, 70064643, 72161797, 72162049, 121447439, 69606159, 69999631, 102833418, 33554443, 106761497, 121447182, 72094734, 33554439, 106762010, 121446668, 72094220, 33554441, 114101272, 121449495, 70127895, 121448981, 121448210, 67962386, 106632987, 121446925, 121447953, 33554440, 121449238, 121448467, 121448724, 33554438, 121447696)),
    ((0, 1, 16, 30, 46, 47, 58, 64, 94, 318), 9, (81861381, 71109124, 69277952, 71108353, 71108867, 71109381, 73272834, 73272577, 73273091, 73273348, 121513489, 69409553, 103679768, 106829579, 121514003, 70192403, 121512461, 121513746, 69076498, 121515031, 70193431, 33554441, 121514774, 70193174, 121514517, 69077269, 33554442, 33554438, 121512204, 121514260, 69077012, 33554440, 121512718, 121512975, 33554439, 121513232)),
    ((14, 46, 47, 49, 51, 319), 11, (78649345, 69343236, 70195200, 72226819, 72289794, 70195461, 106763032, 121578768, 70392848, 104666393, 121579025, 72226577, 121577740, 72225292, 70125068, 106632730, 121578254, 121577997, 121578511)),
    ((34, 79, 93, 95), 4, (110891800, 104729115, 108923930, 107878169)),
    ((34, 85, 94), 4, (105912856, 67440664, 100995353, 105844762, 107941659)),
    ((55, 69, 77, 79), 4, (107877657, 100930586, 109843480, 109713179)),
    ((76,), 1, (111875864,)),
    ((69,), 5, (75634693, 75765760, 72554500, 67374851, 67374594, 72554753, 72620033, 100931096, 100930841)),
    ((81, 86, 88, 91), 8, (71440898, 69474816, 71571460, 71571715, 72620293, 72620545, 100996121, 111874328, 101124634, 105712155)),
    ((74, 103), 2, (111808794, 101061144, 111808537, 111807515)),
    ((86, 92), 4, (100995608, 110237977, 78320409, 72949785)),
    ((55, 76, 137), 3, (101192728, 109842201, 109711386)),
    ((16, 22, 25, 75, 120, 153), 6, (106175515, 77270043, 101256986, 101127704, 109644825, 109646364, 105714717)),
    ((21, 91), 6, (72751106, 71702788, 71703045, 71703296, 69998851, 78253313, 105646873, 107615000, 107615770)),
    ((58, 92, 93), 10, (71899904, 75175937, 72948484, 72948739, 77271301, 73079298, 106568216, 76353816, 111875609, 73075225, 109777946, 107681051)),
    ((4, 10, 12, 14, 38, 42, 44, 60, 61, 74, 78, 92, 93, 108, 125, 332), 15, (72423428, 71833859, 74062337, 73144322, 76286976, 76288261, 106695448, 105060377, 72358681, 73075481, 108860442, 72157210, 122430479, 70065679, 73210895, 106629403, 33554442, 107746332, 122429965, 73077517, 122430222, 73077774, 122432278, 67897878, 33554438, 33554441, 122431507, 122430993, 122430736, 122431764, 122429708, 122431250, 33554439, 33554443, 33554440, 122432535, 122432021)),
    ((13, 15, 35, 37, 45, 47, 61, 69, 73, 76, 92, 93, 94, 108, 125, 161, 333), 9, (71440386, 73079045, 75303936, 73209859, 75304193, 73144836, 73210114, 73210372, 106695193, 76353561, 106760984, 76355352, 107811098, 106628636, 122495244, 73142796, 107810075, 33554440, 122496272, 73143824, 122496786, 69010962, 122495758, 122495501, 73143053, 122496529, 33554439, 33554441, 122498071, 33554438, 122497557, 33554442, 122496015, 122497814, 33554443, 122497043, 122497300)),
    ((32, 34, 46, 50, 63, 93, 94, 95, 110, 334), 10, (72423940, 70064897, 74321667, 72096258, 74322181, 122560780, 73341184, 73208332, 74321153, 74321924, 106829080, 122562065, 73209617, 116202777, 73205785, 106826523, 122561294, 73341454, 122561551, 106760730, 122561808, 73341712, 107877127, 107877898, 33554440, 122562836, 70125588, 122563607, 70126359, 122561037, 33554438, 122562322, 122562579, 122563093, 70125845, 33554441, 122563350, 33554443)),
    ((47, 63, 65, 94, 95, 177, 335), 11, (71440643, 71309573, 72423685, 74322946, 73337856, 73275393, 73338884, 73338370, 73338113, 109909272, 122626316, 73273868, 104663066, 74257434, 122626830, 73274382, 122627601, 107811611, 106826265, 74387481, 107812124, 122627087, 122627344, 122626573)),
    ((65, 76, 92, 95), 3, (101979674, 110890009, 108925464, 110891291)),
    ((76, 78, 79), 4, (110827032, 105192218, 75306522, 106893593)),
    ((51, 91, 94), 3, (101848088, 112857625, 108926234)),
    ((68, 95), 4, (115612440, 68359704, 101913369, 108141082, 74387738)),
    ((56, 68, 69, 73), 3, (100928792, 100931353, 100930330, 111809052, 111744027)),
    ((), 4, (71374852, 71375109, 80025602, 70522881, 67440387, 67439616)),
    ((74,), 7, (80026372, 70589185, 72817155, 69540869, 71637250, 71768064, 111808024)),
    ((41, 86, 122), 3, (100996378, 110693401, 108595992)),
    ((8, 37, 43, 137), 4, (105191961, 76025881, 101192984, 106698522, 106696731)),
    ((4, 41, 71, 75, 92, 136, 153, 154), 6, (102175768, 67636760, 101257497, 110825244, 110825499, 101259034, 110693661, 106629150, 106631711, 106628896)),
    ((27, 75, 93), 4, (110892312, 73140504, 102368793, 75108889, 110892826)),
    ((11, 21, 59, 61, 63, 75, 76, 77, 89, 93, 94, 106, 181, 347), 13, (72489216, 71636997, 70916098, 69933315, 82516740, 77142785, 123413262, 69868558, 74060814, 106759960, 105519385, 75305241, 110824986, 123413776, 71965200, 33554443, 33554441, 33554438, 123414033, 74061585, 123413005, 33554442, 123414547, 33554440, 123415575, 123414804, 123413519, 123415061, 123412748, 123414290, 123415318, 33554439)),
    ((16, 26, 28, 30, 44, 52, 60, 76, 77, 88, 90, 107, 144, 156, 348), 13, (72096005, 71768321, 72358144, 83565058, 72949250, 72030468, 72096515, 83630339, 72162304, 77336066, 109841944, 109843994, 72092186, 107745051, 33554443, 33554442, 108663065, 123480340, 72158740, 33554441, 123479055, 72030991, 123479569, 123479826, 123480597, 72158997, 123478284, 123480854, 123478798, 123481111, 33554439, 123478541, 123479312, 33554440, 123480083, 33554438)),
    ((43, 44, 45, 51, 59, 61, 63, 76, 77, 78, 91, 95, 141, 349), 13, (82843648, 71309313, 82581506, 73013251, 72030213, 72095749, 72161540, 107747608, 75304728, 123544334, 72096782, 123545619, 72224019, 108727579, 123545362, 33554439, 33554438, 123544077, 74191629, 105646105, 75304473, 123546647, 33554443, 33554440, 123545876, 108859418, 106632476, 123544848, 123546390, 33554442, 33554441, 123544591, 123545105, 123546133, 123543820)),
    ((34, 62, 78, 79, 95, 109, 112, 126, 160, 176, 350), 10, (73340928, 75369729, 72227074, 73078785, 72292355, 72227332, 72161285, 75370500, 75370243, 75370757, 75369986, 123609870, 72292878, 123609613, 72293133, 105776920, 123610127, 72293391, 123611669, 71174421, 72290069, 106043913, 71375625, 33554443, 123610898, 123610384, 123611412, 71174164, 123612183, 123611155, 71173907, 123611926, 108926474, 123610641, 123609356, 33554440, 33554439, 33554438)),
    ((78, 79, 81, 94, 110, 351), 12, (72555013, 73271555, 72357888, 74386946, 74323969, 72227589, 72292612, 104864280, 76487704, 73205272, 123674892, 74322444, 108859929, 123675920, 72223248, 123675406, 106763290, 123675149, 106763803, 123676177, 123675663)),
    ((35, 109, 111), 3, (100799000, 111940122, 109974297)),
    ((127,), 2, (111023128, 76484120)),
    ((51, 103, 111), 3, (101061912, 109974553, 107747098)),
    ((120, 126), 2, (101126680, 109908761)),
    ((123,), 1, (111809304,)),
    ((52, 124), 3, (112335384, 80417560, 107680281)),
    ((103,), 5, (74520576, 69474308, 74782723, 77993985, 67506437, 67505666, 101061400)),
    ((120,), 6, (73537539, 77994242, 69605380, 69605637, 71702528, 73799681, 101127192)),
    ((107, 121, 122), 4, (108468760, 74058008, 109647385, 109581594)),
    ((122, 123, 138, 228, 246), 4, (109644313, 108661272, 108595738, 101254939, 75043611, 108599068)),
    ((8, 10, 74, 76, 91, 104, 107, 108, 121, 122, 123, 124, 228, 230, 234, 246, 362), 10, (111938584, 75176472, 124396302, 75043854, 108661019, 108595486, 111939353, 74123545, 124396816, 75176720, 79369497, 108661532, 109841690, 77271834, 33554438, 124397844, 33554441, 33554442, 108660253, 33554440, 124396559, 75044111, 124395788, 33554443, 124397330, 73075730, 33554439, 124396045, 124397073, 124397587, 124398615, 124398101, 124398358)),
    ((7, 27, 43, 75, 101, 106, 109, 122, 123, 124, 187, 229, 231, 237, 363), 12, (73930755, 74914048, 70982149, 75241989, 74057216, 75110914, 75111172, 79367682, 79368196, 75176193, 110955544, 108726041, 33554438, 33554441, 124463123, 73141523, 124461838, 75109390, 109777434, 33554440, 124462095, 124462352, 75109904, 33554439, 124462609, 124463894, 124463380, 124461581, 124464151, 33554443, 124461324, 124463637, 124462866, 33554442)),
    ((32, 38, 44, 50, 57, 76, 92, 93, 98, 110, 116, 123, 124, 125, 140, 172, 364), 12, (74651652, 74782981, 76158978, 74061824, 74062083, 75241473, 108791576, 111941130, 105646361, 76289305, 124527117, 75174669, 105711898, 75306266, 124527631, 75175183, 105645851, 76288795, 124528145, 75175697, 33554441, 124527374, 33554440, 124528659, 124528916, 33554438, 124529173, 124527888, 33554443, 124529687, 124526860, 124528402, 124529430, 33554439)),
    ((33, 43, 45, 77, 79, 111, 124, 125, 126, 157, 225, 365), 13, (73406976, 83630085, 75307010, 75241732, 74127360, 75307267, 75307524, 77402373, 77401345, 108665880, 78450200, 108727066, 108726811, 108927513, 78450969, 124593938, 71108114, 73272338, 33554440, 124593681, 75241233, 110957062, 107677468, 124593167, 75240719, 124594452, 124592396, 75239948, 124592653, 75240205, 124595223, 33554439, 124594966, 33554443, 124593424, 124594709, 33554441, 124592910, 124594195, 33554442)),
    ((64, 66, 78, 79, 95, 125, 126, 127, 142, 366), 10, (74651905, 75372546, 74389504, 75438082, 75438339, 76418048, 76419076, 76418819, 76419333, 124658703, 74193423, 124659988, 72222740, 124659217, 75306769, 109975307, 108925720, 124658189, 75305741, 124659474, 72222226, 124660245, 73338645, 72222997, 124658960, 108990474, 109974793, 124659731, 124660759, 72223511, 124660502, 33554440, 124658446, 33554439, 124657932, 33554438)),
    ((65, 79, 83, 95, 110, 126, 127, 223, 367), 12, (76552704, 73537794, 73406721, 76420612, 75372805, 75435779, 75435265, 75436293, 75435522, 107808280, 108923161, 76484377, 124723982, 74455310, 75371534, 109909530, 101519899, 124724753, 124724496, 124723725, 124724239, 124723468)),
    ((111, 125), 2, (112988696, 106825753)),
    ((102, 124, 127), 4, (102044184, 113711385, 75171353, 110038298)),
    ((83, 119, 125), 3, (102110233, 112989464, 108926746)),
    ((108, 110), 3, (110957337, 113252888, 79369752)),
    ((49,), 1, (107744280,)),
    ((36, 102, 108, 126), 6, (103291672, 68490520, 111483418, 75302426, 112924441, 110695195)),
    ((119,), 1, (102109720, 102109977)),
    ((104, 107, 122), 6, (74586370, 67571459, 74848256, 74848513, 67571973, 67571716, 77011202, 108594712, 112921625, 112922394)),
    ((123, 153), 7, (73603072, 78059523, 69671425, 69671685, 73865218, 71899140, 108660760, 110627609)),
    ((9, 25, 39, 41, 57, 87, 105, 106, 119, 122, 123, 136, 247, 249, 377), 5, (33554440, 110694424, 125380370, 74058770, 33554439, 125378828, 76026380, 33554441, 125379599, 73931279, 33554438, 125379342, 125381398, 125380884, 125379085, 76026637, 33554442, 125380113, 125379856, 125380627, 125381141, 33554443, 125381655)),
    ((22, 26, 42, 90, 92, 105, 106, 107, 109, 120, 123, 124, 218, 246, 250, 378), 11, (72816645, 74913792, 75040513, 75040770, 74063363, 73996804, 33554439, 113972504, 125445392, 73931024, 79433496, 107612699, 112987161, 33554441, 107612186, 33554440, 108791836, 125446677, 74125077, 125444364, 125447191, 74125591, 125446163, 74124563, 33554442, 33554443, 125445649, 33554438, 125446420, 125445906, 74124306, 125444878, 125445135, 125444621, 125446934)),
    ((49, 53, 55, 57, 75, 93, 106, 107, 108, 109, 113, 125, 127, 138, 251, 379), 12, (74979330, 73996292, 75106049, 74062595, 74062853, 74063104, 107677210, 107223064, 77270296, 108598811, 107611929, 79367449, 33554440, 33554443, 33554438, 33554439, 125511699, 125512470, 74190870, 125510157, 76157709, 125511185, 33554442, 125512213, 125510671, 125511442, 125510928, 76158480, 125512727, 33554441, 125510414, 125511956, 125509900)),
    ((44, 48, 56, 58, 60, 107, 108, 109, 122, 125, 126, 188, 380), 14, (74520832, 73734145, 70064389, 75110403, 79433732, 75439107, 75110656, 79433218, 74127617, 74258949, 74259204, 75307778, 111938840, 74259480, 107743769, 125575436, 74127884, 107612954, 125576464, 76224016, 33554439, 33554441, 125576721, 125576207, 125575950, 125578006, 74256406, 125578263, 125575693, 125577492, 74255892, 125577749, 33554440, 33554443, 125576978, 125577235, 33554438, 33554442)),
    ((76, 77, 81, 91, 93, 95, 108, 109, 110, 117, 124, 126, 127, 173, 381), 15, (74455040, 74586115, 82582276, 74258434, 75237635, 74192897, 74258693, 76356097, 111940632, 77401624, 33554439, 125640972, 72091148, 76288524, 108726299, 125641229, 74193677, 33554443, 125641743, 107743513, 77401881, 33554438, 125643028, 74321428, 110956570, 125642514, 72156690, 74320914, 125643799, 72157975, 125642257, 76289809, 125642771, 33554442, 125641486, 125643285, 33554441, 125642000, 125643542, 33554440)),
    ((64, 80, 82, 94, 109, 110, 111, 114, 143, 158, 382), 12, (74783232, 70195716, 70195971, 77467138, 75438597, 75302657, 75438850, 77466624, 77467652, 77467909, 77466881, 125706765, 73603341, 107808792, 107875097, 125707793, 125707536, 74390032, 125707279, 111023369, 125707022, 125708564, 125708307, 73271059, 74386707, 108792602, 33554442, 125706508, 125708050, 73270802, 74386450, 125709078, 33554438, 125708821, 33554439, 33554440, 125709335, 33554443)),
    ((110, 111, 124, 126, 145, 383), 10, (73472002, 74521089, 74389763, 76484612, 76484869, 76483584, 110957592, 125772815, 74320143, 116203034, 75303706, 108857371, 125772301, 110957849, 125773329, 108726556, 125772558, 125773072, 125772044)),
    ((143, 159), 2, (112071449, 113120024)),
    ((138, 158, 159), 5, (110172442, 80548890, 109644056, 113120793, 78581785)),
    ((68, 141), 2, (100929816, 114037785)),
    ((52, 157), 3, (100865048, 115086361, 80547353)),
    ((68, 141), 4, (100928536, 111156249, 78845977, 80483097)),
    ((158,), 2, (114103832, 112006169)),
    ((137, 139, 141), 3, (109578520, 109709850, 114037273)),
    ((136,), 2, (111417368, 68621848)),
    ((8, 40, 88, 104, 121, 134, 137, 150, 153, 168, 184, 198, 200, 230, 232, 249, 392), 10, (76748803, 75962372, 79108096, 69736453, 81205249, 72947714, 67636481, 103291911, 101192198, 126362382, 110627096, 33554443, 33554441, 126361868, 126362896, 126362125, 33554442, 126364695, 75043095, 126363153, 126363924, 126362639, 126364438, 126363410, 33554440, 126364181, 126363667)),
    ((73, 104, 105, 129, 152, 153, 154, 201, 217, 231, 233, 393), 11, (79173637, 71833602, 72882179, 76023553, 76023296, 79173892, 75896835, 76945410, 113711128, 77137944, 103356953, 77138457, 33554443, 33554442, 126429460, 33554439, 33554438, 126428689, 77076241, 126429203, 33554440, 126427404, 77074956, 33554441, 126429974, 126427661, 126427918, 77075470, 126430231, 126429717, 126428946, 126428175, 126428432)),
    ((36, 54, 66, 72, 108, 123, 134, 139, 153, 154, 155, 170, 186, 232, 234, 394), 8, (75569155, 73996548, 77142021, 77142274, 77142528, 77207553, 110757401, 112923672, 78384664, 33554443, 33554441, 110758427, 33554440, 33554442, 110758682, 33554439, 33554438, 126494996, 75173396, 126492940, 77140492, 126494482, 75172882, 126493454, 77141006, 126494225, 126493197, 126494739, 126495767, 126493711, 126495253, 126495510, 126493968)),
    ((33, 37, 39, 41, 75, 107, 124, 141, 154, 155, 156, 157, 171, 172, 203, 219, 235, 395), 8, (75897348, 78256898, 76155653, 76155139, 77207809, 77208064, 113053976, 111872794, 110823961, 33554438, 33554443, 126561303, 33554439, 126558733, 77206285, 33554442, 126561046, 126559247, 77206799, 126559504, 77207056, 126560789, 126560018, 126559761, 126560532, 126558990, 126560275, 126558476, 33554440, 33554441)),
    ((66, 72, 76, 92, 106, 108, 125, 155, 156, 157, 160, 204, 396), 12, (76814338, 76552452, 77273089, 80482051, 80481280, 76421125, 76355589, 76355844, 77404160, 115087128, 77335320, 126624012, 77271564, 110888473, 126625297, 77405201, 114038025, 107743002, 78385946, 126624526, 77272078, 126626325, 126625554, 126624269, 33554443, 126625811, 33554438, 126626068, 126626582, 126624783, 77272335, 126625040, 33554440, 126626839, 33554439, 33554442)),
    ((75, 77, 79, 99, 111, 125, 140, 143, 154, 156, 189, 237, 397), 12, (75766017, 75634946, 75897088, 77338627, 79499268, 76224517, 77273344, 77338885, 77339138, 77404418, 109775640, 110693147, 112004378, 126691861, 73206037, 109775385, 113055242, 126690576, 77338128, 126690833, 113054728, 33554443, 126689805, 126692118, 126692375, 33554441, 126690062, 126691347, 126690319, 126691604, 126691090, 33554438, 126689548, 33554439)),
    ((96, 98, 110, 111, 140, 144, 157, 158, 159, 174, 191, 398), 11, (76617731, 79632645, 78516228, 78516485, 78515457, 76486916, 76487170, 77469698, 77535232, 126755084, 111019545, 126756369, 77403921, 126756112, 77403664, 126757654, 74320406, 126755855, 110954266, 114037016, 112071174, 113119259, 126757140, 74319892, 126757911, 33554440, 126755598, 126756883, 74319635, 126755341, 126756626, 74319378, 33554441, 126757397, 33554439, 33554443, 33554442)),
    ((95, 97, 111, 113, 127, 142, 158, 159, 399), 11, (75503873, 79632384, 77532674, 77533188, 77532931, 77533445, 113121048, 78582040, 103750683, 79564059, 126821648, 77469200, 109906457, 109905946, 126821391, 126820620, 77468172, 112005917, 126821905, 77469457, 126820877, 75368205, 77468429, 109908508, 126821134)),
    ((111, 140, 159, 240), 5, (113120536, 110172698, 76419610, 114036761, 106694171)),
    ((129, 142, 144, 161), 4, (112204312, 79500568, 110954521, 108989466, 113052187)),
    ((71, 155), 2, (110757656, 110890265)),
    ((136, 159), 2, (102176024, 112135193)),
    ((140,), 2, (114036248, 80419096)),
    ((156,), 1, (113053464,)),
    ((137, 153), 3, (102241305, 77072409, 109578264)),
    ((54, 119, 156), 3, (101125657, 110823704, 110695706)),
    ((120, 136, 137, 150, 153, 168, 244, 248, 408), 4, (102240774, 112857880, 33554440, 33554441, 127412243, 76090643, 33554443, 127412757, 76091157, 127413014, 76091414, 127413271, 33554442, 33554439, 127411986, 127412500)),
    ((37, 40, 55, 59, 87, 89, 91, 117, 121, 137, 138, 141, 151, 155, 185, 249, 409), 13, (80025857, 76945666, 71899651, 72947973, 77071872, 80288260, 74979589, 78125825, 76027907, 109644568, 111873307, 77076507, 109643290, 109643801, 33554440, 33554441, 33554439, 33554442, 127477265, 127478807, 76157207, 33554443, 127477779, 127476494, 127477008, 127475980, 127477522, 127478550, 33554438, 127476751, 127476237, 127478036, 127478293)),
    ((56, 58, 138, 139, 146, 155, 186, 216, 232, 250, 410), 10, (72948229, 76093442, 69801984, 69933571, 79239681, 76093700, 79239936, 76356357, 77273603, 33554441, 109643544, 33554440, 127541516, 79240204, 109709081, 33554438, 109708826, 127542030, 33554439, 127542801, 33554442, 127544343, 76222743, 127542544, 127543572, 76221972, 33554443, 127543315, 127543058, 76221458, 127543829, 127542287, 127541773, 127544086)),
    ((73, 75, 81, 89, 91, 106, 123, 139, 140, 141, 151, 154, 156, 157, 189, 411), 9, (76683265, 77203715, 77203458, 76159232, 76159493, 76159748, 110692634, 33554438, 127608337, 78255889, 113908760, 76220184, 109839897, 33554439, 127608594, 127607309, 127607823, 78255375, 127607052, 127609622, 76288022, 127608080, 78255632, 33554442, 33554440, 127607566, 78255118, 33554443, 127608851, 33554441, 127609108, 127609365, 127609879)),
    ((64, 80, 90, 92, 140, 141, 146, 157, 171, 220, 236, 240, 252, 412), 12, (77010947, 77268480, 79501314, 76224772, 77404673, 77404933, 110434328, 76286232, 115086858, 33554441, 33554443, 109841177, 33554438, 109840410, 127674387, 73139987, 76352787, 127672588, 78320140, 127674644, 73140244, 76353044, 127675158, 127674901, 76353301, 33554439, 127674130, 76352530, 127675415, 127673102, 127673873, 127672845, 127673616, 127673359, 33554440)),
    ((107, 109, 115, 125, 127, 140, 141, 142, 145, 156, 158, 159, 205, 413), 13, (75700482, 71112704, 80418819, 80547073, 76290053, 77335044, 77334787, 76290304, 109774360, 113053209, 110823194, 127739409, 127740180, 76418580, 33554438, 127738381, 76290573, 127739923, 74254099, 127738638, 76418323, 127740951, 74255127, 110824219, 127740437, 74254613, 127738895, 78386447, 127738124, 127740694, 74254870, 33554441, 127739152, 127739666, 33554439, 33554440, 110827292, 33554443, 33554442)),
    ((97, 126, 142, 143, 173, 190, 414), 10, (75831300, 75569666, 79563776, 76487425, 77399552, 79565061, 79564547, 77535493, 77535747, 76421633, 76421892, 79564290, 127804174, 75831566, 127803917, 76487949, 127803660, 112070168, 127804688, 127806230, 75368982, 113119750, 127804945, 127805973, 33554441, 127805202, 75367954, 33554443, 127805716, 75368468, 127806487, 75369239, 33554440, 127804431, 33554442, 127805459, 33554439)),
    ((142, 143, 158, 174, 191, 415), 11, (76552195, 75503617, 75569412, 76749056, 78581250, 76421376, 76486661, 127869710, 78517262, 113054232, 127869967, 78517519, 110955289, 110954778, 127870481, 78518033, 127870224, 78517776, 127869196, 127869453)),
    ((132, 174, 175, 191, 225), 5, (114168344, 112531737, 77797401, 80613145, 106828058, 114168859, 109840156)),
    ((16, 190), 5, (110172952, 82646552, 81661976, 105714458, 114102809)),
    ((165, 173), 3, (114759960, 78382616, 114167833)),
    ((160,), 1, (112003352,)),
    ((135,), 1, (101191704,)),
    ((117, 174, 188), 4, (111286553, 78449177, 101388824, 78977560, 112005658)),
    ((102, 103, 184), 2, (101059864, 101061657, 101193498)),
    ((120, 172), 2, (101127448, 111872537)),
    ((8, 153, 171, 187), 6, (112662808, 76024856, 101323546, 78251802, 112854809, 110626587)),
    ((84, 170, 173, 185, 186, 187, 201, 217, 233, 425), 3, (33554442, 112794891, 101390104, 33554438, 33554439, 33554441, 33554440, 128526869, 128526098, 128526355, 128526612, 128527383, 128527126)),
    ((42, 44, 70, 74, 84, 86, 100, 139, 155, 168, 184, 186, 187, 189, 202, 426), 10, (69867776, 81336323, 67767810, 79239172, 67767553, 67768581, 78187269, 78186241, 79239426, 79304963, 79370240, 112855066, 109709339, 112985881, 33554439, 128590863, 128590349, 101324555, 109710872, 128592919, 128591377, 128590606, 128590092, 33554442, 33554440, 128592405, 128591120, 33554438, 128592662, 128591634, 128591891, 128592148, 33554441)),
    ((43, 67, 69, 71, 75, 139, 153, 156, 167, 172, 173, 186, 187, 188, 189, 235, 251, 427), 12, (80091139, 78125569, 79174148, 82450688, 80353282, 79305477, 79174400, 103488537, 79366681, 101387288, 33554440, 33554441, 128655885, 33554442, 33554438, 33554443, 109778202, 128656399, 79303951, 33554439, 128656913, 79304465, 128658198, 77336598, 128656142, 128656656, 128657684, 128657170, 128657427, 128658455, 128657941, 128655628)),
    ((96, 106, 108, 124, 125, 138, 140, 157, 162, 173, 187, 189, 192, 202, 206, 220, 221, 252, 428), 10, (78059780, 76225029, 78317570, 78452992, 78453249, 79502083, 112986648, 115150601, 128721164, 79368716, 128721421, 79368973, 128723220, 74188820, 128722706, 74188306, 128723991, 74189591, 128721935, 128723734, 33554438, 33554443, 33554439, 128722963, 128721678, 128723477, 128722192, 33554442, 128722449, 33554440)),
    ((47, 109, 133, 141, 143, 163, 165, 172, 175, 188, 190, 205, 221, 237, 429), 13, (77731840, 81468161, 81596420, 81532933, 78383363, 81595906, 81596677, 111745048, 79366936, 113051931, 111871513, 128787214, 79434766, 111871770, 128789270, 75303446, 128786957, 79434509, 128789013, 75303189, 77467413, 128787985, 79435537, 115152394, 33554443, 128786700, 128788499, 33554438, 128788242, 128787728, 128787471, 33554441, 128789527, 33554440, 128788756, 33554439)),
    ((128, 142, 158, 159, 176, 189, 190, 191, 206, 430), 11, (77928708, 78715136, 77601027, 80612609, 81729794, 78584069, 80613637, 80612866, 128853521, 128853264, 113184007, 128854292, 76417044, 128854035, 77532435, 76416787, 128852493, 79500045, 33554440, 128854549, 76417301, 128852750, 114169611, 33554438, 128855063, 76417815, 128853778, 33554441, 128853007, 128854806, 76417558, 128852236, 33554442)),
    ((129, 143, 147, 159, 174, 190, 191, 431), 11, (77600768, 78714884, 79629826, 79567105, 79567362, 79630083, 79630597, 115217176, 80678168, 117251354, 83761690, 82645530, 112003865, 128918286, 79565838, 128919057, 128918543, 128918800, 128917772, 128918029)),
    ((63, 145, 191), 4, (112269848, 73274136, 115217433, 112070426)),
    ((174, 175, 176), 5, (112335129, 81596953, 114169368, 81730840, 105843994)),
    ((101, 177, 191), 3, (115216920, 114166809, 112987418)),
    ((132,), 1, (113052952,)),
    ((188,), 1, (101389080,)),
    ((160, 165, 230), 3, (106630936, 112920090, 115152153)),
    ((187,), 2, (117053976, 79301400, 112854553)),
    ((136, 168), 2, (102175256, 101123609)),
    ((137, 171), 5, (111548952, 76024600, 115875353, 76024345, 101324314, 78252570, 111805979)),
    ((154, 169, 170), 4, (102307352, 78187032, 115940634, 77137690, 110691867, 111740953, 102307613, 111743516)),
    ((43, 58, 82, 152, 168, 170, 171, 182, 187, 190, 218, 442), 9, (102372874, 111741209, 102372617, 111807259, 114891032, 77205784, 33554440, 33554443, 109711900, 114104093, 111744282, 77205274, 33554439, 129640724, 78319124, 129640210, 78318610, 129640467, 129640981, 129641495, 129641238, 33554438)),
    ((59, 106, 107, 115, 117, 119, 123, 138, 170, 171, 172, 173, 181, 189, 219, 443), 11, (79042565, 67833089, 79301124, 79042816, 82515970, 79300867, 78321664, 82516483, 78125313, 78256642, 111740440, 129704718, 129706260, 74123284, 33554442, 33554440, 33554439, 33554443, 129705232, 129704204, 129705746, 33554441, 129707031, 74124055, 78385431, 129706517, 129705489, 129706774, 74123798, 129706003, 129704975, 33554438, 129704461)),
    ((45, 60, 112, 114, 122, 124, 170, 172, 173, 178, 189, 190, 236, 444), 11, (78911489, 81467906, 77928448, 67835139, 78321924, 78452741, 79501569, 79501827, 33554443, 129770768, 80288528, 33554441, 129770254, 80417806, 108793624, 78322200, 33554438, 33554442, 129771025, 33554439, 129771282, 75236882, 78449682, 129771796, 129769740, 129772310, 75237910, 78450710, 129770511, 129771539, 129772053, 78450453, 129772567, 33554440, 129769997)),
    ((139, 141, 145, 149, 156, 157, 159, 172, 173, 174, 179, 188, 191, 204, 219, 253, 445), 11, (78256385, 79566850, 79432453, 79431939, 79431168, 78387204, 129836304, 80483856, 111872283, 112920345, 129835790, 129838103, 76352279, 110823448, 33554441, 33554443, 112920858, 129836561, 80484113, 129837589, 76351765, 129836818, 78515218, 129837846, 76350994, 129837075, 76351251, 129836047, 129837332, 33554438, 129835276, 33554442, 129835533, 33554440, 33554439)),
    ((128, 129, 142, 143, 144, 158, 175, 189, 222, 446), 13, (77666308, 81661699, 81468418, 79632901, 81661185, 78584320, 78453507, 81661442, 114168601, 78513945, 129900812, 77666572, 112068634, 129902097, 79306001, 112986136, 129901583, 80549135, 129903125, 77465877, 78581525, 129903639, 77466391, 129901326, 33554441, 129901069, 33554439, 129902868, 77465620, 129902354, 129901840, 33554438, 129903382, 77466134, 129902611, 77465363, 78581011, 33554443, 33554440, 33554442)),
    ((142, 143, 174, 175, 190, 206, 223, 447), 12, (78780416, 78649602, 80678659, 80678916, 80679173, 78583809, 129966862, 77601550, 113055513, 109970968, 77532184, 115216666, 79498010, 129967119, 80614671, 129967633, 78514961, 129966605, 129966348, 129967376)),
    ((115, 204, 206, 207, 223), 5, (114366745, 82711833, 101453592, 116266524, 116266011, 80611355, 111939610)),
    ((222,), 3, (114628632, 67966488, 116200729)),
    ((3, 207), 2, (100796440, 116266777)),
    ((4,), 1, (100861464,)),
    ((), 0, ()),
    ((85, 86, 153, 206), 3, (100994584, 101256473, 114100762, 100996635)),
    ((7, 171), 3, (101324056, 80353816, 109580057)),
    ((113, 137), 2, (101258264, 113971737)),
    ((24,), 1, (109581848,)),
    ((25, 56, 153, 188, 221), 8, (101519129, 81271065, 116922906, 67702810, 114694168, 76091672, 113972763, 111744540)),
    ((155, 171, 198, 205, 221), 4, (114034201, 101323800, 78252056, 111806746, 111938075, 114035996)),
    ((45, 101, 122, 148, 157, 188, 199, 201, 204, 219, 221, 234, 459), 5, (114956824, 80547608, 33554440, 33554438, 33554441, 130755093, 33554442, 130755607, 33554443, 116200474, 130755350, 130754836, 109774873, 130754579, 33554439, 130754322)),
    ((12, 130, 132, 134, 140, 142, 144, 148, 189, 202, 205, 220, 221, 236, 460), 12, (79697923, 80615429, 67898625, 81467394, 81467652, 67898368, 82450945, 80415493, 80414208, 81598467, 115083800, 130819087, 81468687, 114956555, 130818316, 115084057, 101455113, 33554439, 101454342, 130820886, 76286486, 130820629, 130819601, 130819858, 79498258, 130818830, 130821143, 33554440, 130819344, 130820115, 33554442, 130820372, 130818573)),
    ((47, 61, 129, 131, 133, 157, 161, 186, 190, 197, 203, 206, 207, 220, 221, 223, 237, 461), 11, (82320130, 83499012, 80481029, 80353536, 82582529, 81533187, 80480001, 114825240, 67964440, 33554439, 130884109, 81531661, 33554440, 33554441, 130884623, 101520154, 130885908, 33554442, 130885137, 130883852, 81531404, 33554443, 130886422, 77400598, 112002841, 33554438, 130884366, 130886165, 130885651, 130886679, 130885394, 130884880)),
    ((160, 162, 174, 177, 178, 190, 191, 192, 204, 207, 221, 223, 238, 462), 13, (80026116, 80545537, 82710789, 80680963, 82709761, 82710532, 82710275, 81664000, 81730050, 81730304, 115215129, 130949645, 80550157, 81597197, 101454104, 113253386, 130949902, 130950930, 79629330, 78513682, 130950673, 81730577, 130951187, 130950159, 33554441, 130951701, 78514453, 33554440, 111937562, 33554443, 130950416, 130951958, 78514710, 130952215, 33554439, 130949388, 130951444, 33554438)),
    ((175, 191, 206, 222, 463), 11, (79698179, 79829253, 80746752, 80812033, 80611844, 81726978, 81727492, 81727749, 81726464, 131015695, 81663247, 101521177, 83696665, 131016209, 81663761, 114100504, 131015952, 81663504, 131014924, 131015181, 131015438)),
    ((17, 207, 223), 3, (101717272, 117314331, 117314074, 116265497)),
    ((192, 207), 3, (115281689, 116265752, 83826712)),
    ((19, 223), 2, (101844504, 117315097)),
    ((20,), 1, (101911064,)),
    ((21,), 1, (101975832,)),
    ((193, 219), 2, (115149336, 101389337)),
    ((201,), 1, (102239000,)),
    ((136, 162), 2, (102175512, 115149849)),
    ((201, 205, 233), 3, (115083545, 102503448, 81528856, 110759194)),
    ((9, 170, 186), 3, (102307096, 109647130, 111744793)),
    ((27, 203, 204, 235), 4, (108664600, 101455641, 115086618, 112858651)),
    ((173, 188, 190, 204), 7, (102437912, 80414744, 114628890, 79366170, 115150107, 102438425, 80415257, 113051676, 80419356, 109775133)),
    ((131, 140, 156, 173, 204, 205, 216, 218, 252, 476), 7, (114034969, 101519370, 68949514, 111938328, 131869719, 80548119, 131868691, 77334291, 102504203, 33554439, 33554441, 131869462, 80547862, 131868948, 77334548, 33554438, 131868434, 33554440, 131869205)),
    ((172, 173, 177, 181, 204, 206, 213, 215, 219, 222, 223, 253, 477), 11, (80288003, 80549890, 82647297, 80484356, 80484613, 82647557, 82647808, 113969432, 101390601, 114104839, 131933456, 80354064, 33554440, 33554438, 131932942, 80615950, 131934227, 131932685, 78382861, 131933970, 78448146, 131933713, 131933199, 33554442, 33554443, 131934484, 78448660, 131935255, 131934998, 131932428, 131934741)),
    ((161, 175, 176, 178, 190, 191, 206, 207, 236, 242, 254, 478), 9, (79763460, 81594627, 81729536, 83695874, 80681221, 81594113, 131998735, 79763727, 116263960, 33554443, 132000277, 79563029, 131998221, 83697165, 131999763, 79562515, 131999506, 79562258, 80677906, 131999249, 82646801, 132000020, 79562772, 80678420, 132000791, 79563543, 33554442, 131998478, 33554441, 132000534, 79563286, 33554439, 33554438, 131998992, 131997964, 33554440)),
    ((174, 177, 206, 207, 209, 222, 255, 479), 13, (81861635, 80877828, 80747008, 80747265, 82319874, 82776325, 80615685, 116264474, 80545818, 132064014, 79698702, 107944728, 81593880, 132064785, 115151897, 132064528, 114099739, 132063500, 132064271, 115152668, 113184797, 132063757)),
    ((1, 18, 238, 239), 5, (101779992, 100668185, 116464667, 82385691, 68030747, 101586202)),
    ((2, 17, 62, 223), 7, (100731672, 100731417, 116398362, 67178010, 111155739, 74258203, 116529948, 83368220, 82775836)),
    ((3, 35), 1, (100796953, 100796696, 100799258)),
    ((4,), 1, (100862233, 100861720)),
    ((5, 10, 83), 3, (100927256, 100927513, 107551770, 74060058, 100929563)),
    ((6, 16, 241), 3, (100993560, 107681561, 116197658)),
    ((8, 11), 4, (112531480, 74061080, 67766552, 109580569)),
    ((6, 9, 13, 26, 232), 6, (100992536, 117054233, 83302937, 76092185, 107680794, 101123867, 109647644)),
    ((8, 42, 59, 184, 205, 223, 249), 8, (115809048, 76025112, 110761756, 109710361, 101454875, 82582811, 101193246, 117314586, 82583066, 101189661)),
    ((25, 26, 58, 185, 224, 234), 7, (116792344, 83434264, 76092440, 114825754, 78189338, 109645337, 116198171, 101258013, 101255452)),
    ((10, 43, 171, 204, 251), 5, (107613976, 82385944, 109712411, 101323289, 113968922, 109712668)),
    ((12, 31, 60, 91, 187, 236, 252), 6, (104667929, 67832601, 101387800, 109778716, 101388058, 116197917, 114957083, 78319643, 116196894, 111875359)),
    ((93, 125, 205, 232, 238, 255), 9, (101584922, 82517274, 117312281, 83696410, 110892056, 112989723, 101454620, 114034717, 115214366)),
    ((28, 78, 127, 161, 175, 193, 203, 221, 222, 229, 233, 235, 238, 253, 493), 8, (107680536, 83565336, 101518617, 83630617, 101519642, 33554439, 101518363, 83630875, 114101020, 112006942, 109909021, 33554442, 33554440, 132983317, 33554443, 132983574, 132983831, 33554441, 132982803, 132982546, 132983060, 33554438)),
    ((14, 192, 194, 206, 208, 209, 222, 223, 254, 255, 494), 11, (81795845, 82909699, 69147136, 68029697, 82582020, 68030211, 68029440, 68029954, 82642689, 83695618, 117311000, 133047825, 82648081, 117311769, 133047311, 117378311, 133047568, 117379082, 133048853, 80611605, 133047054, 133046540, 133046797, 101585414, 133049367, 80612119, 33554440, 133049110, 33554443, 133048339, 80611091, 133048596, 33554441, 133048082, 80610834)),
    ((223, 225, 254, 255, 495), 6, (81795587, 83761153, 83761412, 83824130, 83824901, 83823616, 83824387, 116398872, 68095512, 101650202, 101650713, 133112847, 133113361, 83760913, 133113104, 133112333, 133112076, 133112590)),
    ((93, 225, 239, 254), 6, (101717017, 101585690, 110107416, 77337112, 102634523, 83757083)),
    ((1, 18, 32, 224, 238), 3, (101779736, 101778969, 115677722, 69014810, 101783067, 102569756)),
    ((19, 21, 225), 3, (101845528, 101844761, 101976090, 115214619)),
    ((20, 52), 2, (101910808, 100864537)),
    ((5, 21, 25), 4, (100928280, 102237977, 77075225, 110630170, 101976859)),
    ((20, 22, 24), 3, (102172697, 101910040, 102041370, 102041883)),
    ((7, 10, 23, 233), 5, (102107160, 102106649, 107551514, 74059034, 101058587, 108662300)),
    ((24, 231), 3, (102173208, 108597273, 102303514)),
    ((25, 201, 225), 3, (102238744, 77075992, 102241818, 77072922, 117314841)),
    ((9, 16, 41, 233), 6, (108596760, 82320664, 76026904, 110693913, 102303771, 102435610)),
    ((59, 182, 205, 231), 5, (101455384, 110760985, 101388570, 68818714, 108662043)),
    ((22, 43, 44, 92, 237), 5, (108729880, 108728089, 82451481, 111875098, 102434587, 102303260)),
    ((92, 109, 237), 5, (111941400, 115083034, 110890777, 82517785, 102502939, 81528347)),
    ((30, 175, 207, 222, 236, 238), 5, (101520409, 81594393, 102566682, 102568984, 82642968, 115149596, 102569499, 113051165, 113051422, 82645790)),
    ((15, 30, 175, 208, 210, 232, 236, 238, 239, 240, 248, 510), 8, (116398616, 82708248, 101586457, 82709017, 101649414, 69079558, 102635275, 134097686, 81660438, 82776086, 102634761, 134096915, 81659667, 82775315, 134097943, 134096658, 81659410, 82775058, 102634247, 134097172, 82775572, 115215386, 33554440, 134097429, 33554442)),
    ((209, 238, 239, 511), 7, (82778114, 68095233, 68096004, 82581765, 82712576, 82712835, 82778373, 82778627, 134161166, 68031502, 134161937, 68032273, 134160652, 82707980, 134161423, 134160909, 134161680, 115281176)),
)

LEFT, RIGHT0, RIGHT1 = CHUNKS, 2 * CHUNKS, 3 * CHUNKS
SIZE = 384 // CHUNKS
MAX_SENDS = max(len(p[2]) for p in PLAN)
MAX_FROM = max(1, max(len(p[0]) for p in PLAN))
MESH = pl.DeviceIdType.MESH


def nt_dot(left, right):
    return lax.dot_general(left, right, (((1,), (1,)), ((), ())), preferred_element_type=jnp.float32)


def choose(index, low, high, leaf):
    if all(PLAN[i] == PLAN[low] for i in range(low, high)):
        leaf(PLAN[low])
        return
    middle = (low + high) // 2

    @pl.when(index < middle)
    def _():
        choose(index, low, middle, leaf)

    @pl.when(index >= middle)
    def _():
        choose(index, middle, high, leaf)


def kernel(upper_ref, mask_hbm, out_ref, buf, acc, mask_ref, table, origin, count, in_sem, send_sem, recv_sem):
    brow, column = lax.axis_index("brow"), lax.axis_index("bcol")
    row, half = brow // 2, brow % 2
    own = buf.at[pl.ds(0, 384)]
    load = pltpu.make_async_copy(upper_ref, own, in_sem.at[0])
    load.start()
    load_mask = pltpu.make_async_copy(mask_hbm, mask_ref, in_sem.at[1])
    load_mask.start()

    def leaf(plan):
        origins, targets, sends = plan
        count[0] = len(origins)
        count[1] = targets
        count[2] = len(sends)
        for i, v in enumerate(origins):
            origin[i] = v
        for i, v in enumerate(sends):
            table[i] = v

    choose(row * 16 + column, 0, 256, leaf)
    sends = count[2]
    barrier = pltpu.get_barrier_semaphore()

    @pl.loop(0, count[0])
    def _(i):
        v = origin[i]
        there = ((v >> 4) & 15) * 2 + (half ^ (v >> 8))
        pl.semaphore_signal(barrier, inc=1, device_id=(there, v & 15), device_id_type=MESH)

    load_mask.wait()
    load.wait()
    for i in range(3):
        for j in range(6):
            keep = mask_ref[i, j].astype(jnp.float32)
            at = (pl.ds(i * 128, 128), pl.ds(j * 128, 128))
            buf[at] = (buf[at].astype(jnp.float32) * keep).astype(jnp.bfloat16)

    @pl.when(count[1] > 0)
    def _():
        pl.semaphore_wait(barrier, count[1])

    def slot(index):
        return buf.at[pl.ds(pl.multiple_of(index * SIZE, SIZE), SIZE)]

    def copy(v, i):
        there = ((v >> 20) & 15) * 2 + (half ^ ((v >> 24) & 1))
        return pltpu.make_async_remote_copy(
            src_ref=slot(v & 255),
            dst_ref=slot((v >> 8) & 255),
            send_sem=send_sem.at[i],
            recv_sem=recv_sem.at[(v >> 8) & 255],
            device_id=(there, (v >> 16) & 15),
            device_id_type=MESH,
        )

    def arrived(index):
        pltpu.make_async_copy(slot(index), slot(index), recv_sem.at[index]).wait()

    @pl.loop(0, sends)
    def _(i):
        v = table[i]

        @pl.when((v & (1 << 25)) != 0)
        def _():
            arrived(v & 255)

        @pl.when((v & (1 << 26)) != 0)
        def _():
            copy(v, i).start()

    has0 = (row == 0) | ((column >= row) & (row + column >= 16))
    has1 = (column < 15) & ((row <= 1) | ((column + 1 >= row) & (row + column >= 16)))
    here = pl.ds(pl.multiple_of(half * 384, 128), 384)
    other = pl.ds(pl.multiple_of(384 - half * 384, 128), 384)

    def rows(index):
        return buf[pl.ds(pl.multiple_of(index * SIZE, SIZE), 384), :]

    @pl.when(has0)
    def _():
        @pl.loop(0, CHUNKS)
        def _(j):
            arrived(SIB + j)

        right = jnp.where(row + column == 0, 0, RIGHT0)
        acc[:, here] = nt_dot(rows(0), rows(right))
        acc[:, other] = nt_dot(rows(0), rows(SIB))

    @pl.when(has1)
    def _():
        @pl.loop(0, CHUNKS)
        def _(j):
            arrived(SIB + CHUNKS + j)

        left = jnp.where(column == 0, RIGHT1, LEFT)
        for columns, right in ((here, RIGHT1), (other, SIB + CHUNKS)):
            term = nt_dot(rows(left), rows(right))

            @pl.when(has0)
            def _():
                out_ref[:, columns] = (acc[:, columns] + term).astype(jnp.bfloat16)

            @pl.when(jnp.logical_not(has0))
            def _():
                out_ref[:, columns] = term.astype(jnp.bfloat16)

    @pl.when(has0 & jnp.logical_not(has1))
    def _():
        out_ref[...] = acc[...].astype(jnp.bfloat16)

    @pl.when(jnp.logical_not(has0 | has1))
    def _():
        out_ref[...] = jnp.zeros_like(out_ref)

    @pl.loop(0, sends)
    def _(i):
        v = table[i]

        @pl.when((v & (1 << 26)) != 0)
        def _():
            copy(v, i).wait_send()


def per_device(upper_store, block_mask):
    return pl.pallas_call(
        kernel,
        out_shape=jax.ShapeDtypeStruct((384, 768), jnp.bfloat16),
        in_specs=[pl.BlockSpec(memory_space=pl.ANY)] * 2,
        out_specs=pl.BlockSpec(memory_space=pltpu.VMEM),
        scratch_shapes=[
            pltpu.VMEM((SLOTS * SIZE, 768), jnp.bfloat16),
            pltpu.VMEM((384, 768), jnp.float32),
            pltpu.SMEM((3, 6), jnp.int32),
            pltpu.SMEM((MAX_SENDS,), jnp.int32),
            pltpu.SMEM((MAX_FROM,), jnp.int32),
            pltpu.SMEM((3,), jnp.int32),
            pltpu.SemaphoreType.DMA((2,)),
            pltpu.SemaphoreType.DMA((MAX_SENDS,)),
            pltpu.SemaphoreType.DMA((SLOTS,)),
        ],
        compiler_params=pltpu.CompilerParams(
            collective_id=0, has_side_effects=True, vmem_limit_bytes=60 * 2**20
        ),
        name="cannon_steps",
    )(upper_store, block_mask)


def solution(mesh):
    spec = P("brow", "bcol")
    return jax.shard_map(per_device, mesh=mesh, in_specs=(spec, spec), out_specs=spec, check_vma=False)
```

```python
import jax
import jax.numpy as jnp
from jax import lax
from jax.experimental import pallas as pl
from jax.experimental.pallas import tpu as pltpu
from jax.sharding import PartitionSpec as P

CHUNKS = 6
SLOTS = 46
SIB = 34
PLAN = (
    ((1, 10, 14, 16, 17, 18, 19, 31, 224, 240, 241, 256), 6, (83894784, 83895041, 83895298, 83895555, 83895812, 83896069, 102630937, 115808792, 74059032, 103682075, 101717274, 117452055, 103683612, 117451284, 117451798, 103683101, 117451541, 117451027, 117450770)),
    ((2, 3, 13, 15, 17, 18, 33, 48, 65, 225, 227, 257), 12, (68295428, 81795586, 67114757, 68360707, 82843649, 82909696, 117517334, 68225558, 117516049, 68163345, 117516820, 68225044, 117515278, 68162574, 103683353, 117515021, 68162317, 100863514, 117515792, 68163088, 104665112, 117515535, 117516306, 68224530, 117514764, 117517077, 117517591, 117516563, 33554439, 33554440, 33554443, 33554442, 33554441, 33554438)),
    ((3, 18, 19, 32, 34, 50, 51, 130, 194, 226, 258), 7, (81860610, 68294661, 67176193, 81860868, 117580300, 68360460, 81991683, 117580557, 68227853, 81991936, 101845272, 117580814, 68228110, 117581328, 117581071, 68228624, 68228367, 117581585, 117581842, 117582099, 117583127, 117582356, 117582613, 117582870, 33554440, 33554441, 33554438, 33554439, 33554442, 33554443)),
    ((1, 5, 17, 18, 19, 20, 33, 35, 36, 49, 51, 53, 195, 242, 259), 7, (79828996, 68294912, 67241986, 81926149, 68295169, 67242243, 100731928, 101911065, 117647121, 68294417, 117645836, 117648663, 68293132, 117648149, 117647892, 117646607, 68293903, 117648406, 117646093, 117647378, 117646864, 117647635, 117646350, 33554441, 33554442, 33554440, 33554438, 33554443, 33554439)),
    ((5, 19, 21, 23, 54, 66, 68, 84, 86, 96, 164, 180, 226, 228, 260), 8, (79894530, 68360196, 68425731, 82974721, 68426240, 117711886, 70457614, 67442693, 101976344, 102107417, 117712400, 68359696, 117712657, 68359953, 117711372, 117712143, 117713428, 117713171, 117714199, 117713685, 117713942, 117711629, 117712914, 33554443, 33554440, 33554441, 33554439, 33554442, 33554438)),
    ((4, 7, 20, 21, 37, 67, 69, 71, 73, 82, 83, 197, 229, 245, 261), 8, (78911488, 67373829, 81926401, 67373058, 82057732, 67373315, 101910041, 100862744, 117777679, 68424975, 117778193, 68425489, 117777422, 117777165, 68424461, 117778450, 117779735, 117778707, 117779221, 117778964, 117776908, 117779478, 117777936, 33554440, 33554438, 33554441, 33554439, 33554442, 33554443)),
    ((7, 12, 21, 22, 23, 38, 55, 56, 87, 100, 102, 113, 118, 130, 134, 228, 230, 262), 10, (80025600, 69540353, 68491266, 82123523, 102041368, 82123780, 102107930, 83171589, 117843472, 68490768, 117842444, 68489740, 105647385, 67574553, 73077529, 117842958, 117843215, 117844500, 117844757, 117844243, 117845271, 117845014, 117843986, 117842701, 117843729, 33554442, 33554441, 33554443, 33554440, 33554439, 33554438)),
    ((6, 9, 22, 23, 24, 27, 39, 73, 86, 87, 101, 103, 119, 231, 263), 11, (82057472, 69605634, 68556805, 70720257, 67504644, 67504387, 106567960, 102172953, 117909008, 74124568, 68556304, 100995866, 117907980, 68555276, 117909265, 68556561, 117908751, 117910550, 117909522, 101386011, 117910036, 117910293, 117908237, 117910807, 117909779, 117908494, 33554439, 33554443, 33554438, 33554441, 33554440, 33554442)),
    ((10, 23, 24, 25, 40, 42, 70, 89, 104, 120, 136, 166, 232, 248, 264), 13, (82253824, 68622853, 68688129, 69474563, 82254084, 67705091, 105520152, 67700760, 78125570, 68623106, 113842713, 75043864, 68684569, 117974030, 68753678, 78126084, 104406299, 102237978, 68753947, 74059803, 117973773, 68621069, 117975058, 117975829, 117974287, 117975315, 117976086, 117974544, 117975572, 117974801, 117973516, 117976343, 33554441, 33554442, 33554440, 33554438, 33554439, 33554443)),
    ((8, 11, 24, 25, 26, 27, 41, 43, 89, 105, 135, 137, 153, 231, 233, 235, 265), 13, (68753411, 68622594, 81139713, 75041792, 68688388, 83302661, 72947972, 80222469, 69737217, 68688896, 69737733, 107679512, 68815128, 101124377, 102304282, 118039052, 102303259, 102304540, 118039823, 118039566, 68686862, 118040080, 118040594, 118041622, 118040851, 118041879, 118040337, 118041365, 118041108, 118039309, 33554443, 33554441, 33554440, 33554438, 33554439, 33554442)),
    ((11, 26, 27, 42, 168, 170, 186, 187, 196, 200, 202, 230, 236, 266), 11, (82188288, 67115009, 69736451, 67639298, 67835909, 68884483, 82450693, 67640068, 102369048, 104537611, 118105102, 68752398, 118104845, 118107415, 118104588, 68751884, 118105616, 118106130, 118106644, 118106901, 118106387, 118107158, 118105873, 118105359, 33554440, 33554438, 33554439, 33554441, 33554442)),
    ((7, 10, 26, 27, 28, 43, 75, 163, 169, 171, 173, 182, 185, 187, 216, 218, 235, 267), 9, (70719746, 68818945, 67767045, 82450436, 70981888, 68819203, 67766274, 70589188, 67765760, 101255960, 70851075, 82451461, 118170895, 68818191, 118171666, 118171923, 118170638, 118172437, 118172180, 118170381, 118172694, 118170124, 118172951, 118171409, 118171152, 33554438, 33554442, 33554443, 33554441, 33554440, 33554439)),
    ((13, 24, 29, 44, 204, 205, 215, 218, 222, 234, 238, 252, 268), 10, (67508481, 72093186, 68950016, 68884740, 69868035, 68884997, 70982400, 70720517, 102500120, 118236945, 72093700, 102500633, 69016081, 72093957, 118237973, 80480533, 118236688, 118236174, 68883470, 118238230, 118237459, 118238487, 118237202, 118235660, 118236431, 118237716, 118235917, 33554443, 33554439, 33554442, 33554441, 33554440, 33554438)),
    ((15, 28, 29, 43, 45, 192, 193, 203, 205, 207, 219, 221, 222, 223, 237, 269), 14, (71047682, 69015555, 67180548, 68688644, 71109632, 69015809, 69146882, 69998597, 116333080, 67898117, 68880152, 71110917, 102636057, 72159513, 105713690, 68946458, 118302738, 118301453, 68948749, 118301967, 68949263, 118303252, 118301196, 68948492, 118303509, 118302995, 118302481, 118303766, 118304023, 118301710, 118302224, 33554439, 33554442, 33554438, 33554441, 33554440, 33554443)),
    ((15, 16, 30, 31, 46, 224, 238, 239, 240, 252, 255, 270), 9, (70126592, 69146626, 68098305, 70127363, 67115780, 68098820, 70127877, 102631960, 70126849, 102565913, 71244292, 118367760, 69015056, 100670728, 69144072, 70127106, 118367503, 118366989, 118369302, 118367246, 102699018, 118369559, 118369045, 82708757, 118368788, 102698247, 118366732, 82708500, 118368274, 118368017, 118368531, 33554441, 33554438, 33554443)),
    ((14, 17, 28, 30, 31, 225, 239, 241, 255, 271), 11, (69212933, 68163588, 69143552, 70128385, 67180803, 68028418, 104732440, 105714970, 101517081, 68028675, 101517851, 69144323, 118432525, 100733724, 105713181, 118433553, 69080849, 101517342, 118433296, 69080592, 118432268, 118433039, 118432782)),
    ((0, 1, 15, 30, 224, 272), 6, (100670488, 68028952, 105323033, 82909977, 104729882, 71176217, 104729627, 118500631, 118499346, 118499860, 118500117, 118499603, 118500374)),
    ((1, 2, 18, 19, 31, 49, 241, 273), 8, (81795328, 67178757, 67311616, 67177986, 67115523, 67177729, 101653511, 67178500, 103747608, 67178243, 118565139, 100734731, 103682585, 118564882, 118565396, 118565910, 118566167, 118565653, 33554442, 33554440, 33554441, 33554438)),
    ((1, 2, 3, 34, 48, 80, 210, 240, 242, 274), 9, (71374851, 82909189, 68224769, 69278208, 67180036, 67179522, 100731672, 100795929, 100796186, 100668955, 118631446, 67309590, 118630932, 118631703, 118630418, 118630675, 118631189, 33554441, 33554440, 33554442, 33554438, 33554443, 33554439)),
    ((1, 2, 3, 4, 5, 21, 51, 53, 81, 85, 115, 243, 275), 9, (72357892, 80877570, 67246083, 80877824, 82974981, 82975233, 100862488, 101782041, 100668698, 118695954, 118696211, 67374355, 118696982, 118696725, 118697239, 118696468, 33554442, 33554440, 33554439, 33554438, 33554441, 33554443)),
    ((4, 5, 21, 23, 26, 28, 52, 114, 212, 244, 276), 11, (74651653, 67311876, 83040258, 67442944, 68491521, 100862232, 83040515, 100861466, 105191705, 70851609, 102106652, 73142553, 118762518, 108662043, 118761490, 67439634, 67440662, 118762261, 118762775, 118762004, 118761747, 33554439, 33554441, 33554442, 33554438, 33554443, 33554440)),
    ((6, 20, 23, 53, 117, 149, 211, 229, 245, 247, 277), 8, (81008644, 67377155, 68421377, 83105797, 83106304, 83106562, 100993048, 101910297, 118827283, 67505427, 118827540, 118828054, 118828311, 118827026, 118827797, 33554439, 33554442, 33554443, 33554441, 33554440, 33554438)),
    ((4, 6, 7, 20, 38, 54, 86, 116, 228, 246, 278), 8, (80943107, 67508225, 82123013, 68622340, 83171330, 83302912, 101059352, 118892819, 67570963, 118893076, 67571220, 118893590, 118892562, 118893847, 118893333, 33554443, 33554441, 33554439, 33554438, 33554440, 33554442)),
    ((7, 8, 9, 22, 24, 25, 55, 57, 151, 166, 213, 247, 249, 279), 13, (82057218, 67377411, 69605380, 67508741, 83236865, 68426752, 102042136, 111548697, 67635225, 75042329, 101124890, 80222746, 101124123, 118959383, 118958098, 118958869, 118958612, 118958355, 118959126, 33554439, 33554441, 33554442, 33554443, 33554440, 33554438)),
    ((8, 9, 13, 28, 40, 56, 120, 152, 214, 233, 246, 280), 13, (67574019, 83302405, 70850564, 83433986, 68617985, 83434240, 114825753, 67569433, 101190170, 105649691, 67897883, 107681304, 101189148, 73142296, 119023891, 67702035, 119023634, 119024919, 119024662, 119024405, 119024148, 33554443, 33554439, 33554441, 33554440, 33554438, 33554442)),
    ((8, 9, 10, 26, 187, 200, 215, 245, 249, 281), 11, (80156672, 72882180, 67639557, 80287747, 69736707, 67639809, 80288002, 69802497, 116791832, 67635480, 75042584, 83237122, 103357191, 102175769, 101255706, 119090198, 119089684, 119090455, 119089427, 119089941, 119089170, 33554442, 33554438, 33554443, 33554440, 33554441)),
    ((9, 10, 11, 42, 58, 60, 182, 185, 202, 216, 218, 282), 12, (83106050, 71702532, 68749057, 80878080, 70785285, 68426497, 83368195, 67705348, 105520408, 67766040, 67705600, 101320985, 67705861, 119155734, 67833878, 119154963, 119155477, 119155220, 119155991, 119154706, 33554439, 33554441, 33554440, 33554438, 33554443, 33554442)),
    ((10, 12, 13, 28, 29, 57, 59, 61, 203, 211, 219, 221, 283), 9, (70719488, 67573761, 67770369, 70916357, 67704835, 71113476, 69540866, 101255448, 70916866, 101386777, 101387034, 119221270, 119220499, 119221013, 119220242, 119221527, 119220756, 33554442, 33554439, 33554441, 33554440, 33554438, 33554443)),
    ((12, 13, 29, 30, 220, 252, 284), 13, (68425989, 70653955, 67966977, 68687876, 69081089, 70916096, 68880900, 69868290, 101653768, 71178760, 101385752, 106697222, 119286806, 67964950, 119286035, 119286292, 119286549, 119287063, 119285778, 33554439, 33554441, 33554442, 33554443)),
    ((12, 13, 14, 30, 59, 235, 236, 241, 253, 255, 285), 10, (68945922, 81861120, 70064131, 67901441, 67967237, 72158465, 67901699, 67967492, 68945408, 103553304, 103553817, 67897113, 71110424, 71109913, 102438682, 119352085, 119351314, 119351571, 119352342, 119352599, 119351828, 33554438, 33554441, 33554440, 33554442, 33554443, 33554439)),
    ((0, 13, 14, 15, 28, 47, 62, 239, 240, 254, 286), 11, (69540101, 82122753, 68032770, 68098563, 69010944, 71175682, 68163844, 81992192, 69011715, 68164097, 71175939, 68164352, 106695960, 101586713, 104732170, 104731142, 102501146, 119417107, 119417621, 119417364, 119418135, 119417878, 119416850, 33554439, 33554441, 33554443, 33554440)),
    ((13, 14, 15, 46, 287), 9, (77666306, 67115264, 70129667, 68098053, 68032516, 68229124, 70192385, 70192128, 104666136, 119480844, 68229388, 68099608, 68027916, 104664601, 119481615, 119481358, 119481872, 119482129, 119481101)),
    ((15, 34, 35, 76), 4, (100797976, 100798233, 100798746, 70327066, 103683867, 100799260, 107876381)),
    ((18, 51, 52, 63), 4, (100865816, 100863769, 100733466, 105913371, 72289307)),
    ((35, 51), 4, (69212162, 70391812, 67243008, 69212419, 67243265, 69212677, 101848600, 100800281)),
    ((51, 52, 62), 7, (100864280, 75634947, 69213185, 69343493, 70392320, 70457858, 100865561, 70392580, 100864538, 100864795, 107812124)),
    ((8, 45, 52, 59, 62), 5, (100865304, 110760730, 109580057, 107746331, 104663324)),
    ((6, 27, 30, 85, 86), 5, (100995352, 103815961, 70983449, 72161049, 100996379, 107679260, 100992794)),
    ((7, 23, 42, 55), 5, (102107672, 106503194, 101058585, 76156698, 107615259)),
    ((59, 60, 119, 120), 2, (101126424, 109775898, 109778459, 101126937)),
    ((9, 10, 25, 42, 134, 136), 5, (107613976, 102238489, 109711386, 101189403, 101191708, 77141530, 101190429, 101193502)),
    ((25, 153, 154), 9, (70326533, 83433475, 70588929, 81336320, 77139458, 70589700, 104340248, 67702552, 110629658, 76090650, 101259033, 109646619)),
    ((12, 28, 43, 55, 60, 136, 171), 14, (82581509, 69605891, 76156418, 82319360, 69736964, 78256385, 109712921, 103488282, 72093466, 103488539, 101191452, 73141787, 70983707, 101323544, 108793885, 102368798)),
    ((42, 46, 61, 154), 12, (82450944, 69867780, 75174149, 70850817, 83564803, 72161538, 107810328, 101258777, 101516826, 106632475, 67832091, 107680796)),
    ((13, 29, 60, 61), 8, (81795073, 70588672, 71047171, 70981637, 71112706, 71964676, 105649944, 101452057, 72095001, 101451802, 105648923, 101451292, 72094236)),
    ((29, 46, 62, 125), 12, (81926656, 69475074, 73144581, 70982146, 71113728, 73207812, 70982915, 70392835, 73207041, 105713432, 104406554, 112004121, 74256922, 101517595, 71111963, 101518108)),
    ((0, 1, 14, 15, 17, 31, 32, 60, 62, 63, 64, 74, 78, 108, 302), 12, (70326787, 71113217, 72224772, 72223744, 120463884, 69933580, 104731928, 72225029, 71244556, 120464655, 70064911, 111939097, 104728346, 72224258, 120465169, 70065169, 71179025, 120465683, 68028179, 120464141, 71111437, 111808795, 105780746, 71241738, 120464398, 105779718, 120466711, 69144855, 71240710, 105779975, 68029207, 120466197, 120464912, 120466454, 120465426, 120465940, 33554440, 33554441, 33554443)),
    ((17, 31, 62, 63, 303), 8, (71309314, 71047425, 71241475, 71178244, 71241989, 71178496, 71240961, 105843992, 120529677, 69076749, 71176973, 120529420, 105714713, 120530448, 120530705, 120530191, 120529934)),
    ((37, 51, 60, 62, 63), 6, (100735512, 68293656, 111483161, 75238937, 106826778, 104730907, 106827804)),
    ((32, 41, 46, 51, 64, 65), 7, (116398360, 67308824, 104864538, 101783323, 73209114, 110694681, 101779740, 104795677)),
    ((34, 35, 45, 63), 3, (100798488, 100799002, 106829337, 100800027, 107746588)),
    ((4, 35, 52), 9, (70260738, 69343236, 70588416, 69408773, 70326273, 69277955, 100865048, 100799514, 101913625)),
    ((67, 85), 5, (69277701, 69474307, 70457346, 69409028, 69409280, 69409537, 101979672, 101979161)),
    ((11, 41, 44, 51, 84, 87), 6, (100863000, 108728857, 110693658, 101913884, 106631195, 102044958, 110694429)),
    ((28, 58, 69, 101), 7, (107420440, 70851352, 110565914, 73142040, 100930073, 77204506, 102110491)),
    ((7, 11, 12, 27, 136), 6, (103423512, 74124312, 103160601, 73076249, 101058331, 106632988, 102176026)),
    ((26, 41, 103, 153), 4, (101062424, 102240794, 107552025, 102241563, 75108633)),
    ((8, 11, 20, 24, 43, 45, 54), 7, (102173208, 108727577, 107615514, 73076506, 102435099, 108598813, 104662558, 102435612)),
    ((27, 28, 61), 10, (79305475, 72882433, 70654464, 83368452, 79305989, 104668440, 79306242, 108664601, 71048473, 108795674, 73141272, 102369307, 75109403, 102369820)),
    ((10, 11, 12, 37, 42, 44, 45, 62), 11, (82515972, 71965443, 69474817, 83433730, 69671424, 82516997, 108730136, 106630169, 106631707, 106762013, 106761754, 104662812, 102566687, 106631454, 102434848)),
    ((13, 44, 47, 58, 61, 74), 12, (70260994, 75238657, 81402115, 107745048, 75239685, 69671684, 103679769, 79436800, 69868804, 103553562, 72094746, 111807515, 108795420, 102370077)),
    ((1, 13, 27, 29, 31, 36, 44, 45, 46, 57, 58, 59, 62, 63, 91, 109, 317), 13, (70916613, 82582272, 72161793, 71048196, 69933058, 108729368, 74256131, 111873305, 106763034, 104471579, 74125339, 121446924, 69999628, 106761244, 121448980, 121448209, 107680285, 68879901, 121447695, 121447438, 121448723, 121447181, 121447952, 121449494, 121448466, 121449237, 121449751, 33554442, 33554440, 33554441, 33554439, 33554438, 33554443)),
    ((15, 16, 28, 30, 46, 47, 48, 79, 94, 161, 318), 15, (71243780, 82647301, 70064640, 73272577, 71244034, 69475331, 70982657, 73272834, 103680536, 80550148, 69409795, 121512974, 70195470, 73273605, 103679513, 70261248, 121513231, 73273091, 121514773, 69077269, 121515287, 70193431, 106697754, 69077783, 70192917, 121514259, 121512717, 104666907, 121514516, 69077012, 70192660, 121513488, 121512460, 121515030, 121514002, 121513745, 33554439, 33554441, 33554440, 33554443, 33554438, 33554442)),
    ((14, 46, 47, 49, 62, 319), 10, (69278464, 72227074, 70195201, 70392068, 70130177, 72290565, 73274627, 121578767, 72226063, 72290051, 121579281, 72226577, 103816216, 71109144, 121578253, 104663065, 104666650, 104665627, 121579024, 121577996, 121578510)),
    ((47, 49, 79), 7, (103882008, 72225816, 70125592, 108075801, 72222233, 74322457, 109843994, 72092186, 105778971)),
    ((18, 92), 4, (103881752, 67179800, 111024409, 78320409)),
    ((68, 69, 74, 76, 79), 7, (100929816, 100931097, 111808282, 110566171, 106109724, 72222748, 76288283, 74322972)),
    ((85, 86, 94), 4, (104077592, 67440152, 108337945, 76354329, 100996122)),
    ((69,), 6, (72423425, 67374594, 72620036, 73406464, 72685568, 71440389, 72620291, 100930584, 100930841)),
    ((20, 85), 7, (71440644, 77862913, 70654208, 72751365, 71571458, 100994840, 71571715, 107681561)),
    ((26, 74, 137), 3, (108662808, 111808538, 101193241, 111808027)),
    ((16, 75, 86, 93), 4, (100995609, 109906968, 111875099, 105715226)),
    ((77,), 1, (109843480,)),
    ((86, 92, 120), 4, (100996632, 106437145, 78320153, 101127962)),
    ((8, 26, 44, 59, 91, 93, 123), 12, (71440899, 71047936, 78253313, 71703044, 70130437, 71703298, 106633752, 74190872, 106694169, 110761243, 108661530, 107613724, 105645598, 106630429, 74060573)),
    ((76, 91, 92), 8, (83564544, 72817154, 77271301, 72620804, 77270787, 72817412, 105323288, 73074712, 77270273, 111873817, 106628634, 106629403, 106629660, 101386269, 73077789)),
    ((6, 12, 24, 42, 44, 60, 64, 74, 78, 91, 92, 93, 100, 108, 125, 332), 12, (71441157, 73078784, 76287490, 82712579, 72948227, 76287233, 102767896, 75306520, 76288004, 106695193, 122430478, 72031502, 77338137, 106694682, 122430992, 73078288, 122431249, 122432020, 107744027, 122430735, 107746844, 122432534, 122430221, 122432791, 122432277, 122431763, 122431506, 122429964, 33554440, 33554443, 33554442, 33554438, 33554439, 33554441)),
    ((13, 15, 29, 37, 43, 45, 47, 61, 71, 78, 79, 94, 125, 225, 227, 229, 333), 10, (75304707, 72292356, 71833602, 73209861, 73144322, 75304193, 73079040, 105847576, 73206552, 122495757, 73143053, 108727833, 106568218, 74255642, 122496271, 73143567, 122496785, 73144081, 122497813, 122498327, 122496528, 73143824, 107811611, 122495500, 122497299, 122497042, 122497556, 122496014, 122498070, 33554442, 33554439, 33554441, 33554440, 33554438, 33554443)),
    ((46, 63, 64, 66, 93, 94, 95, 110, 334), 13, (72095748, 72554757, 74320896, 72292609, 72157700, 72423939, 74321410, 73275395, 74322181, 73275650, 106760472, 75370264, 74321153, 106828825, 108925210, 122562064, 73341200, 105913627, 73271579, 122561036, 73341452, 122562321, 73209617, 122561550, 73208846, 122563349, 70125845, 122563092, 122563863, 70126359, 107878155, 122563606, 122562578, 122561807, 122561293, 122562835, 33554438, 33554440, 33554441, 33554439, 33554442)),
    ((33, 47, 63, 77, 78, 94, 95, 335), 12, (71309568, 75372547, 73338113, 71441410, 73338884, 104864280, 75304984, 73339141, 105711385, 75305753, 73338627, 122627857, 73275153, 107941146, 73271066, 122626829, 73274125, 109909787, 122627343, 122626572, 71173644, 107811868, 122627086, 122627600)),
    ((19, 33, 78, 92, 95), 5, (101845528, 108925465, 106826523, 110891290, 106828316, 107941661, 75371805)),
    ((68, 78, 94), 4, (101913368, 109386009, 73205785, 108860698)),
    ((86, 93), 2, (110892824, 100996890, 110892057)),
    ((66, 78, 85, 94), 4, (100994328, 108861209, 109909274, 106892827)),
    ((68, 75, 91), 4, (100929560, 104143897, 67374873, 112858138, 111810075)),
    ((68,), 7, (74586112, 71505922, 70522884, 71636995, 72554497, 69539845, 101913112)),
    ((69, 91, 119), 10, (72489477, 69540611, 71899140, 71768320, 102109976, 71506434, 67574273, 100931353, 111613978, 79304474)),
    ((75, 102, 120), 5, (104144408, 67505944, 101127193, 109451802, 77270554, 110825499)),
    ((25, 58, 73), 4, (110630424, 115939865, 77204761, 110890010)),
    ((9, 38, 76, 137, 154), 5, (108597273, 101192475, 110826778, 101258520, 110695708)),
    ((7, 77, 123), 2, (108661016, 108663577, 108794650)),
    ((6, 43, 53, 55, 57, 59, 74, 75, 76, 77, 93, 95, 347), 13, (72620546, 71112961, 72030467, 76225284, 72751621, 82516480, 110826008, 105520665, 74062105, 75303961, 108729882, 123413004, 74060300, 123414546, 72092690, 123413518, 123414803, 123415574, 123415831, 123415060, 123413261, 123414032, 123414289, 123415317, 123413775, 33554440, 33554439, 33554443, 33554438, 33554441, 33554442)),
    ((20, 24, 28, 30, 42, 45, 54, 58, 62, 74, 76, 77, 93, 124, 156, 348), 12, (72030210, 71375105, 82123267, 77336580, 73210113, 71899392, 73340933, 83630850, 72030720, 72358405, 105646104, 72030979, 77336323, 72031236, 106896153, 74192665, 110891526, 123480339, 123478797, 123479311, 123480082, 123479054, 123478540, 123480853, 123480596, 123479825, 123481367, 123479568, 123481110, 33554439, 33554442, 33554440, 33554441, 33554443)),
    ((45, 49, 59, 61, 77, 78, 81, 92, 95, 117, 124, 141, 349), 11, (72488965, 71964928, 74258435, 72096004, 73139969, 72489218, 71768064, 74258945, 72096258, 105646872, 106628889, 75305240, 123545104, 72096784, 123544333, 74191629, 123545875, 72224019, 123546389, 123544076, 123546903, 123544847, 123546132, 123544590, 123546646, 123545618, 123545361, 33554441, 33554443, 33554440, 33554438, 33554442, 33554439)),
    ((48, 50, 62, 63, 78, 79, 80, 95, 111, 126, 350), 11, (72423682, 73472000, 72161285, 72226819, 71506177, 75370500, 72227333, 75369472, 72555011, 75369729, 105711896, 74321688, 123609869, 72162061, 123610126, 72293390, 123610897, 123611925, 71174421, 105711641, 123610383, 123611668, 71174164, 72289812, 123612439, 71174935, 123612182, 71174678, 72290326, 108926474, 123611411, 123609612, 123611154, 123610640, 33554440, 33554441, 33554439, 33554443, 33554438)),
    ((78, 79, 83, 92, 113, 351), 10, (72227587, 74387460, 72358144, 72292865, 74387717, 72358661, 74386946, 123675405, 74322701, 73271298, 123676176, 74323472, 116072728, 73075480, 123676433, 72223505, 123675919, 106763801, 106762778, 106762523, 123675148, 123675662)),
    ((68, 125, 143), 3, (100928536, 112071961, 109843738)),
    ((94, 110), 2, (109908504, 107808281)),
    ((109,), 1, (111941400,)),
    ((126,), 1, (109909528,)),
    ((103, 108, 115, 125, 140), 5, (112924440, 101061145, 114036250, 105646363, 107611932)),
    ((108, 119, 120, 122, 124, 126), 6, (104209176, 67571480, 101127705, 110237978, 107677211, 80417562, 112005660, 113972765)),
    ((103,), 5, (74782721, 76879877, 72816643, 74782978, 75896834, 67506180, 67505152, 101061656)),
    ((54, 119, 120), 8, (74520580, 75634689, 70785029, 73799682, 74848259, 73668864, 101125144, 101126681, 101127450, 107681051)),
    ((109, 121, 123, 136), 4, (101190936, 109714457, 74188825, 109580826, 109713179)),
    ((56, 108, 122, 139, 214), 5, (112923672, 74123288, 108595993, 108595738, 101258267, 108596508, 109647645)),
    ((0, 8, 38, 40, 57, 74, 91, 100, 107, 122, 123, 124, 187, 230, 234, 362), 5, (124396815, 75044111, 111939352, 124397329, 75044625, 79369496, 124396301, 124398614, 75043597, 124396044, 109842969, 124397072, 124398871, 124396558, 124398357, 124397843, 124398100, 124397586, 33554441, 33554440, 33554438, 33554442, 33554443, 33554439)),
    ((7, 9, 24, 37, 43, 55, 61, 69, 101, 103, 105, 108, 122, 124, 125, 239, 363), 9, (74651905, 79367168, 75175938, 75110916, 79367939, 74783236, 75176709, 74057987, 108792344, 78450712, 124461580, 75108876, 124462351, 75109647, 108727065, 124461837, 124462608, 75109904, 124462094, 124464150, 124463379, 124463893, 124462865, 124463636, 124464407, 124463122, 33554439, 33554443, 33554442, 33554440, 33554441, 33554438)),
    ((36, 50, 60, 74, 76, 92, 93, 104, 123, 124, 125, 172, 224, 226, 236, 364), 12, (73668613, 75241475, 78385156, 70129922, 73996290, 73734912, 74123009, 74124037, 76159488, 74123780, 108726296, 108791833, 78384385, 108792090, 124528144, 124527887, 75175183, 105645851, 76288795, 124529943, 124527373, 124528915, 124528401, 124529172, 124527630, 124529429, 124528658, 124529686, 124527116, 33554438, 33554440, 33554439, 33554443, 33554441, 33554442)),
    ((35, 43, 45, 61, 77, 79, 93, 97, 111, 124, 126, 127, 157, 205, 237, 365), 15, (74717444, 73931010, 79501827, 82582017, 75307013, 75241728, 73537541, 75045122, 108796440, 76353304, 75307520, 116071961, 75172121, 109907226, 75307780, 124593423, 75240719, 109777691, 109778716, 124592909, 124595479, 71109399, 124593166, 75240462, 110957576, 124594194, 124595222, 124594965, 124594451, 124593937, 124594708, 124592652, 124593680, 33554441, 33554438, 33554439, 33554443, 33554442)),
    ((32, 64, 66, 78, 94, 95, 111, 126, 127, 142, 366), 9, (74389762, 76419333, 75438081, 83695619, 75372803, 76419076, 124658188, 75305484, 73472256, 76418048, 124658702, 75438350, 108927495, 76418305, 124659473, 108857112, 76418562, 124658445, 108990474, 108857625, 76420618, 124660501, 72222997, 124659987, 124658959, 72222483, 124660758, 124659730, 72223254, 109974022, 108990731, 124660244, 124659216, 124661015, 33554440, 33554441)),
    ((79, 80, 95, 110, 126, 127, 367), 10, (74520835, 74319617, 76420869, 75435522, 75435008, 74320388, 111023896, 75435265, 124724752, 73271824, 112006682, 107808793, 124725009, 75372305, 112005915, 124724238, 75371534, 77466907, 124723981, 75371277, 124724495, 124723724)),
    ((125,), 1, (112989976, 112988953)),
    ((64, 103, 111, 126), 6, (101062168, 109974809, 110107162, 75303450, 75435801, 106892315)),
    ((85,), 1, (101978648,)),
    ((20, 107), 3, (101911320, 107224089, 79367449)),
    ((109, 119), 2, (102110232, 111941145)),
    ((67, 102, 107), 3, (102044440, 102044697, 112922650, 106759963)),
    ((103,), 1, (101061912,)),
    ((), 6, (74717186, 72751105, 73865216, 73734147, 69670917, 67571716)),
    ((123, 137, 153, 155), 11, (73734404, 72816898, 73865472, 69671169, 73865731, 71899653, 108660761, 101192730, 102241819, 76023834, 110757400, 77072923)),
    ((8, 9, 23, 25, 57, 89, 105, 106, 109, 122, 123, 125, 179, 247, 377), 5, (125379084, 73931276, 112004632, 110956057, 125379855, 125381140, 125379598, 125380112, 76027408, 125380369, 125381397, 125381911, 125379341, 125380883, 125381654, 125380626, 33554440, 33554441, 33554438, 33554443, 33554442, 33554439)),
    ((20, 56, 58, 70, 74, 90, 107, 120, 123, 124, 210, 244, 248, 378), 11, (73996549, 75176192, 73996804, 75176449, 75040770, 112924952, 73735448, 75041027, 112987161, 75171353, 113973019, 107612698, 74127643, 79433752, 79434011, 125447447, 125445648, 76092944, 74125591, 125445391, 125445134, 125446676, 125444620, 125446162, 125446419, 125444877, 125446933, 125445905, 125447190, 33554442, 33554438, 33554439, 33554440, 33554443, 33554441)),
    ((43, 53, 57, 59, 61, 77, 91, 107, 108, 109, 122, 125, 138, 183, 187, 251, 379), 11, (71965189, 74979586, 75106820, 73013251, 75105792, 75106049, 107612184, 79367704, 108594713, 125511441, 73931537, 112922907, 108594970, 74058523, 125512983, 74191127, 125512212, 74190356, 125511698, 74189842, 125510670, 76157966, 125510413, 76157709, 125512726, 125510927, 125512469, 125511184, 125511955, 125510156, 33554441, 33554440, 33554438, 33554439, 33554443, 33554442)),
    ((42, 48, 58, 60, 90, 107, 108, 109, 125, 126, 188, 218, 236, 380), 11, (73734657, 75110404, 74258691, 79433218, 74192898, 75110656, 75307265, 75111173, 79433475, 107616280, 74123544, 107742745, 125575949, 74259213, 125576977, 74259473, 106694938, 112989192, 106760731, 112989706, 125578519, 74256663, 125578262, 125576206, 125577234, 74256406, 125578005, 125575692, 125576463, 125576720, 125577491, 125577748, 33554438, 33554441, 33554443, 33554439)),
    ((76, 77, 79, 81, 83, 91, 93, 109, 110, 113, 124, 126, 127, 140, 159, 253, 381), 15, (74455045, 70064384, 74127364, 74193154, 76355843, 74455297, 75044866, 74193411, 75236864, 125641999, 73669391, 73406991, 105650968, 77402392, 108726041, 125641485, 74193677, 109846042, 77401114, 125643798, 125642256, 110956571, 125642770, 72156690, 125642513, 125644055, 125643027, 76289809, 72157975, 110957340, 125641228, 125643541, 74189339, 125643284, 125641742, 33554438, 33554439, 33554441, 33554442, 33554440, 33554443)),
    ((78, 79, 80, 94, 110, 111, 133, 143, 158, 382), 13, (77467138, 82647813, 74323969, 74390020, 75302400, 74521092, 77467395, 74324227, 73735168, 77467909, 125707792, 73603088, 75242256, 74390273, 107877656, 77466624, 125706764, 107809049, 76418841, 125707021, 125707535, 109974298, 125708049, 125709591, 125708306, 73270802, 74386450, 125708820, 125708563, 125709077, 125707278, 125709334, 33554442, 33554438, 33554443, 33554439, 33554441, 33554440)),
    ((110, 111, 113, 383), 9, (83826946, 74389509, 76421121, 76421635, 77469188, 77468160, 125772814, 76420110, 76483584, 108862488, 125772300, 74319372, 74254104, 125772557, 108860441, 125773071, 125773328, 125773585)),
    ((140, 143, 159), 4, (113120793, 109971224, 114036506, 111020827)),
    ((159,), 2, (113119768, 78580760)),
    ((35, 103), 2, (101061400, 100799769)),
    ((132, 158, 159), 4, (110237720, 78581528, 112006425, 109775386)),
    ((140,), 2, (109255192, 80482328, 114035737)),
    ((81, 158), 3, (114103576, 108924441, 76354585)),
    ((87, 102, 137), 4, (101060120, 103292441, 76024601, 111809562)),
    ((153, 154, 157), 4, (101257241, 110565656, 67703320, 110499866, 80547354)),
    ((36, 104, 120, 121, 134, 137, 153, 166, 168, 184, 200, 214, 216, 246, 392), 10, (67636738, 73930753, 77010949, 81074180, 70720003, 77993984, 69868547, 69737476, 101192969, 110627608, 110627097, 110626330, 126362638, 126363923, 126363152, 126362895, 126364951, 126363666, 126364180, 126362381, 126363409, 126364694, 126362124, 126364437, 33554442, 33554439, 33554443, 33554438, 33554440)),
    ((41, 105, 122, 138, 139, 152, 153, 154, 199, 201, 210, 244, 248, 393), 11, (75897093, 71702788, 83367936, 76024067, 74979842, 79173632, 76024324, 72948481, 76023553, 110692120, 67703576, 110692633, 126427660, 77074956, 126428431, 126429973, 126428174, 126427917, 126429716, 126429202, 126429459, 126428945, 126430230, 126430487, 126428688, 33554438, 33554443, 33554441, 33554442, 33554439, 33554440)),
    ((38, 40, 42, 104, 108, 123, 139, 154, 155, 156, 157, 170, 232, 234, 236, 394), 9, (77142021, 76224771, 77142276, 76225537, 77142530, 110758680, 76088832, 110757657, 126493710, 77141006, 111938586, 79368730, 109841179, 126495766, 75173910, 126494481, 77141777, 126494738, 75172882, 111940636, 126493453, 126494224, 126493196, 126493967, 126495252, 126495509, 126496023, 126494995, 33554442, 33554439, 33554443, 33554438, 33554440, 33554441)),
    ((39, 91, 109, 131, 138, 140, 141, 154, 155, 156, 165, 171, 203, 235, 249, 395), 9, (77338880, 76155396, 76154625, 77207554, 76155653, 107551512, 77137944, 113053210, 77207811, 109644057, 109643548, 111874075, 126559760, 126559246, 77206542, 126558732, 77206028, 126560017, 126561302, 126560531, 126559503, 126561559, 126561045, 126560788, 126560274, 126558989, 33554443, 33554440, 33554438, 33554441, 33554439, 33554442)),
    ((64, 66, 72, 76, 96, 106, 108, 125, 138, 142, 155, 156, 157, 172, 187, 238, 396), 15, (75765764, 73669122, 77339137, 77273347, 80482565, 75766016, 77339394, 76221189, 75504131, 76356352, 110823704, 110889754, 81532698, 126624782, 77405454, 110823195, 110888732, 113055001, 126624525, 78515993, 110889245, 77405965, 114038025, 126625296, 77272592, 126626324, 75304468, 111940126, 126625039, 126625553, 126627095, 126626838, 126626067, 126624268, 126626581, 126625810, 33554442, 33554440, 33554443, 33554439, 33554438)),
    ((67, 71, 79, 83, 97, 99, 109, 125, 133, 140, 143, 145, 156, 157, 158, 189, 397), 11, (76814341, 76225026, 79498240, 77338627, 77404165, 76552448, 77404420, 79498497, 77339650, 77404931, 110822936, 114102298, 77335066, 112004889, 109774363, 126690575, 126691346, 73205266, 77337871, 109774620, 126690061, 77337357, 113054471, 113054728, 126691603, 126689804, 126692631, 126692117, 126692374, 126691089, 126691860, 126690318, 126690832, 33554438, 33554443, 33554442, 33554441)),
    ((110, 111, 113, 126, 127, 128, 158, 159, 160, 174, 398), 11, (76617989, 76290307, 77469697, 77535236, 79499776, 76487426, 78515457, 78515200, 111090201, 78515714, 79565081, 111022872, 126756625, 77403921, 111023386, 126756368, 77403664, 126758167, 74320663, 126755340, 77536268, 126755597, 112072202, 126755854, 126757396, 74319892, 126756111, 112071431, 77532423, 126757653, 74320149, 126757910, 126757139, 126756882, 33554438, 33554440, 33554443, 33554441)),
    ((127, 142, 157, 158, 159, 255, 399), 13, (76617733, 73406723, 77600768, 77533188, 75503617, 79567362, 77532160, 112136472, 77532931, 110955033, 77532674, 114101274, 109905947, 126820876, 126821390, 75368462, 77468686, 126821904, 126822161, 126821133, 126821647)),
    ((113, 141, 157), 3, (114037273, 110888472, 111022106)),
    ((142, 143, 158), 7, (111155992, 77533464, 112070937, 77405721, 114104090, 76352281, 112006171)),
    ((101, 131), 3, (113120536, 77465880, 112987417)),
    ((158,), 1, (114103320,)),
    ((141,), 1, (114038552,)),
    ((102,), 2, (115743256, 68491032)),
    ((135,), 1, (115086360,)),
    ((54, 66, 135, 136), 5, (115874072, 68622104, 111743514, 110827291, 110691865)),
    ((41, 88, 120, 136, 137, 153, 157, 184, 201, 212, 408), 4, (102241031, 110888984, 127413270, 68684310, 76091414, 127412499, 127412242, 127413527, 127412756, 127413013, 33554440, 33554443, 33554441, 33554442, 33554438)),
    ((40, 41, 49, 53, 89, 137, 138, 139, 151, 155, 185, 217, 249, 409), 10, (69801987, 77072129, 82384898, 75962628, 70785536, 77072386, 82385157, 74980100, 67701760, 109644568, 76027909, 109644313, 76028163, 109643802, 76028416, 127476750, 127478292, 127476493, 127477007, 127476236, 127477521, 127478806, 127478549, 127477264, 127479063, 127477778, 127478035, 33554440, 33554443, 33554439, 33554442, 33554441, 33554438)),
    ((36, 54, 74, 88, 120, 138, 139, 155, 156, 186, 248, 252, 410), 9, (76224514, 75962368, 72947715, 77273093, 76093441, 69802245, 77273604, 76093699, 69933316, 109709336, 109709593, 127544085, 76222229, 127542543, 127542029, 127543571, 76221715, 127542286, 127542800, 127543057, 127544342, 127541772, 127543828, 127543314, 127544599, 33554441, 33554442, 33554443, 33554439, 33554440, 33554438)),
    ((75, 87, 89, 91, 140, 141, 151, 154, 156, 157, 251, 411), 9, (74979328, 79304962, 76158981, 77203715, 76159233, 77203972, 110693144, 110692890, 127608593, 109775129, 78255889, 127608079, 78255375, 127607565, 78254861, 127608850, 76286994, 127607822, 127609364, 127609878, 127607308, 127609621, 127608336, 127609107, 127610135, 33554442, 33554441, 33554439, 33554438, 33554443, 33554440)),
    ((76, 80, 82, 88, 92, 139, 140, 141, 144, 152, 158, 235, 252, 412), 11, (76290051, 76355584, 77269508, 76290817, 77404677, 109840664, 77405186, 109911066, 80481562, 127673872, 109708825, 78453520, 109774875, 109840412, 127673615, 127675671, 73141015, 76353815, 127675414, 127674900, 76353044, 110761757, 76353558, 127673358, 127674129, 127675157, 127674643, 127673101, 127674386, 127672844, 33554443, 33554442, 33554439, 33554440, 33554441, 33554438)),
    ((109, 121, 125, 140, 141, 142, 143, 145, 156, 159, 189, 191, 205, 219, 236, 253, 413), 12, (75962882, 76552192, 76290565, 76356100, 80547587, 77076482, 76487168, 76291073, 80547073, 76291331, 109714200, 79499544, 113053721, 76286489, 113053467, 110824218, 110823452, 110826525, 127739665, 127741207, 74255127, 127739151, 127740950, 74254870, 113055518, 110826271, 127738380, 127738894, 127740693, 127739408, 127738637, 127740179, 127740436, 127739922, 33554442, 33554441, 33554443, 33554438, 33554439, 33554440)),
    ((65, 111, 126, 127, 128, 142, 143, 144, 146, 190, 414), 13, (76748802, 79436033, 76421381, 76486916, 75831299, 79563776, 77535491, 76618245, 79564804, 109905688, 79564547, 127804430, 76618510, 77536014, 79564290, 127804687, 75700495, 127805201, 127806486, 75368982, 76484630, 127803916, 127805458, 75367954, 127806743, 75369239, 127805715, 76484887, 75368211, 127806229, 76483859, 110890265, 75368725, 76484373, 127804173, 127805972, 127804944, 33554439, 33554440, 33554443, 33554441, 33554442, 33554438)),
    ((142, 143, 145, 158, 415), 12, (75700227, 78518274, 76486661, 75503876, 79565569, 75569152, 78580993, 127870480, 76417552, 113055256, 75504389, 78516248, 110954777, 127869452, 127870223, 127869966, 127870737, 110955290, 108857371, 110957084, 127869709)),
    ((143, 145, 175, 191), 3, (112071192, 114169369, 114169626, 109972251, 78518043)),
    ((31, 190), 4, (104731672, 114301465, 78715161, 82646553)),
    ((), 0, ()),
    ((172, 188), 3, (112794905, 67835673, 111871512)),
    ((69,), 1, (100930328,)),
    ((48, 190), 3, (112400664, 82646808, 109777945)),
    ((23, 136, 231), 3, (102175256, 67636248, 109581337, 109579290)),
    ((86,), 1, (111874328,)),
    ((8, 171, 187), 4, (101324568, 78252824, 111806233, 109579802, 109580316, 112855323)),
    ((151, 170, 171, 185, 186, 187, 188, 217, 233, 248, 425), 4, (116988937, 112794392, 67835160, 128526868, 128527382, 128527125, 128527639, 128526611, 128526354, 33554440, 33554442, 33554439, 33554438, 33554443)),
    ((42, 46, 60, 66, 70, 74, 84, 134, 155, 168, 186, 187, 202, 251, 426), 10, (79304704, 79960067, 78186755, 79370244, 80222213, 79239169, 81205505, 78186498, 67767810, 112854552, 128590605, 67767553, 112795161, 76156185, 109712666, 128590348, 128591376, 128591633, 128593175, 128590862, 128592661, 128591119, 128592147, 128592918, 128591890, 128592404, 33554441, 33554443, 33554439, 33554440, 33554438, 33554442)),
    ((61, 65, 71, 73, 75, 139, 163, 167, 172, 173, 181, 186, 188, 189, 229, 235, 427), 12, (82188546, 69867521, 78125061, 79305219, 80353536, 78125313, 80353796, 79305730, 112986904, 101389337, 79366169, 128656655, 79303951, 128656912, 79304208, 128656141, 111744283, 128657426, 79303437, 109777436, 112003610, 128655884, 128658197, 128657683, 128657940, 128656398, 128658454, 128657169, 128658711, 33554439, 33554440, 33554441, 33554442, 33554443, 33554438)),
    ((46, 98, 106, 108, 116, 138, 140, 174, 187, 188, 189, 221, 236, 428), 12, (77797376, 78452739, 79501572, 78317313, 78452997, 78317570, 128722448, 81468176, 112985624, 112986393, 112986650, 128721677, 115150087, 79368973, 128721934, 128723733, 74189077, 114037531, 76285723, 128721420, 128722191, 128724247, 128723990, 128723219, 128723476, 128722962, 128722705, 33554438, 33554442, 33554443, 33554440, 33554441)),
    ((45, 101, 107, 111, 121, 131, 141, 145, 156, 171, 172, 175, 181, 188, 221, 237, 429), 8, (78977024, 81596163, 79435777, 79501314, 81596677, 79436288, 81596420, 79436548, 111872280, 111872793, 101389850, 79366682, 128787727, 79435023, 111875611, 128789526, 128786956, 128787470, 79434252, 128787984, 128788755, 128789783, 128788498, 128788241, 128787213, 128789012, 128789269, 33554440, 33554438, 33554441, 33554439, 33554442, 33554443)),
    ((96, 140, 142, 145, 159, 160, 175, 189, 190, 191, 206, 430), 10, (78714881, 79632389, 80613123, 78584066, 78977284, 80612866, 78584320, 80612352, 80613380, 113051417, 113120280, 128852749, 128852492, 114168326, 79629318, 128853006, 113184778, 128854034, 76416530, 128853520, 128854548, 111937562, 76417044, 128853263, 128853777, 128854805, 76417301, 128855062, 128855319, 128854291, 33554443, 33554439, 33554441, 33554440)),
    ((129, 131, 143, 159, 174, 190, 191, 431), 9, (78649345, 79630597, 79566852, 79630083, 79629826, 77601028, 78513664, 114233624, 79563544, 112003097, 79629569, 112002586, 114232603, 128918285, 128919313, 79566609, 128918799, 114102812, 128918542, 128918028, 128919056)),
    ((175, 191), 2, (114168600, 115217177)),
    ((161, 174), 2, (115151640, 113052185)),
    ((191,), 1, (115217944,)),
    ((165, 230), 2, (108597784, 113052441)),
    ((5,), 1, (100927000,)),
    ((173, 174, 190, 191), 5, (111876633, 81597977, 115149848, 116200730, 79497498, 112003867)),
    ((185, 187), 3, (101387544, 79300376, 68817688, 112855833)),
    ((224,), 1, (108729112,)),
    ((137, 201), 2, (109577752, 110629913)),
    ((163, 169, 170, 186, 187, 232), 6, (112597273, 68818713, 111740696, 67834137, 111740442, 112920859, 110694940, 110695198, 112921373)),
    ((58, 84, 86, 155, 168, 170, 171, 182, 188, 216, 218, 250, 442), 8, (101321752, 79239704, 111806746, 67769626, 110757913, 111806492, 111876891, 77205275, 111744030, 113972255, 77205022, 111744797, 77205789, 129640980, 78319124, 129641751, 129641237, 129641494, 129640723, 129640466, 33554438, 33554439, 33554442, 33554441, 33554440, 33554443)),
    ((100, 105, 106, 107, 115, 117, 122, 123, 138, 170, 171, 172, 173, 185, 188, 189, 219, 251, 443), 16, (80353284, 79042561, 78256128, 81401858, 79239429, 81271040, 78125827, 67833603, 101322776, 78187032, 129704460, 74057228, 68752920, 129705231, 129704974, 129706516, 109839898, 129707287, 78385431, 129705745, 108726809, 129704717, 129706002, 129705488, 129706259, 129707030, 129706773, 33554439, 33554440, 33554442, 33554441, 33554438, 33554443)),
    ((60, 112, 122, 124, 146, 158, 171, 172, 173, 189, 190, 444), 14, (77797637, 82516224, 78190595, 82516737, 78321922, 78453252, 79365889, 111937304, 129770510, 79306510, 113118489, 111937050, 81468697, 111938075, 129770767, 80548633, 111877148, 75238428, 129769996, 80417292, 129772823, 78450967, 75238167, 129771795, 78449939, 75237139, 129771024, 129771281, 129772052, 129772309, 129772566, 129770253, 129771538, 33554440, 33554438, 33554441, 33554443, 33554442, 33554439)),
    ((109, 139, 140, 141, 142, 157, 159, 172, 173, 174, 177, 179, 181, 220, 223, 445), 11, (78321669, 79567105, 78387200, 79431682, 78387459, 78387716, 112073240, 81595928, 111872537, 129835532, 79370764, 129837074, 76350994, 111940890, 77401882, 129835789, 78387981, 129836817, 129836046, 80483342, 129838102, 76352022, 129836560, 80483856, 129837845, 76351765, 129836303, 129837331, 129837588, 129838359, 33554439, 33554442, 33554441, 33554438, 33554443, 33554440)),
    ((128, 129, 142, 143, 146, 158, 159, 174, 175, 188, 189, 207, 222, 254, 446), 11, (77666564, 81661185, 78518529, 77928453, 81661442, 81660928, 112069144, 78977539, 81661699, 129901068, 81662213, 79632652, 78584844, 129902096, 112071706, 80549392, 129901839, 129902867, 77465363, 112985881, 129901582, 129903124, 77465620, 78581268, 129901325, 129902353, 129903638, 77466134, 78581782, 129902610, 77465106, 129903895, 129903381, 33554443, 33554441, 33554440, 33554438, 33554442, 33554439)),
    ((174, 175, 190, 447), 12, (80677888, 78583813, 78780420, 81663235, 78649601, 80678402, 129967889, 77601297, 78514961, 115152664, 78584577, 129967375, 78977816, 80614671, 129967118, 80614414, 129966861, 110954009, 129966604, 129967632)),
    ((206, 207, 222, 223), 3, (114165784, 82711576, 101521177, 116264730, 116265499, 80610843)),
    ((206, 208, 222, 223), 4, (114628888, 67965720, 114101017, 116330778, 116330011)),
    ((3, 223), 3, (100796952, 116266521, 80611865)),
    ((4, 206, 222), 3, (100861976, 114099993, 116200474)),
    ((170,), 1, (101322520,)),
    ((6, 222), 2, (100992536, 116200217)),
    ((215,), 1, (114034712,)),
    ((25,), 2, (114694424, 76090392)),
    ((9, 23, 170), 4, (114891032, 67768600, 68753176, 109582105, 109580570)),
    ((8, 25), 4, (114563352, 76091160, 112728345, 76090905, 110630682, 76091674)),
    ((171, 187, 221), 5, (114957080, 68818456, 101323289, 101324314, 78251545, 115084059, 78252570)),
    ((101, 122, 186, 188, 204, 218, 219, 220, 221, 235, 251, 459), 5, (101519128, 81529112, 102437382, 109778201, 130755863, 130755092, 130754835, 130755349, 130754578, 130755606, 33554443, 33554439, 33554442, 33554440, 33554441)),
    ((12, 100, 128, 132, 140, 144, 148, 156, 172, 189, 198, 205, 218, 221, 238, 460), 10, (81664002, 67899653, 81467393, 81532928, 81598468, 80943363, 82451203, 81467650, 82713088, 80415493, 67899396, 115083288, 115082777, 130819857, 101455370, 101455627, 130818829, 130819600, 130821399, 130819343, 130819086, 130820885, 130820628, 130820114, 130818572, 130821142, 130820371, 33554438, 33554441, 33554439, 33554440)),
    ((62, 133, 135, 141, 143, 145, 147, 157, 175, 188, 190, 193, 195, 207, 220, 221, 222, 225, 233, 461), 11, (81205250, 83630593, 80480772, 81402368, 67900675, 80481029, 117250840, 130884879, 67966232, 81532175, 130884365, 81531661, 107812377, 130885136, 81532432, 130884108, 81531404, 130885907, 130884622, 130886164, 77400084, 130886678, 130886421, 130886935, 130885393, 130885650, 33554441, 33554438, 33554439, 33554443, 33554440, 33554442)),
    ((160, 174, 176, 191, 192, 194, 221, 222, 223, 238, 462), 10, (82710018, 79894785, 81598723, 82710532, 79763717, 80681472, 82709504, 82710789, 79698435, 115213848, 130950415, 81597711, 82709761, 130950158, 81730318, 115148313, 130949644, 81596940, 130950672, 115281416, 130951443, 78513939, 130951957, 78514453, 130951700, 78514196, 130951186, 130952214, 130950929, 130952471, 130949901, 33554443, 33554442, 33554441, 33554439, 33554438)),
    ((175, 191, 206, 222, 223, 463), 11, (81727492, 79697922, 81664261, 81726464, 80812033, 81727235, 80878341, 81727749, 117315096, 115284505, 131015180, 83761420, 114099738, 67966489, 131015694, 79562766, 82776088, 81662990, 116329499, 131016465, 81663761, 131015951, 131015437, 131016208)),
    ((161, 223), 4, (113318680, 81659928, 116329753, 83759897, 115216410)),
    ((207,), 2, (116265752, 81726744)),
    ((19, 26, 207), 4, (101845016, 101844505, 108661786, 76091930, 116266779)),
    ((22, 204), 2, (102041880, 102438169)),
    ((21, 201), 2, (101976600, 110630169)),
    ((136, 193), 2, (102176280, 115148569)),
    ((9, 199), 3, (107551768, 76026648, 102237721)),
    ((170, 205), 3, (113645592, 67900440, 102306585)),
    ((24, 187, 218, 221), 5, (101387289, 68817433, 115083800, 109579546, 112855067)),
    ((41, 200), 2, (110693400, 111741721)),
    ((60, 187, 202, 205), 8, (114826008, 67833368, 113973529, 75239193, 114034202, 67899930, 68817944, 112855579)),
    ((172, 188, 204, 221, 237), 7, (116006168, 80414488, 113969177, 101518874, 68883224, 115148828, 112924187, 110954269)),
    ((140, 150, 202, 203, 204, 205, 216, 221, 222, 476), 6, (113968664, 102503432, 131869461, 131869975, 80548119, 113051161, 82645529, 131868947, 131869718, 131868690, 131869204, 33554439, 33554441, 33554438, 33554443, 33554442)),
    ((172, 173, 177, 181, 189, 191, 204, 206, 213, 219, 223, 253, 477), 17, (80418819, 83630084, 81729536, 80484354, 81528577, 81270788, 82647557, 80484608, 81467906, 67964161, 80354053, 131933455, 82583055, 113969688, 68883992, 114100505, 131933969, 78383889, 131933712, 131933198, 131935511, 80613655, 131934997, 78448917, 131934483, 80612627, 78448403, 131934226, 131935254, 131932684, 131932941, 131934740, 33554438, 33554443, 33554441, 33554442, 33554440, 33554439)),
    ((176, 178, 190, 191, 204, 206, 207, 208, 239, 254, 478), 15, (79763457, 82647042, 80549891, 80681220, 80615680, 79698181, 67965440, 81729797, 101453336, 114166553, 131998477, 80025869, 131998734, 79895054, 81730574, 131998220, 81533196, 132000533, 79563029, 80678677, 131998991, 131999505, 117314054, 117314568, 132000790, 80678934, 79563286, 132000276, 132000019, 79562515, 132001047, 131999248, 131999762, 33554442, 33554439, 33554441, 33554443)),
    ((206, 207, 209, 221, 222, 479), 12, (80746498, 82581763, 80680964, 80615424, 80746753, 79763973, 132064784, 79829264, 101518360, 132063756, 79698700, 80681728, 132064527, 82711823, 115149593, 132065041, 115149338, 132064013, 115151899, 113051676, 80611085, 132064270)),
    ((1, 17, 44, 239), 7, (112662552, 101716505, 74190104, 100668442, 101585947, 82910235, 116464924, 82707996, 68031004)),
    ((2, 29, 238, 255), 4, (100730904, 100731417, 105712666, 101649947, 114100252)),
    ((3, 5, 45), 3, (100797208, 100927257, 107745818)),
    ((2, 30), 2, (100731160, 100730393, 105714202)),
    ((5, 7, 23), 3, (102107160, 100928026, 101058073)),
    ((6, 22, 30, 92), 5, (102042393, 116072472, 72160024, 111875354, 100993307, 100993564)),
    ((10, 149, 171), 5, (112400408, 82517272, 74058776, 101323801, 101060890)),
    ((0, 8), 3, (111548952, 67569176, 101124633, 101254938)),
    ((42, 151), 3, (112794648, 76155928, 101191961)),
    ((88, 153, 238), 4, (101256728, 102242073, 67703065, 111743770, 114100763)),
    ((10, 11, 43, 204, 219), 5, (107614489, 116137240, 74061336, 117119771, 109711898, 107616028, 67899163, 101453085)),
    ((59, 91, 95, 109, 188, 229, 230, 252), 11, (117185560, 76222488, 117119513, 67834393, 110894364, 101389083, 76222748, 117053466, 78318618, 101254685, 113972510, 116196895, 102565664, 111875873)),
    ((42, 61, 109, 221, 223, 234, 238), 10, (117314841, 109711640, 117251100, 69014812, 116202523, 75239963, 107743002, 77401370, 101321245, 78385946, 111937822)),
    ((62, 126, 161, 165, 181, 195, 197, 220, 221, 222, 235, 236, 239, 253, 254, 255, 493), 7, (115022872, 67965976, 117185818, 107812633, 117251355, 67965210, 78452507, 107809820, 132983830, 132984087, 132983573, 132983059, 132982802, 132983316, 33554443, 33554442, 33554440, 33554438, 33554441, 33554439)),
    ((14, 76, 192, 194, 204, 206, 209, 210, 223, 224, 239, 252, 255, 494), 14, (83761157, 83630336, 83826690, 68030468, 82778372, 82582531, 83827201, 68030211, 83695872, 83827461, 68029697, 133047310, 81861646, 68029954, 133047824, 82385680, 109842200, 133046796, 117311001, 117379339, 101452826, 133048081, 133047053, 133048852, 101585671, 114034459, 133049109, 80611605, 133048595, 133049623, 133047567, 133049366, 133048338, 33554438, 33554442, 33554441, 33554440)),
    ((13, 193, 207, 208, 238, 254, 255, 495), 11, (81795842, 83824387, 69081349, 81796096, 83823873, 68032004, 82709253, 83824644, 101650712, 116197913, 83757848, 107680538, 101649435, 101650204, 116197149, 133112589, 81659661, 133113617, 83760913, 133113360, 81660689, 133112332, 133112846, 133113103)),
    ((1, 49, 254, 255), 5, (100668184, 101847833, 102634522, 101585179, 83757082)),
    ((1, 16, 18, 224, 255), 5, (101780248, 101650457, 100667930, 102566427, 117378588, 117378077)),
    ((4, 19, 255), 3, (101845785, 100861720, 101844762, 117312027)),
    ((20,), 1, (101910552, 101910809)),
    ((21, 26), 4, (116726297, 75107865, 101975578, 76092441, 101976856, 101976091)),
    ((6, 22, 244), 3, (102041624, 100993817, 102303770)),
    ((23, 25), 3, (102106904, 102238233, 109581594)),
    ((9, 22, 24), 3, (102173464, 108597529, 102041114)),
    ((26, 58, 137), 6, (101192216, 116989209, 75108121, 76092697, 110759962, 78190106)),
    ((24, 41, 59, 169, 248), 4, (109776409, 102172698, 110694168, 102172187, 102307100, 102304029)),
    ((235,), 1, (112857624,)),
    ((43, 75, 234, 235), 5, (111811097, 75173657, 111809048, 77270040, 113969435, 112920090)),
    ((92, 205, 221, 235, 237, 238), 7, (102503960, 116072217, 116267802, 68029465, 67900186, 110890523, 110761500, 102504221)),
    ((110, 205, 236, 237, 238, 255), 5, (102568473, 110957848, 102568986, 115149083, 116197660, 108858141)),
    ((207, 208, 222, 236, 238, 239, 240, 242, 255, 510), 7, (116398872, 82643736, 102634247, 102634761, 134097942, 81660438, 134097685, 82775829, 113116697, 102633990, 81662489, 134097171, 81660181, 134096914, 134097428, 134098199, 33554443, 33554440, 33554442)),
    ((127, 238, 239, 241, 511), 14, (82909444, 82778117, 82712832, 68095233, 82844162, 83756801, 81861378, 83757315, 134161679, 117250584, 82975492, 82778880, 134161165, 82708237, 68031759, 82642968, 110038553, 116333850, 82779139, 69014298, 134161936, 102569755, 82709008, 134162193, 134161422, 134160908)),
)

LEFT, RIGHT0, RIGHT1 = CHUNKS, 2 * CHUNKS, 3 * CHUNKS
SIZE = 384 // CHUNKS
MAX_SENDS = max(len(p[2]) for p in PLAN)
MAX_FROM = max(1, max(len(p[0]) for p in PLAN))
MESH = pl.DeviceIdType.MESH


def nt_dot(left, right):
    return lax.dot_general(left, right, (((1,), (1,)), ((), ())), preferred_element_type=jnp.float32)


def choose(index, low, high, leaf):
    if all(PLAN[i] == PLAN[low] for i in range(low, high)):
        leaf(PLAN[low])
        return
    middle = (low + high) // 2

    @pl.when(index < middle)
    def _():
        choose(index, low, middle, leaf)

    @pl.when(index >= middle)
    def _():
        choose(index, middle, high, leaf)


def kernel(upper_ref, mask_hbm, out_ref, buf, acc, mask_ref, table, origin, count, in_sem, send_sem, recv_sem):
    brow, column = lax.axis_index("brow"), lax.axis_index("bcol")
    row, half = brow // 2, brow % 2
    own = buf.at[pl.ds(0, 384)]
    load = pltpu.make_async_copy(upper_ref, own, in_sem.at[0])
    load.start()
    load_mask = pltpu.make_async_copy(mask_hbm, mask_ref, in_sem.at[1])
    load_mask.start()

    def leaf(plan):
        origins, targets, sends = plan
        count[0] = len(origins)
        count[1] = targets
        count[2] = len(sends)
        for i, v in enumerate(origins):
            origin[i] = v
        for i, v in enumerate(sends):
            table[i] = v

    choose(row * 16 + column, 0, 256, leaf)
    sends = count[2]
    barrier = pltpu.get_barrier_semaphore()

    @pl.loop(0, count[0])
    def _(i):
        v = origin[i]
        there = ((v >> 4) & 15) * 2 + (half ^ (v >> 8))
        pl.semaphore_signal(barrier, inc=1, device_id=(there, v & 15), device_id_type=MESH)

    load_mask.wait()
    load.wait()
    for i in range(3):
        for j in range(6):
            keep = mask_ref[i, j].astype(jnp.float32)
            at = (pl.ds(i * 128, 128), pl.ds(j * 128, 128))
            buf[at] = (buf[at].astype(jnp.float32) * keep).astype(jnp.bfloat16)

    @pl.when(count[1] > 0)
    def _():
        pl.semaphore_wait(barrier, count[1])

    def slot(index):
        return buf.at[pl.ds(pl.multiple_of(index * SIZE, SIZE), SIZE)]

    def copy(v, i):
        there = ((v >> 20) & 15) * 2 + (half ^ ((v >> 24) & 1))
        return pltpu.make_async_remote_copy(
            src_ref=slot(v & 255),
            dst_ref=slot((v >> 8) & 255),
            send_sem=send_sem.at[i],
            recv_sem=recv_sem.at[(v >> 8) & 255],
            device_id=(there, (v >> 16) & 15),
            device_id_type=MESH,
        )

    def arrived(index):
        pltpu.make_async_copy(slot(index), slot(index), recv_sem.at[index]).wait()

    @pl.loop(0, sends)
    def _(i):
        v = table[i]

        @pl.when((v & (1 << 25)) != 0)
        def _():
            arrived(v & 255)

        @pl.when((v & (1 << 26)) != 0)
        def _():
            copy(v, i).start()

    has0 = (row == 0) | ((column >= row) & (row + column >= 16))
    has1 = (column < 15) & ((row <= 1) | ((column + 1 >= row) & (row + column >= 16)))
    here = pl.ds(pl.multiple_of(half * 384, 128), 384)
    other = pl.ds(pl.multiple_of(384 - half * 384, 128), 384)

    def rows(index):
        return buf[pl.ds(pl.multiple_of(index * SIZE, SIZE), 384), :]

    @pl.when(has0)
    def _():
        @pl.loop(0, CHUNKS)
        def _(j):
            arrived(SIB + j)

        right = jnp.where(row + column == 0, 0, RIGHT0)
        acc[:, here] = nt_dot(rows(0), rows(right))
        acc[:, other] = nt_dot(rows(0), rows(SIB))

    @pl.when(has1)
    def _():
        @pl.loop(0, CHUNKS)
        def _(j):
            arrived(SIB + CHUNKS + j)

        left = jnp.where(column == 0, RIGHT1, LEFT)
        for columns, right in ((here, RIGHT1), (other, SIB + CHUNKS)):
            term = nt_dot(rows(left), rows(right))

            @pl.when(has0)
            def _():
                out_ref[:, columns] = (acc[:, columns] + term).astype(jnp.bfloat16)

            @pl.when(jnp.logical_not(has0))
            def _():
                out_ref[:, columns] = term.astype(jnp.bfloat16)

    @pl.when(has0 & jnp.logical_not(has1))
    def _():
        out_ref[...] = acc[...].astype(jnp.bfloat16)

    @pl.when(jnp.logical_not(has0 | has1))
    def _():
        out_ref[...] = jnp.zeros_like(out_ref)

    @pl.loop(0, sends)
    def _(i):
        v = table[i]

        @pl.when((v & (1 << 26)) != 0)
        def _():
            copy(v, i).wait_send()


def per_device(upper_store, block_mask):
    return pl.pallas_call(
        kernel,
        out_shape=jax.ShapeDtypeStruct((384, 768), jnp.bfloat16),
        in_specs=[pl.BlockSpec(memory_space=pl.ANY)] * 2,
        out_specs=pl.BlockSpec(memory_space=pltpu.VMEM),
        scratch_shapes=[
            pltpu.VMEM((SLOTS * SIZE, 768), jnp.bfloat16),
            pltpu.VMEM((384, 768), jnp.float32),
            pltpu.SMEM((3, 6), jnp.int32),
            pltpu.SMEM((MAX_SENDS,), jnp.int32),
            pltpu.SMEM((MAX_FROM,), jnp.int32),
            pltpu.SMEM((3,), jnp.int32),
            pltpu.SemaphoreType.DMA((2,)),
            pltpu.SemaphoreType.DMA((MAX_SENDS,)),
            pltpu.SemaphoreType.DMA((SLOTS,)),
        ],
        compiler_params=pltpu.CompilerParams(
            collective_id=0, has_side_effects=True, vmem_limit_bytes=60 * 2**20
        ),
        name="cannon_steps",
    )(upper_store, block_mask)


def solution(mesh):
    spec = P("brow", "bcol")
    return jax.shard_map(per_device, mesh=mesh, in_specs=(spec, spec), out_specs=spec, check_vma=False)
```

```python
import jax
import jax.numpy as jnp
from jax import lax
from jax.experimental import pallas as pl
from jax.experimental.pallas import tpu as pltpu
from jax.sharding import PartitionSpec as P

CHUNKS = 6
SLOTS = 45
SIB = 33
PLAN = (
    ((1, 14, 16, 31, 32, 192, 240, 256), 5, (83894528, 83894785, 83895042, 83895299, 83895556, 83895813, 102630936, 104799001, 117451799, 70127641, 117450514, 117451542, 117451285, 103682842, 117450771, 103683099, 117451028, 68028443)),
    ((2, 3, 13, 14, 15, 17, 18, 33, 225, 227, 257), 10, (79697921, 69212419, 117516307, 68163588, 67114757, 80812051, 82843906, 117515793, 68163345, 117516050, 68224530, 67113472, 117515279, 68162831, 117515536, 68163088, 117517078, 104665112, 117517335, 68225815, 101517849, 117515022, 68162574, 117516821, 117514508, 117516564, 117514765, 33554439, 33554443, 33554440, 33554441, 33554442, 33554438)),
    ((3, 12, 17, 18, 19, 32, 34, 35, 48, 53, 64, 194, 226, 258), 9, (117580301, 68227853, 69278723, 81860610, 117580558, 68294917, 67176193, 68228110, 81861124, 101845272, 81991936, 106371353, 72093721, 117580815, 68228367, 117582100, 117581072, 117582614, 117581586, 117581843, 117581329, 117580044, 117582871, 117582357, 33554438, 33554441, 33554440, 33554442, 33554443, 33554439)),
    ((5, 6, 18, 20, 21, 33, 35, 37, 39, 50, 53, 179, 227, 243, 259), 8, (79828996, 68294658, 67241472, 81926149, 67242243, 81926401, 101914648, 67180056, 117645837, 68293389, 117646608, 117645580, 100992537, 117646351, 68293132, 117648407, 117647122, 68293903, 117647379, 117646865, 117647636, 117648150, 117647893, 117646094, 33554442, 33554439, 33554441, 33554440, 33554438, 33554443)),
    ((5, 19, 20, 21, 34, 36, 64, 66, 68, 82, 84, 85, 164, 210, 228, 260), 8, (78845954, 68425985, 68491268, 81991683, 67442949, 83040256, 101976856, 101910553, 117711630, 101975578, 68359182, 117711116, 101910299, 117711887, 117713686, 117712401, 117713172, 117712658, 117712915, 117713943, 117712144, 117713429, 117711373, 33554441, 33554440, 33554438, 33554443, 33554439, 33554442)),
    ((3, 4, 20, 21, 22, 23, 37, 39, 65, 67, 69, 71, 83, 85, 229, 231, 244, 261), 8, (80877572, 69474560, 68425729, 67373315, 82057221, 67373058, 102041368, 117776909, 68424461, 117777423, 68424975, 102041882, 100862745, 117777937, 68425489, 117777166, 117777680, 117778965, 117778708, 117779479, 117776652, 117778451, 117778194, 117779222, 33554438, 33554441, 33554439, 33554442, 33554443, 33554440)),
    ((7, 12, 21, 22, 23, 38, 87, 102, 116, 130, 164, 230, 262), 11, (67311872, 83106308, 68491779, 117843216, 68490768, 68622849, 82123010, 117842959, 68490511, 82254085, 102106649, 103488792, 102107418, 72092952, 102107931, 73077528, 117843987, 117842188, 68489740, 117844758, 117843473, 117843730, 117844244, 117844501, 117845015, 117842445, 117842702, 33554441, 33554438, 33554440, 33554442, 33554439, 33554443)),
    ((9, 22, 23, 24, 25, 39, 41, 71, 99, 101, 103, 115, 118, 119, 135, 263), 8, (69605892, 82188544, 68556801, 67504387, 82188802, 68557061, 111548696, 75042328, 102172953, 117908752, 68556304, 117908238, 68555790, 117910551, 117907981, 68555533, 117908495, 117909523, 117910037, 117910294, 117909266, 117909009, 117909780, 117907724, 33554439, 33554440, 33554441, 33554443, 33554442, 33554438)),
    ((10, 24, 25, 40, 56, 57, 72, 104, 120, 132, 136, 137, 152, 228, 264), 13, (68622593, 68687874, 83106051, 69475072, 68753667, 68688645, 83367941, 69671684, 105520152, 67700760, 78125828, 69802240, 75043864, 117973774, 68621326, 102237977, 117974288, 68621840, 102239002, 117974031, 68621583, 117974802, 117973517, 117975316, 117975573, 117975059, 117976087, 117974545, 117975830, 117973260, 33554441, 33554440, 33554438, 33554443, 33554442, 33554439)),
    ((8, 11, 24, 26, 27, 41, 43, 57, 73, 105, 135, 137, 153, 199, 233, 265), 13, (82057473, 67573762, 68753411, 71833600, 68688130, 81205253, 69737477, 83368452, 70785284, 83433728, 70851844, 102173208, 118040081, 68687633, 118039310, 68686862, 102304537, 118041366, 118039567, 118039053, 118040595, 118041623, 118039824, 118041109, 118040852, 118038796, 118040338, 33554439, 33554442, 33554440, 33554443, 33554441, 33554438)),
    ((12, 26, 27, 29, 42, 90, 166, 168, 170, 186, 200, 202, 217, 234, 236, 251, 266), 15, (82188288, 69736451, 67639298, 68818945, 68884484, 82450693, 69475332, 67836421, 68885251, 74059009, 67836672, 102369560, 103488281, 102303514, 102368795, 70983193, 72093465, 118104589, 118106902, 118104332, 68751884, 118105617, 101452572, 118104846, 118106131, 118106388, 118105360, 118105103, 118105874, 118106645, 118107159, 33554438, 33554441, 33554443, 33554439, 33554442, 33554440)),
    ((10, 13, 27, 28, 29, 43, 167, 169, 171, 186, 187, 201, 203, 216, 235, 267), 12, (69605634, 68622339, 82450436, 68884736, 69015813, 68819203, 70982145, 82450949, 107679001, 68814617, 82451201, 105716248, 68880920, 101255962, 104664092, 101254683, 118170382, 68817934, 118170896, 68818448, 118171410, 118170125, 68817677, 118170639, 118172438, 118171153, 118171924, 118172695, 118169868, 118172181, 118171667, 33554440, 33554438, 33554442, 33554443, 33554441, 33554439)),
    ((10, 13, 27, 28, 29, 44, 192, 202, 204, 206, 208, 220, 221, 268), 10, (67246340, 67508225, 70981888, 68950274, 69015552, 67770627, 72093186, 69016068, 68885509, 72093957, 102500376, 102500121, 118236689, 69016593, 118236432, 68883984, 105648903, 71109895, 118235404, 118236175, 68882956, 118235661, 118238231, 118236946, 118237717, 118237460, 118235918, 118237203, 118237974, 33554442, 33554441, 33554438, 33554443, 33554440)),
    ((1, 15, 28, 29, 30, 45, 195, 197, 205, 208, 219, 221, 225, 237, 239, 252, 269), 14, (68884995, 67180548, 71047938, 68950788, 69016325, 104208664, 67836928, 68879896, 69998592, 67897089, 78322200, 105713689, 68819737, 116333595, 102566170, 68880155, 118301197, 68948749, 118300940, 68948492, 118302482, 118303253, 118301454, 118303767, 118302225, 118301711, 118302996, 118302739, 118301968, 118303510, 33554440, 33554443, 33554442, 33554439, 33554441, 33554438)),
    ((0, 15, 30, 31, 46, 74, 192, 236, 238, 240, 241, 254, 255, 270), 11, (67115268, 71111939, 68099074, 82778113, 69146880, 67180804, 70126592, 68099333, 102631192, 70127877, 100669959, 69143815, 70126849, 118366990, 111808793, 118366733, 103683594, 69144586, 118367247, 103683337, 69144329, 118369303, 82709271, 118366476, 118367504, 118369046, 118368275, 118368789, 82708757, 118367761, 118368532, 118368018, 33554443, 33554440, 33554438)),
    ((14, 17, 29, 30, 225, 239, 255, 271), 14, (69212928, 68229125, 68028161, 83695621, 69144066, 103095322, 69011482, 68028932, 105713177, 68028675, 101517340, 100731931, 71179036, 69143552, 101518109, 100732184, 71111708, 118433040, 69080592, 118432012, 118432783, 69080335, 118432526, 118432269, 118433297)),
    ((1, 30, 48, 62, 224, 272), 5, (100668952, 104930585, 71176217, 106827034, 118500375, 104729627, 118499090, 118499861, 118500118, 118499347, 118499604)),
    ((1, 2, 15, 18, 19, 48, 49, 81, 209, 241, 273), 7, (70260993, 81795328, 67178757, 68098049, 67178243, 68098816, 67178500, 100734217, 67177986, 103683864, 118564883, 100733960, 118565140, 118564626, 67243026, 118565654, 118565911, 118565397, 33554438, 33554442, 33554443, 33554439)),
    ((2, 3, 19, 48, 50, 80, 210, 212, 242, 274), 7, (67179265, 69277957, 82909186, 67311620, 68225283, 67179008, 100796440, 100731673, 118630676, 67309076, 118630419, 118631190, 118630162, 118631447, 118630933, 33554438, 33554441, 33554440, 33554442, 33554439, 33554443)),
    ((3, 4, 20, 35, 49, 51, 113, 243, 275), 8, (81008642, 68290048, 67246083, 80877828, 82974721, 82974981, 101779992, 118696726, 67375126, 118695955, 118695698, 118696212, 118696469, 118696983, 33554443, 33554442, 33554440, 33554441, 33554438, 33554439)),
    ((4, 5, 21, 26, 28, 36, 52, 82, 212, 244, 276), 11, (83040515, 67377410, 68356869, 100927256, 100861721, 83040768, 67377921, 68356612, 105192218, 68623130, 73142554, 118762262, 111745307, 67440662, 118761234, 75107611, 118761491, 67439634, 118762005, 118762519, 118761748, 33554440, 33554443, 33554439, 33554438, 33554441, 33554442)),
    ((4, 5, 6, 27, 51, 117, 119, 213, 245, 277), 11, (81008899, 70522881, 67377157, 68421634, 100862488, 83106564, 67377664, 112465945, 74124313, 100993306, 118827798, 118827284, 67505684, 118827027, 118827541, 118828055, 118826770, 33554439, 33554442, 33554443, 33554441, 33554438, 33554440)),
    ((6, 7, 54, 118, 214, 230, 246, 278), 7, (70457604, 81074181, 67442689, 83171328, 67443203, 83171586, 101058328, 101059353, 118893591, 67571991, 118892306, 118893334, 67570706, 118892820, 118893077, 118892563, 33554438, 33554441, 33554440, 33554443, 33554442, 33554439)),
    ((6, 7, 8, 9, 11, 20, 55, 57, 151, 183, 247, 279), 10, (81139970, 67508480, 82189057, 67508739, 83237124, 112794905, 67569433, 67508997, 100992794, 106630936, 102435611, 118958099, 118958356, 118958870, 118957842, 118958613, 118959127, 33554441, 33554442, 33554443, 33554439, 33554440, 33554438)),
    ((8, 9, 26, 56, 57, 58, 88, 152, 214, 248, 280), 10, (70719493, 67574019, 83302401, 67704836, 70719744, 70851586, 115874072, 67569688, 101189657, 101124891, 113842714, 75108634, 67705114, 119024406, 67702806, 119024663, 119024149, 119023378, 119023635, 119023892, 33554439, 33554440, 33554443, 33554441, 33554438, 33554442)),
    ((8, 9, 10, 57, 59, 166, 181, 200, 217, 233, 249, 251, 281), 10, (81139715, 72882178, 67639553, 82253829, 73996801, 67639813, 82385412, 70785536, 108597016, 67635480, 101124377, 119090199, 119089428, 119089942, 119089685, 119089171, 119088914, 33554439, 33554442, 33554441, 33554440, 33554438, 33554443)),
    ((10, 11, 13, 28, 58, 186, 216, 246, 250, 282), 13, (68426497, 82384898, 70850820, 67770881, 68688389, 83499264, 75108099, 101254936, 70982659, 101320985, 106696730, 71965444, 102500891, 119154964, 119155735, 119154450, 119155478, 119155221, 119154707, 33554439, 33554441, 33554438, 33554440, 33554442, 33554443)),
    ((10, 11, 12, 13, 23, 28, 29, 219, 221, 249, 251, 283), 14, (68491520, 70588932, 83236866, 67836161, 68950020, 67770371, 69933315, 67771136, 70916613, 101255704, 106630169, 67765785, 101255451, 103553562, 67897626, 71110426, 101387036, 119220500, 67898900, 119220757, 119221014, 119220243, 119221271, 119219986, 33554440, 33554438, 33554442, 33554439, 33554443, 33554441)),
    ((12, 13, 26, 27, 29, 60, 62, 205, 214, 220, 250, 252, 284), 11, (68426245, 83105795, 67966976, 67835908, 73141762, 67967745, 68819460, 71178241, 68880386, 101386265, 103553307, 67897883, 106697222, 102369816, 101455130, 119286550, 67964950, 119285779, 119285522, 119286036, 119286807, 119286293, 33554440, 33554439, 33554443, 33554442, 33554441)),
    ((11, 12, 13, 15, 30, 31, 63, 236, 241, 247, 253, 255, 285), 14, (69933059, 67967236, 68098306, 67901442, 71047429, 68945408, 67901697, 72158465, 101385752, 106631449, 101386778, 103422747, 67771419, 71110939, 119351315, 102438684, 119352086, 119351829, 119352343, 119351572, 119351058, 33554442, 33554443, 33554440, 33554441, 33554439, 33554438)),
    ((0, 14, 15, 31, 46, 47, 62, 239, 254, 286), 11, (69146629, 82122752, 68098562, 71175425, 67967491, 68163844, 71175939, 69011972, 68164352, 71175682, 104731656, 71176453, 101586712, 103746823, 71176967, 119417879, 68096279, 119417622, 83757590, 119417108, 119417365, 119416851, 119416594, 33554438, 33554443, 33554441, 33554442)),
    ((14, 15, 30, 253, 287), 10, (70192128, 68032513, 69076994, 67115008, 70129923, 71177989, 70193156, 111351832, 69012248, 104665625, 119481102, 67115790, 119480588, 119480845, 119481616, 119481873, 119481359)),
    ((1, 15, 34, 35, 44, 46, 61), 6, (100798232, 100668697, 108863002, 103682587, 74190362, 100799772, 107746333, 105779998)),
    ((2, 18, 51, 52), 4, (103815960, 67309592, 103947291, 100734745, 67309851, 100865562, 100731164)),
    ((35, 68), 6, (72423429, 69212163, 67243265, 70326272, 67243522, 70260740, 100929048, 100799001, 100800282)),
    ((51, 62, 63, 64), 9, (100863256, 100863769, 71309569, 69213187, 70589188, 69343488, 69343749, 67245058, 105844762, 101913883, 107812124)),
    ((5, 8, 10, 44, 62, 85, 113), 7, (101979672, 100927001, 108730138, 109579291, 107614236, 104663326, 75044380, 100928797)),
    ((15, 43, 52, 85), 4, (100995353, 100865050, 100865304, 108728603, 105714716)),
    ((7, 11, 103, 119), 4, (101061400, 106371865, 101059098, 69868569, 101059867, 74060825)),
    ((8, 52, 59, 60, 86), 4, (100864536, 109776921, 109775900, 101124635, 100996637, 109778458)),
    ((9, 10, 41, 42, 136), 5, (107613976, 101191449, 104274715, 101190938, 109711646, 76155931, 101190428, 110694175, 101190685)),
    ((8, 57, 59, 120, 138), 11, (70326789, 79239426, 72554753, 75044864, 101127960, 70720004, 69738243, 101123609, 108666138, 76221978, 109647388, 101258523)),
    ((29, 38, 43, 60, 186), 8, (82581508, 76156418, 69737216, 78256129, 69737989, 82319363, 109712920, 108793881, 101323290, 105649947, 101320732)),
    ((6, 10, 27, 29, 139, 154), 10, (69867524, 75173378, 79305217, 69540613, 73079043, 104733208, 75172864, 101258778, 72159000, 107679513, 101386523, 101258268, 101386013)),
    ((13, 27, 28, 60, 61), 9, (81795073, 69474821, 71047171, 70981632, 71964676, 69212674, 101451288, 72094232, 103681819, 105649689, 101451804, 105649434)),
    ((46, 61, 62, 124), 12, (71112962, 81926656, 70392323, 74062337, 70982403, 71113216, 73144325, 73207812, 104537880, 74258200, 104799514, 74256922, 113973017, 105714459, 101517596, 101516829)),
    ((0, 14, 17, 31, 32, 44, 47, 60, 62, 63, 78, 302), 11, (71243781, 72224772, 71112705, 70326531, 72223744, 72224258, 104728088, 72224001, 104729114, 120463628, 70065420, 102768135, 120464913, 71244817, 102631705, 70192921, 120463885, 71111437, 71177497, 104728347, 105780746, 120466455, 68029207, 120465170, 105779718, 71240710, 68027922, 120466198, 120464656, 120465941, 120465427, 120464399, 120465684, 120464142, 33554443, 33554440, 33554441)),
    ((30, 31, 46, 62, 63, 143, 303), 11, (70125313, 71047680, 73275906, 71178500, 71241475, 120529164, 71048204, 71241989, 105843992, 70327298, 71241732, 71240961, 120530192, 69077520, 71177744, 105714969, 114103834, 120530449, 120529935, 120529421, 120529678)),
    ((17, 33, 34, 61, 62), 6, (101783064, 67244056, 101848603, 101716761, 108794394, 106828060)),
    ((34, 41, 46, 47, 82), 6, (101782040, 104864537, 73209113, 110694682, 101914395, 104795676)),
    ((33, 45, 52, 60, 63), 6, (100864792, 106829593, 107289115, 101848860, 75238939, 107746586)),
    ((22, 68, 85), 6, (72357890, 69277700, 70588416, 69408769, 69278469, 69409027, 101914136, 102042137, 101913114)),
    ((21, 67), 6, (69278212, 70588677, 69670912, 69539843, 70391809, 69540354, 101975832, 101979161)),
    ((27, 35, 51, 52, 62), 4, (100863000, 100865817, 107679770, 100800027, 104663068)),
    ((13, 101), 2, (102110488, 106695705)),
    ((24, 40, 41), 2, (102173464, 110694426, 102172185, 110694939)),
    ((9, 25, 58), 6, (110759448, 105454107, 101190169, 77204507, 102237722, 76090394, 77074970)),
    ((9, 24, 26, 107, 137, 153), 8, (101192984, 103357465, 68749849, 102172700, 102240794, 108597277, 112921883, 67701786)),
    ((27, 61, 74, 153), 11, (72751361, 81271043, 70785026, 83368708, 70785792, 79305477, 108795417, 111808539, 102241560, 107680026, 68815642, 75110170)),
    ((10, 11, 12, 26, 44, 45, 62), 10, (83433473, 71965187, 69671172, 69671936, 108728856, 82516485, 69802498, 106631705, 106762011, 102304028, 106630426, 104662813, 106632478, 104663839)),
    ((13, 29, 44, 47), 15, (70392578, 69671428, 75238657, 107745048, 69867780, 79436547, 73014277, 79436800, 103679514, 105649179, 69999643, 102501145, 71110171, 104731164, 72159513, 73144089)),
    ((1, 11, 12, 14, 15, 27, 29, 31, 36, 45, 46, 53, 59, 60, 63, 108, 317), 11, (70261248, 82647041, 70916356, 72161538, 102767897, 74256131, 121448981, 69999381, 70065173, 74256645, 106761242, 106763032, 73207321, 121448210, 121447953, 121446668, 121447439, 113972507, 121447696, 121447182, 121448724, 121449238, 121448467, 121449495, 121446925, 33554442, 33554439, 33554441, 33554440, 33554443, 33554438)),
    ((15, 16, 28, 30, 31, 43, 46, 47, 60, 94, 318), 17, (68164097, 70064133, 73273348, 71244036, 69475843, 70064640, 121512461, 71244301, 73272834, 70064909, 70589442, 80550401, 70982913, 121512975, 70195471, 103680537, 73273091, 69409795, 106695960, 121512718, 121515031, 69077783, 73272320, 70193431, 70261765, 121513489, 105843718, 121514260, 73273862, 102500634, 70192660, 73143578, 121513232, 103681563, 121514774, 121512204, 121514517, 121513746, 121514003, 33554442, 33554440, 33554439, 33554443, 33554441)),
    ((0, 45, 46, 47, 49, 62, 319), 10, (70392069, 70129664, 72226818, 69409284, 70130180, 70195201, 72290051, 106764056, 70130433, 121578511, 72226063, 104663577, 121579025, 72226577, 70126353, 121578768, 102565658, 121577997, 104666651, 104666908, 104662557, 121578254, 121577740)),
    ((35, 49, 68, 79, 95), 4, (102963992, 67374872, 100799257, 105776666, 105778971, 105777180)),
    ((16, 77, 78, 86, 93, 94), 6, (108859416, 106306329, 76353049, 100996890, 106759707, 109909276, 105715229)),
    ((69, 74, 93), 3, (100930072, 111808281, 109843738)),
    ((77, 85, 93), 5, (104077592, 67440152, 109451545, 75304217, 109907994)),
    ((69,), 7, (74520577, 71309315, 69343234, 72685568, 72489221, 70457348, 100931096, 100930585, 100931354)),
    ((20, 78, 85, 86), 7, (100994840, 71440384, 77863171, 71571460, 72620033, 71571714, 71571973, 105711129, 100995866, 107681563)),
    ((74,), 1, (111807512, 111807769, 111808026)),
    ((81, 86, 119), 3, (101125656, 100996377, 105711386)),
    ((9, 77), 3, (101189144, 76026392, 105646617)),
    ((56, 92, 153), 5, (106043928, 72948760, 78320152, 101256985, 111743514)),
    ((8, 26, 44, 59, 123), 9, (71440643, 68032773, 71702528, 70916868, 106633752, 74190872, 71702785, 108661529, 71703042, 110761242, 108662811, 107613724)),
    ((76, 91, 140), 7, (73013507, 72947972, 73078789, 77270273, 83565056, 77270530, 111873817, 109775128, 106632218, 106632987)),
    ((2, 6, 10, 12, 42, 44, 60, 72, 77, 90, 91, 93, 125, 140, 332), 11, (83564803, 74324225, 83696133, 75176192, 76287490, 122430222, 72030734, 106694937, 77337881, 76288004, 122430993, 72030993, 108792600, 108859659, 106695194, 77338138, 76289803, 122431764, 122430736, 122431250, 122431507, 122429965, 122432278, 122430479, 122429708, 122432021, 122432535, 33554438, 33554441, 33554442, 33554439, 33554440)),
    ((11, 13, 15, 29, 37, 43, 45, 47, 60, 61, 65, 69, 71, 92, 93, 94, 95, 125, 163, 229, 333), 12, (71506177, 72751106, 73209859, 71374852, 71833860, 73210624, 73014017, 72092421, 106629144, 107810329, 122495501, 73143053, 122496272, 73143824, 107681306, 122495758, 73143310, 122496015, 107812379, 107811868, 122496529, 122497043, 122496786, 122497557, 122497814, 122497300, 122495244, 122498071, 33554443, 33554442, 33554440, 33554438, 33554441, 33554439)),
    ((32, 46, 63, 64, 79, 93, 94, 95, 110, 334), 10, (72423681, 73340931, 74322181, 73275397, 73210116, 71637248, 73341186, 74320896, 73276163, 74321924, 122561808, 73341456, 104930329, 73206041, 75370265, 106828824, 74321410, 122560780, 73341708, 106760218, 106825499, 122561294, 73208846, 122561037, 107878155, 122562836, 70125588, 122563093, 107876870, 70125845, 122563607, 122562065, 122561551, 122563350, 122562322, 122562579, 33554442, 33554441, 33554440, 33554439)),
    ((35, 47, 62, 63, 94, 95, 335), 8, (73338370, 75372803, 73275652, 73338113, 71309824, 116333336, 75370008, 72223493, 106826009, 74387225, 73338627, 122627087, 73274639, 73339141, 107941146, 73338884, 73337856, 122626573, 73274125, 122627344, 73274896, 122626316, 122626830, 122627601)),
    ((51, 92, 94, 95), 6, (101848088, 107026713, 72948249, 75369753, 108926746, 73272090, 110890267)),
    ((34, 78), 5, (115481368, 110959385, 71768601, 68228888, 74321177)),
    ((68, 73, 85), 4, (101978648, 103881497, 67375385, 110890010)),
    ((41, 86, 108), 3, (112924440, 110693657, 100995610)),
    ((69, 92), 3, (100930328, 113973529, 77336089)),
    ((68,), 8, (72488960, 69474308, 71636995, 71505922, 69540101, 67439873, 104012312, 67374104)),
    ((58, 65, 77, 91), 11, (71375365, 82123266, 71768323, 72555008, 69672196, 109843480, 71637505, 112857626, 111614489, 77204761, 106694683)),
    ((2, 38, 93, 103), 3, (101061144, 106632729, 106630683, 111874842)),
    ((25, 91), 3, (110629912, 68683800, 112858137)),
    ((73, 75, 80, 90, 122), 5, (110825497, 108594712, 106628636, 110825243, 108725789, 106759962)),
    ((60, 75, 77, 123, 171), 7, (106502937, 78255385, 101323544, 108794140, 76224284, 105645851, 108660762)),
    ((6, 23, 27, 29, 43, 59, 74, 75, 77, 87, 89, 92, 93, 106, 347), 12, (72751616, 83695877, 72030467, 76225028, 72882434, 82516225, 110825752, 108728089, 108729882, 123412748, 74060300, 123414290, 72092690, 123414033, 123413519, 74061071, 106761499, 123413005, 123414547, 123414804, 123415061, 123415318, 123415575, 123413776, 123413262, 33554442, 33554441, 33554440, 33554443, 33554439, 33554438)),
    ((20, 26, 28, 45, 54, 60, 62, 76, 77, 86, 93, 109, 156, 244, 348), 13, (71899136, 72620290, 73210369, 83630083, 75372549, 72161282, 73075204, 72358657, 73210885, 123478798, 77336580, 74126350, 73074947, 110892811, 106896408, 74192664, 123479312, 123479569, 123480083, 123479826, 72158226, 123478541, 123479055, 123480854, 123481111, 123478284, 123480597, 123480340, 33554441, 33554439, 33554442, 33554440, 33554438)),
    ((45, 49, 59, 61, 63, 65, 77, 78, 89, 91, 92, 94, 95, 109, 349), 15, (71375106, 82582016, 72096003, 73140997, 74258689, 71506436, 104995352, 105712153, 116267803, 72091163, 106371610, 72096260, 75303963, 72091928, 75306521, 123544848, 106629916, 74192400, 123546647, 72225047, 73074458, 75304728, 108860445, 123543820, 123545876, 123546133, 123544591, 123545619, 123546390, 123544334, 123545362, 123544077, 123545105, 33554443, 33554441, 33554440, 33554438, 33554442, 33554439)),
    ((16, 47, 48, 50, 62, 78, 79, 80, 126, 350), 10, (72358145, 72227075, 72292354, 75370500, 73206533, 72227330, 75370757, 75369472, 105712408, 71375616, 107877913, 72223257, 123610384, 72162064, 107876123, 105780250, 123609870, 72162318, 123610127, 123611412, 71174164, 123609356, 108926217, 72289812, 123612183, 71174935, 123611669, 108925703, 72290583, 71174421, 123609613, 123610898, 123611155, 123610641, 123611926, 33554443, 33554438, 33554442, 33554440)),
    ((78, 79, 92, 351), 12, (72358405, 74323972, 72292611, 72227585, 74386946, 108860696, 75371008, 72292865, 123675406, 83827470, 106765593, 71310350, 123675149, 72157209, 74322701, 74386432, 123675663, 106763802, 123676177, 106762779, 123675920, 123674892, 106762524)),
    ((110, 111, 127), 2, (108075544, 76420888, 109972761, 109974810, 109973019)),
    ((80, 126), 2, (112006936, 109908761)),
    ((111,), 1, (109974296,)),
    ((115, 117, 120, 126), 3, (101127448, 112006425, 107808282, 112005659)),
    ((108,), 2, (111938840, 79368984)),
    ((50, 119, 124), 4, (104208408, 67571480, 113972761, 109777946)),
    ((103,), 5, (74717184, 77862917, 74913793, 67506180, 74782722, 67505923, 101062168, 101061657)),
    ((120,), 6, (75634693, 74717443, 69605377, 73799684, 72816640, 73799938, 101127192)),
    ((123, 136), 3, (108660504, 101191962, 108660249, 109712411)),
    ((25, 108, 122, 138, 154, 230), 5, (108595481, 109645082, 101259036, 77138716, 108595995, 109644312, 107677470, 108597789)),
    ((10, 36, 38, 40, 45, 74, 91, 108, 120, 122, 123, 155, 187, 230, 234, 362), 9, (108661272, 111938587, 124396045, 75043597, 106634010, 74191642, 108730908, 78385436, 124396559, 75044111, 110757401, 124397073, 75044625, 112922377, 124398358, 73076758, 124395788, 124398615, 124396816, 124397330, 124397587, 124396302, 124397844, 124398101, 33554440, 33554439, 33554438, 33554443, 33554442)),
    ((11, 21, 43, 53, 58, 69, 77, 92, 105, 109, 122, 123, 124, 125, 135, 157, 171, 229, 239, 363), 12, (74782981, 79367168, 75175938, 70851329, 74783492, 75110659, 74979845, 75111169, 108595225, 75111428, 112989464, 75237656, 78450456, 124461581, 124463380, 75109133, 124462352, 108726810, 75109904, 124461324, 124462095, 75109647, 107809051, 124462609, 124463894, 124464151, 124461838, 124462866, 124463637, 124463123, 33554440, 33554438, 33554441, 33554439, 33554443, 33554442)),
    ((32, 50, 60, 74, 92, 93, 106, 123, 124, 125, 140, 156, 157, 224, 226, 364), 13, (72554501, 76159492, 73668609, 74062592, 75241730, 82713091, 78384642, 74783747, 74062853, 75242243, 108791832, 74258944, 73997825, 104667929, 75172121, 124527888, 124527631, 75175183, 124528659, 124529687, 124527117, 124529430, 124527374, 124526860, 124528402, 124529173, 124528145, 124528916, 33554439, 33554443, 33554440, 33554441, 33554438, 33554442)),
    ((35, 45, 61, 77, 93, 99, 107, 108, 111, 124, 125, 126, 127, 157, 205, 237, 365), 13, (83630337, 75307008, 77401602, 75241985, 82582788, 75307781, 77339139, 75308036, 112004120, 77401859, 75236888, 109907225, 73139993, 107677210, 124593167, 75240719, 106760731, 76355099, 124593681, 75241233, 109777693, 124592910, 75240462, 124592653, 109909788, 124595223, 75240205, 124593938, 124594195, 124594709, 124593424, 124594966, 124594452, 124592396, 33554440, 33554442, 33554439, 33554443, 33554441, 33554438)),
    ((76, 78, 81, 94, 95, 111, 126, 127, 142, 255, 366), 11, (74651904, 77403395, 75438085, 75307522, 74390020, 76419076, 75438337, 124659217, 75438865, 76419333, 124657932, 108857626, 75439116, 108926488, 73406721, 76418819, 124658960, 73407234, 109841689, 124658446, 108989446, 76419590, 124660245, 72222997, 124660502, 124659731, 72222483, 124660759, 124658703, 109975050, 124658189, 124659988, 124659474, 33554441, 33554443, 33554440, 33554439)),
    ((79, 95, 110, 126, 127, 367), 11, (73406469, 75435779, 73537537, 75435522, 75436036, 111023896, 108075289, 74319360, 110038555, 75368475, 75435265, 124723982, 78451481, 75371534, 107809306, 77466905, 76484888, 124724239, 124723468, 124723725, 124724496, 124724753)),
    ((125,), 2, (112989976, 112989721, 112988442, 75237913)),
    ((68, 96, 111), 4, (103030040, 68358936, 108990746, 108857113)),
    ((125,), 3, (109517336, 75237144, 79434520)),
    ((110, 120), 4, (101126936, 107158041, 75045145, 76418073)),
    ((102, 103, 117, 124), 3, (101059608, 101061913, 112987930, 111021083)),
    ((102, 107, 108, 126), 5, (102044696, 112922905, 107158298, 74717978, 112922651, 112923932, 75302426)),
    ((119, 120), 2, (102111000, 102109721, 101127706)),
    ((102, 120), 7, (73734147, 74848261, 75962369, 71768066, 74848512, 67571716, 103160600, 68490008, 101126681)),
    ((107, 137), 8, (74651649, 69801989, 73603075, 74914048, 74848772, 73865218, 101192472, 101193241, 107612954)),
    ((7, 8, 25, 36, 41, 57, 89, 105, 106, 107, 115, 122, 151, 215, 249, 377), 4, (110693400, 125379599, 76027151, 125379342, 125380884, 110957081, 125380627, 125378828, 125380113, 125381141, 125381398, 125379856, 125379085, 125380370, 125381655, 33554442, 33554441, 33554439, 33554440, 33554438, 33554443)),
    ((20, 24, 26, 41, 58, 74, 90, 104, 106, 107, 123, 124, 180, 246, 250, 378), 10, (72947712, 73996547, 74127618, 73997061, 113711384, 75041284, 72949016, 107612441, 125445135, 76225551, 75040513, 107682330, 107611931, 79433754, 79432728, 107612700, 125446420, 125444364, 74124820, 110760989, 125445649, 125445392, 125446163, 125444621, 125447191, 125446934, 125445906, 125444878, 125446677, 33554441, 33554442, 33554443, 33554439, 33554438, 33554440)),
    ((36, 37, 43, 59, 76, 89, 91, 106, 107, 108, 125, 138, 157, 185, 186, 379), 11, (71964933, 73930753, 74061828, 75106563, 73013762, 73931008, 107612184, 79367704, 125510414, 73931534, 110826009, 125511442, 74189842, 125509900, 76157452, 125512727, 74191127, 125510671, 76158223, 107678490, 125511185, 76158737, 125512470, 125512213, 125510157, 125511956, 125511699, 125510928, 33554443, 33554441, 33554439, 33554440, 33554442, 33554438)),
    ((42, 48, 50, 58, 60, 76, 90, 107, 108, 109, 112, 114, 141, 188, 380), 15, (75307269, 77207809, 75110400, 70064389, 73734404, 74193155, 79433218, 75110916, 74717699, 75308289, 116138008, 76286488, 77405186, 125575693, 74259725, 107743002, 107677721, 107677979, 112004616, 79434760, 125578006, 74256406, 125576721, 125576978, 74255378, 125577749, 125576207, 125576464, 125575950, 125578263, 125575436, 125577492, 125577235, 33554438, 33554441, 33554443, 33554439, 33554442)),
    ((32, 65, 67, 76, 93, 95, 109, 110, 113, 117, 124, 127, 140, 147, 157, 173, 381), 11, (74586113, 74192898, 74258432, 74127363, 72095749, 74455045, 74455300, 109845272, 108010009, 75172633, 110956827, 74189595, 107808794, 77403162, 77401112, 125643285, 72157461, 108726045, 110956572, 125640972, 125642000, 76289552, 125643542, 108729374, 125641229, 110957343, 74189340, 125642257, 125641743, 125643799, 125643028, 125642771, 125642514, 125641486, 33554441, 33554442, 33554438, 33554439, 33554440, 33554443)),
    ((78, 79, 80, 92, 94, 95, 110, 111, 142, 158, 382), 14, (74783232, 77467138, 74389761, 83761156, 74324483, 73472005, 77467395, 75438596, 125707536, 74259216, 77467909, 109779736, 107877657, 125707793, 74259473, 77336856, 125706508, 73603331, 76354060, 125708050, 73270802, 125707279, 125706765, 125707022, 125709078, 73271830, 74387478, 125709335, 74387735, 125708564, 73271316, 125708821, 125708307, 33554440, 33554438, 33554441, 33554442, 33554443, 33554439)),
    ((110, 111, 113, 126, 383), 10, (82712833, 74389509, 76421124, 74390274, 76421376, 76421891, 125772815, 73406991, 110958360, 74320143, 76484355, 125772558, 108863257, 76420110, 125773072, 74254105, 74320400, 108857882, 125772301, 108861211, 108859932, 125772044, 125773329)),
    ((129, 140, 141, 143), 3, (110172696, 78517528, 114036505, 114035994, 112069915)),
    ((142, 158, 159), 5, (112135193, 110434330, 80549658, 109905688, 75504408)),
    ((103, 143), 2, (101062424, 112072473)),
    ((157,), 2, (115085848, 80546840)),
    ((137, 140), 3, (101193496, 76024600, 114036761)),
    ((156, 158), 2, (114103065, 110823960)),
    ((67, 137, 154, 215), 3, (109578008, 113971994, 109843225, 109582107)),
    ((114, 119, 137, 138), 4, (101125400, 101257753, 112004378, 107678235)),
    ((36, 72, 121, 132, 134, 139, 151, 152, 153, 166, 168, 184, 185, 228, 232, 244, 248, 392), 8, (69736707, 67636738, 77010945, 69736961, 67637252, 69737728, 79108096, 73931269, 79108357, 110626584, 109709337, 110626842, 126363410, 126362896, 126363153, 126361868, 126363667, 126364181, 126364438, 126363924, 126362639, 126362382, 126362125, 126364695, 33554440, 33554441, 33554443, 33554438, 33554439, 33554442)),
    ((41, 56, 105, 138, 139, 151, 152, 154, 155, 169, 201, 231, 233, 393), 13, (75765765, 70850563, 77076482, 78125059, 75896833, 74979329, 79173888, 77011460, 74979588, 67637760, 109517080, 77137432, 101258009, 77137689, 126429460, 126427661, 77075213, 126428432, 77075984, 126428689, 126427918, 126428946, 126429974, 126427404, 126429717, 126430231, 126428175, 126429203, 33554441, 33554438, 33554439, 33554440, 33554443, 33554442)),
    ((40, 42, 104, 108, 123, 136, 139, 154, 155, 170, 186, 232, 236, 394), 13, (77011202, 73996292, 77273088, 76089603, 77273857, 77274117, 103357208, 77138200, 110758169, 126493454, 77141006, 110758683, 111939610, 75963162, 110757916, 79369754, 126495510, 75173910, 126493968, 111809309, 126494225, 77141777, 126493197, 126492940, 126494482, 126494739, 126493711, 126495253, 126495767, 126494996, 33554441, 33554442, 33554439, 33554440, 33554443, 33554438)),
    ((39, 41, 75, 90, 91, 101, 109, 122, 126, 140, 141, 154, 155, 157, 171, 173, 188, 235, 249, 395), 10, (76028162, 77207556, 76155139, 77208069, 77208320, 103488536, 77137944, 114102041, 77334809, 76154625, 111874074, 126558733, 77206285, 126559504, 109647132, 111875867, 77207056, 126558476, 77206028, 126560018, 126561046, 126559761, 126560275, 126561303, 126558990, 126559247, 126560532, 126560789, 33554443, 33554439, 33554442, 33554440, 33554441, 33554438)),
    ((66, 76, 86, 110, 124, 125, 134, 141, 142, 155, 156, 157, 170, 172, 236, 238, 253, 396), 18, (76355585, 76683266, 72030211, 77273602, 80482565, 77338880, 75766020, 76356100, 75503875, 76221189, 113055000, 110889753, 110823194, 81532697, 78515992, 126624526, 77405454, 126625040, 77405712, 107742747, 78385691, 113053706, 126626068, 72091668, 126624269, 77271821, 75304468, 126625297, 126626839, 126626582, 126626325, 126624783, 126624012, 126625554, 126625811, 33554441, 33554440, 33554438, 33554443, 33554439)),
    ((65, 67, 97, 109, 126, 129, 140, 145, 156, 173, 189, 239, 397), 12, (75241476, 77273346, 79370240, 77404163, 77338624, 82582533, 78388225, 77404677, 109058584, 76220184, 79498497, 76286211, 110822937, 109775386, 126689805, 77337357, 113054471, 126691090, 113055499, 126690062, 77337614, 126692118, 126690576, 126691604, 126690319, 126692375, 126691861, 126690833, 126691347, 126689548, 33554441, 33554442, 33554438, 33554440)),
    ((96, 98, 110, 115, 127, 143, 144, 158, 159, 174, 398), 11, (75569153, 76290051, 78515200, 77535236, 76617733, 79632642, 78515714, 111023640, 126756112, 77536272, 110954778, 111022617, 75367961, 126756369, 108923163, 126755855, 77468955, 112072202, 126757911, 74320663, 112071174, 111086855, 126757140, 74319892, 78516999, 126756883, 126755084, 74319635, 126756626, 126755341, 126757397, 126757654, 126755598, 33554443, 33554440, 33554441)),
    ((111, 127, 158, 159, 399), 11, (75503619, 77532674, 77469701, 76552193, 77532160, 75634949, 76417540, 103750168, 77400600, 77533188, 113120025, 77533445, 113120538, 126821391, 78581017, 126821134, 77468686, 78581530, 126821905, 126821648, 126820620, 126820877)),
    ((143, 159), 2, (109971224, 111019545)),
    ((128, 142, 158), 5, (111155736, 76352280, 113056537, 80548889, 111087386)),
    ((140,), 1, (114036248,)),
    ((158,), 2, (112006168, 75302936)),
    ((157,), 2, (115086360, 80547352)),
    ((129,), 1, (110955288,)),
    ((153,), 1, (110627608,)),
    ((136, 137, 138, 228), 4, (102175512, 109643801, 109578778, 108596507)),
    ((56, 88, 136, 137, 150, 153, 168, 184, 214, 408), 5, (101192728, 76023832, 102241802, 102241031, 127412500, 76090900, 127412757, 76091157, 127412243, 127413271, 127413014, 127411986, 33554438, 33554443, 33554440, 33554441)),
    ((40, 49, 55, 83, 105, 121, 137, 138, 139, 154, 185, 187, 232, 249, 409), 11, (77072900, 82385154, 76027905, 70916099, 76945413, 77071872, 80156673, 70851072, 67703045, 76028418, 71899395, 78126083, 127478036, 127475980, 127477008, 127476494, 127476237, 127476751, 127477265, 127478293, 127477522, 127477779, 127478550, 127478807, 33554442, 33554441, 33554438, 33554440, 33554439, 33554443)),
    ((56, 74, 86, 106, 122, 124, 138, 139, 155, 156, 186, 216, 248, 410), 10, (76158979, 76093440, 76224514, 69933572, 76093697, 73997317, 77138436, 109709848, 109451801, 109710106, 79432985, 109708827, 127542030, 78189582, 127543829, 76222229, 127542287, 127542801, 127542544, 127543315, 127541516, 127544086, 127541773, 127543058, 127544343, 127543572, 33554439, 33554441, 33554442, 33554443, 33554440, 33554438)),
    ((75, 89, 91, 123, 133, 138, 140, 141, 156, 157, 159, 187, 251, 411), 10, (74062080, 76159235, 77203201, 76159749, 76160002, 109643288, 77203972, 109643547, 113908761, 76285977, 109644572, 127607309, 76160269, 109774874, 127607566, 78255118, 79498777, 127608337, 78255889, 127608080, 78255632, 127608594, 76286994, 127609365, 127607823, 127607052, 127609108, 127608851, 127609879, 127609622, 33554440, 33554439, 33554438, 33554443, 33554441, 33554442)),
    ((76, 80, 82, 84, 92, 109, 126, 139, 140, 141, 157, 158, 188, 220, 235, 236, 252, 412), 13, (75831300, 76290561, 76355840, 77535747, 77404421, 77268994, 112007961, 80481305, 107743514, 127673616, 109839896, 78454032, 78386458, 127673359, 127674901, 76353301, 127675415, 127673873, 76353815, 127674130, 73139730, 76352530, 110761755, 127675158, 127673102, 127674387, 127672845, 127672588, 127674644, 33554439, 33554443, 33554441, 33554438, 33554442, 33554440)),
    ((81, 109, 110, 121, 124, 125, 127, 140, 141, 142, 143, 149, 156, 159, 172, 189, 413), 18, (76814338, 80547073, 76224771, 76290309, 77334273, 75700224, 78453252, 77469952, 113053464, 127738638, 78518798, 74188814, 127740437, 113053978, 74128149, 110824217, 108726300, 127738895, 108860187, 127739409, 78386961, 127740951, 74255127, 127740180, 110826525, 127738124, 110827038, 127739152, 127739923, 127740694, 127738381, 127739666, 33554442, 33554441, 33554439, 33554438, 33554440, 33554443)),
    ((111, 116, 126, 142, 143, 144, 157, 159, 190, 238, 254, 414), 11, (75569669, 76486660, 77535489, 79563776, 76617986, 76421635, 79564547, 75831553, 79564290, 127804174, 76748814, 109972248, 77536000, 79564804, 127804431, 113121035, 79565061, 127804945, 110888473, 127806230, 75368982, 76484630, 127806487, 127805202, 75369239, 76483602, 127805459, 75368211, 76483859, 127804688, 127803917, 127805973, 127805716, 127803660, 33554438, 33554440, 33554439, 33554441, 33554442)),
    ((142, 143, 145, 156, 158, 415), 11, (75569408, 78518274, 77466373, 78581764, 76486913, 76487171, 127869710, 78517262, 76552448, 127869196, 112008216, 76416524, 112073497, 127870224, 78516248, 110823706, 127870481, 77399833, 110954011, 110958108, 127869967, 127869453)),
    ((145, 175), 3, (112269592, 80614680, 114169625, 112070938)),
    ((174,), 1, (116200216,)),
    ((165, 175), 2, (114168600, 78513944, 114167833)),
    ((31,), 1, (105715480,)),
    ((69, 102), 3, (114628888, 67506456, 100930841)),
    ((172, 174, 190), 6, (111286552, 78977560, 78449176, 116201242, 79108634, 111871513)),
    ((7, 170), 3, (101322520, 68752664, 109581337)),
    ((86, 186, 187), 3, (101387544, 79042584, 111740441, 111743770)),
    ((8, 137, 153, 171), 4, (109578520, 101323801, 78252057, 109580315, 101324058, 110627100, 78252314)),
    ((20, 73, 154, 167, 170, 185, 186, 188, 201, 217, 248, 425), 4, (101389848, 79366680, 109646617, 128527383, 128527126, 128526869, 128526612, 128526355, 128526098, 33554439, 33554441, 33554440, 33554442, 33554443, 33554438)),
    ((14, 42, 58, 66, 70, 90, 138, 155, 168, 171, 184, 186, 202, 251, 426), 12, (79239169, 79304960, 80222213, 77993987, 81336322, 79239682, 83565316, 79239940, 67767553, 78186755, 112925464, 76156184, 101324555, 109842201, 128590092, 128590863, 128592405, 128592148, 128591377, 128591120, 128591634, 128590349, 128592919, 128590606, 128592662, 128591891, 33554439, 33554438, 33554440, 33554442, 33554441)),
    ((13, 73, 75, 87, 139, 165, 172, 173, 186, 187, 188, 203, 235, 237, 253, 427), 11, (79304704, 79173637, 73013249, 80353284, 78251777, 78125314, 78125571, 101388312, 101389337, 79366169, 128657170, 128656656, 79304208, 107680282, 128656399, 79303951, 109778203, 128657941, 128655885, 128658455, 128656913, 128655628, 128657684, 128658198, 128656142, 128657427, 33554439, 33554443, 33554440, 33554442, 33554441, 33554438)),
    ((100, 106, 108, 138, 140, 141, 156, 157, 174, 188, 189, 204, 236, 238, 252, 428), 11, (77928704, 79436036, 79370498, 78452995, 78317313, 78318341, 112986392, 112920857, 112986650, 128721678, 112985627, 81468686, 114037532, 115149830, 76285724, 128721164, 79368716, 115150087, 128722192, 128722963, 77401363, 128721421, 128723477, 128721935, 128723734, 128722706, 128722449, 128723991, 128723220, 33554442, 33554443, 33554441, 33554440)),
    ((97, 99, 107, 109, 111, 124, 135, 147, 156, 157, 159, 165, 172, 175, 188, 221, 237, 429), 11, (81467394, 79435776, 79501316, 81596163, 79436289, 79501573, 112920344, 114102298, 79437338, 111872281, 128786700, 79434252, 115151880, 109774363, 113055260, 76352028, 128789527, 111875613, 75303703, 128788499, 128787214, 128787471, 128789013, 128787985, 128786957, 128788756, 128788242, 128789270, 128787728, 33554439, 33554442, 33554438, 33554441, 33554443)),
    ((128, 130, 140, 142, 157, 159, 160, 162, 190, 191, 206, 222, 430), 14, (77928452, 80613123, 78583810, 79632384, 78714881, 81730053, 78584321, 80612352, 128852236, 79499788, 111220761, 81661209, 113120280, 78649858, 80613637, 79496985, 128852750, 114169354, 79630346, 114168326, 128854292, 76417044, 128854549, 111940634, 76417301, 128853007, 113118491, 128854806, 128853264, 128855063, 128853778, 128853521, 128854035, 128852493, 33554440, 33554439, 33554441, 33554443)),
    ((129, 143, 159, 174, 190, 191, 431), 9, (77600771, 79566852, 79629312, 81664514, 77601029, 79630597, 77731841, 79629826, 112003096, 79629569, 114301977, 112002842, 128918800, 80677913, 79566352, 128917772, 114232604, 112002587, 79565324, 128918029, 128918286, 128918543, 128919057)),
    ((174, 191, 223), 3, (117314328, 115217945, 114167322)),
    ((160, 174), 2, (115151640, 113184537)),
    ((189, 190, 195), 2, (112986136, 115217177, 115215130)),
    ((4,), 1, (100861976,)),
    ((21,), 1, (108663320,)),
    ((165, 185, 190), 4, (113318424, 79497496, 102306585, 115152410)),
    ((167,), 1, (112854808,)),
    ((136, 165), 2, (102175256, 102176537, 113052442)),
    ((137, 171, 231), 3, (111807256, 109577753, 110630682)),
    ((23, 41, 170, 189, 224), 6, (112531736, 78186264, 111740954, 111741467, 110693913, 108729116, 116200478, 109579549)),
    ((43, 58, 86, 88, 170, 171, 182, 187, 188, 202, 216, 218, 442), 13, (103422488, 78251544, 101321753, 78059801, 101388555, 108727578, 68818699, 76157722, 111744795, 77205787, 113972252, 129640210, 78318610, 129640724, 78319124, 129641238, 129640981, 129641495, 129640467, 33554442, 33554440, 33554441, 33554439, 33554438)),
    ((57, 83, 100, 106, 107, 117, 123, 138, 141, 169, 170, 171, 172, 173, 189, 219, 251, 253, 443), 12, (78059521, 78321668, 80418819, 79301381, 81271296, 79301124, 67833346, 79300610, 80354051, 111872025, 113052696, 129704204, 74057228, 129704718, 110695195, 129705489, 129706774, 110827290, 129705232, 129706003, 129707031, 129706517, 129705746, 129704461, 129704975, 129706260, 33554441, 33554439, 33554442, 33554443, 33554440, 33554438)),
    ((60, 107, 112, 114, 116, 122, 124, 154, 172, 173, 178, 189, 190, 220, 444), 13, (82515968, 78190596, 78387459, 78452737, 80288005, 78321922, 82516739, 111937048, 79501829, 111872537, 82517249, 111937306, 129770254, 79305742, 108793627, 78322459, 108792860, 76223004, 114102813, 110889502, 129769997, 129772567, 78450967, 129772310, 78450710, 129770768, 129771282, 129771539, 129769740, 129772053, 129771796, 129770511, 129771025, 33554443, 33554441, 33554442, 33554438, 33554439, 33554440)),
    ((140, 141, 145, 155, 157, 173, 174, 181, 183, 187, 188, 190, 191, 445), 11, (78780418, 81533441, 78387203, 79432453, 78387716, 78387968, 115150872, 78383640, 115151129, 78383897, 112795144, 112921370, 129835533, 129836047, 80483599, 129837589, 129835276, 76351765, 80482828, 129836818, 76350994, 129836561, 129837332, 76351508, 110954523, 129835790, 129837846, 129836304, 129837075, 129838103, 33554441, 33554439, 33554438, 33554442, 33554443)),
    ((143, 158, 174, 175, 191, 207, 208, 222, 446), 12, (78977027, 78518529, 79497218, 81660928, 77928965, 79632900, 81662213, 79633152, 112069144, 81661442, 129900812, 79437068, 112335111, 81661699, 78584839, 129901583, 80549135, 81661956, 129901326, 129901840, 129902868, 77465620, 78581268, 129902097, 129902611, 77465363, 129903639, 78582039, 129903125, 77465877, 129903382, 77466134, 129902354, 129901069, 33554441, 33554440, 33554442, 33554438, 33554443)),
    ((142, 174, 175, 177, 190, 447), 11, (80615941, 79562497, 81663235, 78584064, 78649604, 80678402, 129966348, 78513676, 112139032, 81596952, 129967633, 129966862, 113054745, 116200986, 129966605, 113051163, 79497754, 129967376, 129967119)),
    ((1, 222, 239), 4, (100668184, 101585945, 101455386, 82708505)),
    ((181, 206, 208), 3, (114099992, 116330265, 116200730)),
    ((3, 207, 223), 3, (100796952, 114497561, 82711833, 116265498)),
    ((206, 223), 3, (112335384, 83760920, 101520921)),
    ((), 0, ()),
    ((206, 222), 4, (114497816, 80546072, 114629401, 67965721)),
    ((), 0, ()),
    ((122, 153), 2, (101256472, 113971737)),
    ((170,), 3, (114891032, 67768600, 68753176)),
    ((24, 188, 204, 216), 4, (101390105, 113969176, 109647642, 111744283)),
    ((155, 171, 187, 205), 5, (101324312, 101454361, 80479769, 112855323, 114034714, 78252568, 114037788)),
    ((45, 61, 84, 101, 134, 186, 187, 199, 201, 204, 219, 220, 221, 459), 4, (117053976, 67833624, 111875097, 130755607, 130755350, 130754836, 130754322, 130755093, 130754579, 33554443, 33554441, 33554439, 33554442, 33554438, 33554440)),
    ((128, 132, 140, 146, 156, 172, 189, 202, 205, 219, 220, 221, 222, 236, 460), 10, (83564546, 80615424, 81533185, 81598467, 80287746, 67899653, 81467908, 67899396, 81468160, 115083288, 80415493, 130819601, 101455627, 115082777, 101454599, 111937818, 111937563, 130818316, 130820115, 130820629, 130819087, 130821143, 130818830, 130819858, 130820372, 130818573, 130820886, 130819344, 33554441, 33554438, 33554442, 33554440)),
    ((47, 62, 129, 131, 133, 139, 145, 148, 157, 173, 188, 190, 193, 197, 207, 220, 221, 222, 223, 237, 461), 11, (81664004, 81532929, 80353536, 68950531, 80481029, 80747010, 81533699, 80353794, 101518360, 117185305, 130884109, 81402125, 67965209, 101519131, 107811610, 130884880, 130884623, 81532175, 81532432, 130886165, 130886679, 130885394, 130885651, 130885908, 130883852, 130884366, 130886422, 130885137, 33554442, 33554443, 33554440, 33554439, 33554441, 33554438)),
    ((160, 162, 174, 176, 191, 204, 207, 221, 222, 223, 238, 462), 12, (80025603, 81729536, 81664258, 82710789, 79763457, 81729797, 80681220, 82709761, 82710532, 101452824, 113449241, 81594905, 130950159, 115218202, 80747290, 81597711, 115149595, 130949388, 116265735, 130950673, 130951701, 78514453, 116265992, 130952215, 130951444, 78514967, 130951187, 130951958, 130949902, 130950930, 130950416, 130949645, 33554438, 33554443, 33554441, 33554442)),
    ((175, 191, 206, 222, 223, 463), 12, (79829251, 83826693, 81726464, 81795844, 81726978, 80611073, 81727492, 117314584, 114100761, 81726721, 82775576, 131015438, 79562766, 81662990, 116199962, 131014924, 81662476, 131015695, 131016209, 131015181, 131015952)),
    ((175, 205, 206, 222, 223), 7, (114629145, 67965465, 113318168, 81660184, 80878360, 101454874, 113117979, 113116700)),
    ((1,), 1, (101779224,)),
    ((5, 19, 208, 255), 4, (100928024, 101845529, 117314843, 116266778)),
    ((194, 197), 2, (115281688, 116264729)),
    ((19, 21), 2, (101845016, 101976345)),
    ((22, 164, 197, 208), 2, (102042392, 102045465, 115148314, 115148571)),
    ((23, 25, 216), 4, (102238488, 77075736, 102107161, 102503706)),
    ((9,), 2, (109452056, 75043096)),
    ((58, 187, 221, 253), 8, (114694680, 81529112, 114956314, 67832858, 110759705, 80288537, 68817434, 112858907)),
    ((170, 200), 3, (101322264, 68752408, 111741721)),
    ((205, 216, 235), 2, (112854552, 115086105, 112857882)),
    ((172, 173, 204, 220, 221), 6, (101518873, 113969690, 114039576, 113968667, 81595928, 102437660, 112923677)),
    ((131, 140, 148, 189, 204, 205, 216, 218, 221, 250, 252, 476), 9, (114034456, 115022873, 67898649, 114034971, 80414489, 102503432, 112985882, 131869719, 80548119, 131868948, 77334548, 131868434, 131869205, 131868691, 131869462, 33554441, 33554439, 33554442, 33554438, 33554443)),
    ((172, 173, 177, 181, 189, 191, 204, 206, 213, 219, 223, 241, 253, 477), 13, (81270787, 83499012, 80549888, 80484354, 81467650, 67964161, 80550149, 80484608, 101453592, 80415000, 80550659, 68883736, 131933199, 80484879, 81528577, 131933456, 131933970, 131933713, 131934741, 78448917, 131934227, 80612627, 131932942, 131935255, 78449431, 131934484, 131932428, 131932685, 131934998, 33554442, 33554443, 33554441, 33554438, 33554440, 33554439)),
    ((174, 175, 176, 178, 190, 191, 205, 206, 207, 208, 223, 254, 478), 15, (81860866, 80746752, 80615684, 82647299, 80025857, 80616197, 83630597, 113252888, 116264473, 131997964, 80681484, 80480792, 117315082, 131999249, 80545817, 112068634, 80614426, 131998478, 132000277, 80678677, 131998735, 79563029, 132000791, 80679191, 131998992, 131998221, 132000534, 79563286, 80678934, 132000020, 131999763, 131999506, 33554441, 33554440, 33554439, 33554443, 33554438)),
    ((174, 206, 207, 211, 255, 479), 13, (80746499, 78649345, 81660420, 82775040, 79894533, 80680962, 116202008, 132063500, 79829516, 80610828, 82709528, 132064014, 80611342, 114101017, 132064528, 115152666, 132063757, 132064785, 80612113, 132064271)),
    ((17, 44, 207, 239), 4, (101716505, 112794648, 74190104, 116262426, 116266523)),
    ((2, 222, 255), 4, (100730904, 100731418, 116464153, 101649947, 67965977)),
    ((3, 45, 81), 2, (100797208, 100796185, 100798747, 107745818)),
    ((2, 4), 2, (100862232, 100730393)),
    ((5, 9), 4, (100928280, 110566169, 67634969, 76026649)),
    ((6, 30, 86, 244, 255), 5, (116857112, 72159768, 100996122, 107681051, 100993049, 116197148)),
    ((7, 10, 23), 4, (107552024, 101058073, 74058776, 101058586, 102106907)),
    ((6, 25), 3, (112728600, 76091672, 100993817)),
    ((24, 42, 241), 4, (109711128, 77141272, 109579801, 116197914)),
    ((25, 26, 153, 250), 6, (116791832, 83434264, 76092440, 101256729, 116923418, 76091418, 109646363, 68748827)),
    ((10, 11), 3, (107614489, 116137752, 74061336, 107616026, 67767066, 107615003, 67766043)),
    ((59, 91, 188, 238, 255), 7, (117120024, 67834392, 110893850, 114956825, 101389595, 76222746, 101389085, 78318873, 116197404, 116198174)),
    ((42, 93, 109, 124, 141, 234, 238, 255), 12, (117311257, 101583899, 116988952, 76156952, 83696667, 116197662, 110891546, 69014814, 109841180, 101321247, 111941149, 80484124, 114038304)),
    ((61, 161, 165, 185, 191, 193, 207, 222, 223, 229, 232, 235, 236, 252, 253, 254, 493), 7, (107810072, 117251353, 67966233, 111875355, 114099738, 112006684, 132983574, 132983831, 132982546, 132982803, 132983317, 132983060, 33554441, 33554438, 33554440, 33554443, 33554442, 33554439)),
    ((14, 93, 108, 127, 192, 194, 206, 210, 211, 222, 223, 224, 239, 254, 255, 494), 13, (82909444, 83826945, 82582272, 68029954, 82844165, 83827205, 82583043, 68029697, 117311512, 133047825, 82516994, 68030211, 133046797, 83696386, 111022873, 133047568, 101585671, 83823879, 111939354, 133047054, 101585414, 109842971, 83823622, 133048853, 133046540, 80611605, 133048339, 117379082, 133049110, 80611862, 133048596, 133048082, 133047311, 133049367, 33554443, 33554440, 33554441)),
    ((13, 14, 79, 193, 207, 223, 254, 255, 495), 12, (81795584, 79698178, 69081093, 83824387, 83761412, 82708225, 83824130, 101650201, 83171845, 133112076, 101517080, 83759628, 101649690, 109909019, 107680540, 133112590, 133112847, 133113104, 133112333, 133113361)),
    ((1, 238, 255), 3, (117311000, 100668441, 101585178)),
    ((18, 225, 238), 5, (101779480, 115874329, 68030489, 69015065, 115148826)),
    ((19,), 1, (101844760, 101845785)),
    ((4, 20), 2, (100861464, 101910809, 101910042)),
    ((6, 8, 21, 28), 6, (116988440, 82123544, 73142040, 100993562, 109580057, 101976603)),
    ((22, 239), 2, (102041112, 102041625, 117379354)),
    ((23, 27, 233), 3, (108663832, 68814872, 102107673, 108662298)),
    ((24, 229), 2, (102172440, 102565401)),
    ((8, 9, 58, 233, 255), 5, (109580568, 109581850, 117311769, 110759963, 78190107, 102238748)),
    ((9, 59, 233, 236, 244), 5, (109776152, 108596249, 102303771, 102435098, 110695964)),
    ((26, 203, 221), 5, (115940121, 75107353, 102503960, 81529368, 102372634)),
    ((75, 76, 170, 204, 235), 6, (102437912, 111810841, 77272345, 101322779, 68752923, 111809050, 77270042, 112920092)),
    ((92, 109, 205, 222), 6, (116202264, 77336344, 111940377, 101521178, 102504219, 81529627)),
    ((15, 76, 91, 236, 237, 238), 8, (114826009, 112925210, 102699288, 76288282, 102568987, 78319897, 102568476, 82642460, 115149085)),
    ((30, 126, 176, 195, 207, 210, 222, 236, 238, 239, 240, 248, 255, 510), 8, (102635275, 101586457, 82709017, 116202520, 77467672, 102634504, 134097686, 82776086, 102634247, 134097172, 81659924, 134096915, 82775315, 102633990, 134096658, 81659667, 134097943, 81659410, 82776343, 134097429, 33554441, 33554442)),
    ((95, 207, 238, 239, 245, 511), 16, (82843648, 82581761, 68096004, 83757829, 82712578, 81861378, 83368195, 68094976, 82778371, 82778625, 115678233, 69014297, 114432536, 134161423, 116071962, 68031759, 81727768, 69015322, 134161166, 107877403, 134160909, 134161937, 134160652, 134161680)),
)

LEFT, RIGHT0, RIGHT1 = CHUNKS, 2 * CHUNKS, 3 * CHUNKS
SIZE = 384 // CHUNKS
MAX_SENDS = max(len(p[2]) for p in PLAN)
MAX_FROM = max(1, max(len(p[0]) for p in PLAN))
MESH = pl.DeviceIdType.MESH


def nt_dot(left, right):
    return lax.dot_general(left, right, (((1,), (1,)), ((), ())), preferred_element_type=jnp.float32)


def choose(index, low, high, leaf):
    if all(PLAN[i] == PLAN[low] for i in range(low, high)):
        leaf(PLAN[low])
        return
    middle = (low + high) // 2

    @pl.when(index < middle)
    def _():
        choose(index, low, middle, leaf)

    @pl.when(index >= middle)
    def _():
        choose(index, middle, high, leaf)


def kernel(upper_ref, mask_hbm, out_ref, buf, acc, mask_ref, table, origin, count, in_sem, send_sem, recv_sem):
    brow, column = lax.axis_index("brow"), lax.axis_index("bcol")
    row, half = brow // 2, brow % 2
    own = buf.at[pl.ds(0, 384)]
    load = pltpu.make_async_copy(upper_ref, own, in_sem.at[0])
    load.start()
    load_mask = pltpu.make_async_copy(mask_hbm, mask_ref, in_sem.at[1])
    load_mask.start()

    def leaf(plan):
        origins, targets, sends = plan
        count[0] = len(origins)
        count[1] = targets
        count[2] = len(sends)
        for i, v in enumerate(origins):
            origin[i] = v
        for i, v in enumerate(sends):
            table[i] = v

    choose(row * 16 + column, 0, 256, leaf)
    sends = count[2]
    barrier = pltpu.get_barrier_semaphore()

    @pl.loop(0, count[0])
    def _(i):
        v = origin[i]
        there = ((v >> 4) & 15) * 2 + (half ^ (v >> 8))
        pl.semaphore_signal(barrier, inc=1, device_id=(there, v & 15), device_id_type=MESH)

    load_mask.wait()
    load.wait()
    for i in range(3):
        for j in range(6):
            keep = mask_ref[i, j].astype(jnp.float32)
            at = (pl.ds(i * 128, 128), pl.ds(j * 128, 128))
            buf[at] = (buf[at].astype(jnp.float32) * keep).astype(jnp.bfloat16)

    @pl.when(count[1] > 0)
    def _():
        pl.semaphore_wait(barrier, count[1])

    def slot(index):
        return buf.at[pl.ds(pl.multiple_of(index * SIZE, SIZE), SIZE)]

    def copy(v, i):
        there = ((v >> 20) & 15) * 2 + (half ^ ((v >> 24) & 1))
        return pltpu.make_async_remote_copy(
            src_ref=slot(v & 255),
            dst_ref=slot((v >> 8) & 255),
            send_sem=send_sem.at[i],
            recv_sem=recv_sem.at[(v >> 8) & 255],
            device_id=(there, (v >> 16) & 15),
            device_id_type=MESH,
        )

    def arrived(index):
        pltpu.make_async_copy(slot(index), slot(index), recv_sem.at[index]).wait()

    @pl.loop(0, sends)
    def _(i):
        v = table[i]

        @pl.when((v & (1 << 25)) != 0)
        def _():
            arrived(v & 255)

        @pl.when((v & (1 << 26)) != 0)
        def _():
            copy(v, i).start()

    has0 = (row == 0) | ((column >= row) & (row + column >= 16))
    has1 = (column < 15) & ((row <= 1) | ((column + 1 >= row) & (row + column >= 16)))
    here = pl.ds(pl.multiple_of(half * 384, 128), 384)
    other = pl.ds(pl.multiple_of(384 - half * 384, 128), 384)

    def rows(index):
        return buf[pl.ds(pl.multiple_of(index * SIZE, SIZE), 384), :]

    @pl.when(has0)
    def _():
        right = jnp.where(row + column == 0, 0, RIGHT0)
        acc[:, here] = nt_dot(rows(0), rows(right))

        @pl.loop(0, CHUNKS)
        def _(j):
            arrived(SIB + j)

        acc[:, other] = nt_dot(rows(0), rows(SIB))

    @pl.when(has1)
    def _():
        left = jnp.where(column == 0, RIGHT1, LEFT)
        for columns, right in ((here, RIGHT1), (other, SIB + CHUNKS)):
            if right != RIGHT1:

                @pl.loop(0, CHUNKS)
                def _(j):
                    arrived(SIB + CHUNKS + j)

            term = nt_dot(rows(left), rows(right))

            @pl.when(has0)
            def _():
                out_ref[:, columns] = (acc[:, columns] + term).astype(jnp.bfloat16)

            @pl.when(jnp.logical_not(has0))
            def _():
                out_ref[:, columns] = term.astype(jnp.bfloat16)

    @pl.when(has0 & jnp.logical_not(has1))
    def _():
        out_ref[...] = acc[...].astype(jnp.bfloat16)

    @pl.when(jnp.logical_not(has0 | has1))
    def _():
        out_ref[...] = jnp.zeros_like(out_ref)

    @pl.loop(0, sends)
    def _(i):
        v = table[i]

        @pl.when((v & (1 << 26)) != 0)
        def _():
            copy(v, i).wait_send()


def per_device(upper_store, block_mask):
    return pl.pallas_call(
        kernel,
        out_shape=jax.ShapeDtypeStruct((384, 768), jnp.bfloat16),
        in_specs=[pl.BlockSpec(memory_space=pl.ANY)] * 2,
        out_specs=pl.BlockSpec(memory_space=pltpu.VMEM),
        scratch_shapes=[
            pltpu.VMEM((SLOTS * SIZE, 768), jnp.bfloat16),
            pltpu.VMEM((384, 768), jnp.float32),
            pltpu.SMEM((3, 6), jnp.int32),
            pltpu.SMEM((MAX_SENDS,), jnp.int32),
            pltpu.SMEM((MAX_FROM,), jnp.int32),
            pltpu.SMEM((3,), jnp.int32),
            pltpu.SemaphoreType.DMA((2,)),
            pltpu.SemaphoreType.DMA((MAX_SENDS,)),
            pltpu.SemaphoreType.DMA((SLOTS,)),
        ],
        compiler_params=pltpu.CompilerParams(
            collective_id=0, has_side_effects=True, vmem_limit_bytes=60 * 2**20
        ),
        name="cannon_steps",
    )(upper_store, block_mask)


def solution(mesh):
    spec = P("brow", "bcol")
    return jax.shard_map(per_device, mesh=mesh, in_specs=(spec, spec), out_specs=spec, check_vma=False)
```

```python
import jax
import jax.numpy as jnp
from jax import lax
from jax.experimental import pallas as pl
from jax.experimental.pallas import tpu as pltpu
from jax.sharding import PartitionSpec as P

CHUNKS = 6
SLOTS = 45
SIB = 33
PLAN = (
    ((1, 14, 16, 31, 32, 192, 240, 256), 5, (83894528, 83894785, 83895042, 83895299, 83895556, 83895813, 134217728, 102630936, 104799001, 117451799, 70127641, 117450514, 117451542, 117451285, 103682842, 117450771, 103683099, 117451028, 68028443)),
    ((2, 3, 13, 14, 15, 17, 18, 33, 225, 227, 257), 10, (79697921, 69212419, 117516307, 68163588, 67114757, 80812051, 82843906, 117515793, 68163345, 117516050, 68224530, 67113472, 117515279, 68162831, 117515536, 68163088, 117517078, 104665112, 117517335, 68225815, 101517849, 117515022, 68162574, 117516821, 117514508, 117516564, 117514765, 134217728, 33554439, 33554443, 33554440, 33554441, 33554442, 33554438)),
    ((3, 12, 17, 18, 19, 32, 34, 35, 48, 53, 64, 194, 226, 258), 9, (117580301, 68227853, 69278723, 81860610, 117580558, 68294917, 67176193, 68228110, 81861124, 101845272, 81991936, 106371353, 72093721, 117580815, 68228367, 117582100, 117581072, 117582614, 117581586, 117581843, 117581329, 117580044, 117582871, 117582357, 134217728, 33554438, 33554441, 33554440, 33554442, 33554443, 33554439)),
    ((5, 6, 18, 20, 21, 33, 35, 37, 39, 50, 53, 179, 227, 243, 259), 8, (79828996, 68294658, 67241472, 81926149, 67242243, 81926401, 101914648, 67180056, 117645837, 68293389, 117646608, 117645580, 100992537, 117646351, 68293132, 117648407, 117647122, 68293903, 117647379, 117646865, 117647636, 117648150, 117647893, 117646094, 134217728, 33554442, 33554439, 33554441, 33554440, 33554438, 33554443)),
    ((5, 19, 20, 21, 34, 36, 64, 66, 68, 82, 84, 85, 164, 210, 228, 260), 8, (78845954, 68425985, 68491268, 81991683, 67442949, 83040256, 101976856, 101910553, 117711630, 101975578, 68359182, 117711116, 101910299, 117711887, 117713686, 117712401, 117713172, 117712658, 117712915, 117713943, 117712144, 117713429, 117711373, 134217728, 33554441, 33554440, 33554438, 33554443, 33554439, 33554442)),
    ((3, 4, 20, 21, 22, 23, 37, 39, 65, 67, 69, 71, 83, 85, 229, 231, 244, 261), 8, (80877572, 69474560, 68425729, 67373315, 82057221, 67373058, 102041368, 117776909, 68424461, 117777423, 68424975, 102041882, 100862745, 117777937, 68425489, 117777166, 117777680, 117778965, 117778708, 117779479, 117776652, 117778451, 117778194, 117779222, 134217728, 33554438, 33554441, 33554439, 33554442, 33554443, 33554440)),
    ((7, 12, 21, 22, 23, 38, 87, 102, 116, 130, 164, 230, 262), 11, (67311872, 83106308, 68491779, 117843216, 68490768, 68622849, 82123010, 117842959, 68490511, 82254085, 102106649, 103488792, 102107418, 72092952, 102107931, 73077528, 117843987, 117842188, 68489740, 117844758, 117843473, 117843730, 117844244, 117844501, 117845015, 117842445, 117842702, 134217728, 33554441, 33554438, 33554440, 33554442, 33554439, 33554443)),
    ((9, 22, 23, 24, 25, 39, 41, 71, 99, 101, 103, 115, 118, 119, 135, 263), 8, (69605892, 82188544, 68556801, 67504387, 82188802, 68557061, 111548696, 75042328, 102172953, 117908752, 68556304, 117908238, 68555790, 117910551, 117907981, 68555533, 117908495, 117909523, 117910037, 117910294, 117909266, 117909009, 117909780, 117907724, 134217728, 33554439, 33554440, 33554441, 33554443, 33554442, 33554438)),
    ((10, 24, 25, 40, 56, 57, 72, 104, 120, 132, 136, 137, 152, 228, 264), 13, (68622593, 68687874, 83106051, 69475072, 68753667, 68688645, 83367941, 69671684, 105520152, 67700760, 78125828, 69802240, 75043864, 117973774, 68621326, 102237977, 117974288, 68621840, 102239002, 117974031, 68621583, 117974802, 117973517, 117975316, 117975573, 117975059, 117976087, 117974545, 117975830, 117973260, 134217728, 33554441, 33554440, 33554438, 33554443, 33554442, 33554439)),
    ((8, 11, 24, 26, 27, 41, 43, 57, 73, 105, 135, 137, 153, 199, 233, 265), 13, (82057473, 67573762, 68753411, 71833600, 68688130, 81205253, 69737477, 83368452, 70785284, 83433728, 70851844, 102173208, 118040081, 68687633, 118039310, 68686862, 102304537, 118041366, 118039567, 118039053, 118040595, 118041623, 118039824, 118041109, 118040852, 118038796, 118040338, 134217728, 33554439, 33554442, 33554440, 33554443, 33554441, 33554438)),
    ((12, 26, 27, 29, 42, 90, 166, 168, 170, 186, 200, 202, 217, 234, 236, 251, 266), 15, (82188288, 69736451, 67639298, 68818945, 68884484, 82450693, 69475332, 67836421, 68885251, 74059009, 67836672, 102369560, 103488281, 102303514, 102368795, 70983193, 72093465, 118104589, 118106902, 118104332, 68751884, 118105617, 101452572, 118104846, 118106131, 118106388, 118105360, 118105103, 118105874, 118106645, 118107159, 134217728, 33554438, 33554441, 33554443, 33554439, 33554442, 33554440)),
    ((10, 13, 27, 28, 29, 43, 167, 169, 171, 186, 187, 201, 203, 216, 235, 267), 12, (69605634, 68622339, 82450436, 68884736, 69015813, 68819203, 70982145, 82450949, 107679001, 68814617, 82451201, 105716248, 68880920, 101255962, 104664092, 101254683, 118170382, 68817934, 118170896, 68818448, 118171410, 118170125, 68817677, 118170639, 118172438, 118171153, 118171924, 118172695, 118169868, 118172181, 118171667, 134217728, 33554440, 33554438, 33554442, 33554443, 33554441, 33554439)),
    ((10, 13, 27, 28, 29, 44, 192, 202, 204, 206, 208, 220, 221, 268), 10, (67246340, 67508225, 70981888, 68950274, 69015552, 67770627, 72093186, 69016068, 68885509, 72093957, 102500376, 102500121, 118236689, 69016593, 118236432, 68883984, 105648903, 71109895, 118235404, 118236175, 68882956, 118235661, 118238231, 118236946, 118237717, 118237460, 118235918, 118237203, 118237974, 134217728, 33554442, 33554441, 33554438, 33554443, 33554440)),
    ((1, 15, 28, 29, 30, 45, 195, 197, 205, 208, 219, 221, 225, 237, 239, 252, 269), 14, (68884995, 67180548, 71047938, 68950788, 69016325, 104208664, 67836928, 68879896, 69998592, 67897089, 78322200, 105713689, 68819737, 116333595, 102566170, 68880155, 118301197, 68948749, 118300940, 68948492, 118302482, 118303253, 118301454, 118303767, 118302225, 118301711, 118302996, 118302739, 118301968, 118303510, 134217728, 33554440, 33554443, 33554442, 33554439, 33554441, 33554438)),
    ((0, 15, 30, 31, 46, 74, 192, 236, 238, 240, 241, 254, 255, 270), 11, (67115268, 71111939, 68099074, 82778113, 69146880, 67180804, 70126592, 68099333, 102631192, 70127877, 100669959, 69143815, 70126849, 118366990, 111808793, 118366733, 103683594, 69144586, 118367247, 103683337, 69144329, 118369303, 82709271, 118366476, 118367504, 118369046, 118368275, 118368789, 82708757, 118367761, 118368532, 134217728, 118368018, 33554443, 33554440, 33554438)),
    ((14, 17, 29, 30, 225, 239, 255, 271), 14, (69212928, 68229125, 68028161, 83695621, 69144066, 103095322, 69011482, 68028932, 105713177, 68028675, 101517340, 100731931, 71179036, 69143552, 101518109, 100732184, 71111708, 118433040, 69080592, 118432012, 118432783, 69080335, 118432526, 118432269, 118433297, 134217728)),
    ((1, 30, 48, 62, 224, 272), 5, (100668952, 104930585, 71176217, 106827034, 118500375, 104729627, 118499090, 118499861, 118500118, 118499347, 118499604)),
    ((1, 2, 15, 18, 19, 48, 49, 81, 209, 241, 273), 7, (70260993, 81795328, 67178757, 68098049, 67178243, 68098816, 67178500, 100734217, 67177986, 103683864, 118564883, 100733960, 118565140, 118564626, 67243026, 118565654, 118565911, 118565397, 33554438, 33554442, 33554443, 33554439)),
    ((2, 3, 19, 48, 50, 80, 210, 212, 242, 274), 7, (67179265, 69277957, 82909186, 67311620, 68225283, 67179008, 100796440, 100731673, 118630676, 67309076, 118630419, 118631190, 118630162, 118631447, 118630933, 33554438, 33554441, 33554440, 33554442, 33554439, 33554443)),
    ((3, 4, 20, 35, 49, 51, 113, 243, 275), 8, (81008642, 68290048, 67246083, 80877828, 82974721, 82974981, 101779992, 118696726, 67375126, 118695955, 118695698, 118696212, 118696469, 118696983, 33554443, 33554442, 33554440, 33554441, 33554438, 33554439)),
    ((4, 5, 21, 26, 28, 36, 52, 82, 212, 244, 276), 11, (83040515, 67377410, 68356869, 100927256, 100861721, 83040768, 67377921, 68356612, 105192218, 68623130, 73142554, 118762262, 111745307, 67440662, 118761234, 75107611, 118761491, 67439634, 118762005, 118762519, 118761748, 33554440, 33554443, 33554439, 33554438, 33554441, 33554442)),
    ((4, 5, 6, 27, 51, 117, 119, 213, 245, 277), 11, (81008899, 70522881, 67377157, 68421634, 100862488, 83106564, 67377664, 112465945, 74124313, 100993306, 118827798, 118827284, 67505684, 118827027, 118827541, 118828055, 118826770, 33554439, 33554442, 33554443, 33554441, 33554438, 33554440)),
    ((6, 7, 54, 118, 214, 230, 246, 278), 7, (70457604, 81074181, 67442689, 83171328, 67443203, 83171586, 101058328, 101059353, 118893591, 67571991, 118892306, 118893334, 67570706, 118892820, 118893077, 118892563, 33554438, 33554441, 33554440, 33554443, 33554442, 33554439)),
    ((6, 7, 8, 9, 11, 20, 55, 57, 151, 183, 247, 279), 10, (81139970, 67508480, 82189057, 67508739, 83237124, 112794905, 67569433, 67508997, 100992794, 106630936, 102435611, 118958099, 118958356, 118958870, 118957842, 118958613, 118959127, 33554441, 33554442, 33554443, 33554439, 33554440, 33554438)),
    ((8, 9, 26, 56, 57, 58, 88, 152, 214, 248, 280), 10, (70719493, 67574019, 83302401, 67704836, 70719744, 70851586, 115874072, 67569688, 101189657, 101124891, 113842714, 75108634, 67705114, 119024406, 67702806, 119024663, 119024149, 119023378, 119023635, 119023892, 33554439, 33554440, 33554443, 33554441, 33554438, 33554442)),
    ((8, 9, 10, 57, 59, 166, 181, 200, 217, 233, 249, 251, 281), 10, (81139715, 72882178, 67639553, 82253829, 73996801, 67639813, 82385412, 70785536, 108597016, 67635480, 101124377, 119090199, 119089428, 119089942, 119089685, 119089171, 119088914, 33554439, 33554442, 33554441, 33554440, 33554438, 33554443)),
    ((10, 11, 13, 28, 58, 186, 216, 246, 250, 282), 13, (68426497, 82384898, 70850820, 67770881, 68688389, 83499264, 75108099, 101254936, 70982659, 101320985, 106696730, 71965444, 102500891, 119154964, 119155735, 119154450, 119155478, 119155221, 119154707, 33554439, 33554441, 33554438, 33554440, 33554442, 33554443)),
    ((10, 11, 12, 13, 23, 28, 29, 219, 221, 249, 251, 283), 14, (68491520, 70588932, 83236866, 67836161, 68950020, 67770371, 69933315, 67771136, 70916613, 101255704, 106630169, 67765785, 101255451, 103553562, 67897626, 71110426, 101387036, 119220500, 67898900, 119220757, 119221014, 119220243, 119221271, 119219986, 33554440, 33554438, 33554442, 33554439, 33554443, 33554441)),
    ((12, 13, 26, 27, 29, 60, 62, 205, 214, 220, 250, 252, 284), 11, (68426245, 83105795, 67966976, 67835908, 73141762, 67967745, 68819460, 71178241, 68880386, 101386265, 103553307, 67897883, 106697222, 102369816, 101455130, 119286550, 67964950, 119285779, 119285522, 119286036, 119286807, 119286293, 33554440, 33554439, 33554443, 33554442, 33554441)),
    ((11, 12, 13, 15, 30, 31, 63, 236, 241, 247, 253, 255, 285), 14, (69933059, 67967236, 68098306, 67901442, 71047429, 68945408, 67901697, 72158465, 101385752, 106631449, 101386778, 103422747, 67771419, 71110939, 119351315, 102438684, 119352086, 119351829, 119352343, 119351572, 119351058, 33554442, 33554443, 33554440, 33554441, 33554439, 33554438)),
    ((0, 14, 15, 31, 46, 47, 62, 239, 254, 286), 11, (69146629, 82122752, 68098562, 71175425, 67967491, 68163844, 71175939, 69011972, 68164352, 71175682, 104731656, 71176453, 101586712, 103746823, 71176967, 119417879, 68096279, 119417622, 83757590, 119417108, 119417365, 119416851, 119416594, 33554438, 33554443, 33554441, 33554442)),
    ((14, 15, 30, 253, 287), 10, (70192128, 68032513, 69076994, 67115008, 70129923, 71177989, 70193156, 111351832, 69012248, 104665625, 119481102, 67115790, 119480588, 119480845, 119481616, 119481873, 119481359, 134217728)),
    ((1, 15, 34, 35, 44, 46, 61), 6, (100798232, 100668697, 108863002, 103682587, 74190362, 100799772, 107746333, 105779998)),
    ((2, 18, 51, 52), 4, (103815960, 67309592, 103947291, 100734745, 67309851, 100865562, 100731164)),
    ((35, 68), 6, (72423429, 69212163, 67243265, 70326272, 67243522, 70260740, 100929048, 100799001, 100800282)),
    ((51, 62, 63, 64), 9, (100863256, 100863769, 71309569, 69213187, 70589188, 69343488, 69343749, 67245058, 105844762, 101913883, 107812124)),
    ((5, 8, 10, 44, 62, 85, 113), 7, (101979672, 100927001, 108730138, 109579291, 107614236, 104663326, 75044380, 100928797)),
    ((15, 43, 52, 85), 4, (100995353, 100865050, 100865304, 108728603, 105714716)),
    ((7, 11, 103, 119), 4, (101061400, 106371865, 101059098, 69868569, 101059867, 74060825)),
    ((8, 52, 59, 60, 86), 4, (100864536, 109776921, 109775900, 101124635, 100996637, 109778458)),
    ((9, 10, 41, 42, 136), 5, (107613976, 101191449, 104274715, 101190938, 109711646, 76155931, 101190428, 110694175, 101190685)),
    ((8, 57, 59, 120, 138), 11, (70326789, 79239426, 72554753, 75044864, 101127960, 70720004, 69738243, 101123609, 108666138, 76221978, 109647388, 101258523)),
    ((29, 38, 43, 60, 186), 8, (82581508, 76156418, 69737216, 78256129, 69737989, 82319363, 109712920, 108793881, 101323290, 105649947, 101320732)),
    ((6, 10, 27, 29, 139, 154), 10, (69867524, 75173378, 79305217, 69540613, 73079043, 104733208, 75172864, 101258778, 72159000, 107679513, 101386523, 101258268, 101386013)),
    ((13, 27, 28, 60, 61), 9, (81795073, 69474821, 71047171, 70981632, 71964676, 69212674, 101451288, 72094232, 103681819, 105649689, 101451804, 105649434)),
    ((46, 61, 62, 124), 12, (71112962, 81926656, 70392323, 74062337, 70982403, 71113216, 73144325, 73207812, 104537880, 74258200, 104799514, 74256922, 113973017, 105714459, 101517596, 101516829)),
    ((0, 14, 17, 31, 32, 44, 47, 60, 62, 63, 78, 302), 11, (71243781, 72224772, 71112705, 70326531, 72223744, 72224258, 104728088, 72224001, 104729114, 120463628, 70065420, 102768135, 120464913, 71244817, 102631705, 70192921, 120463885, 71111437, 71177497, 104728347, 105780746, 120466455, 68029207, 120465170, 105779718, 71240710, 68027922, 120466198, 120464656, 120465941, 120465427, 120464399, 120465684, 120464142, 134217728, 33554443, 33554440, 33554441)),
    ((30, 31, 46, 62, 63, 143, 303), 11, (70125313, 71047680, 73275906, 71178500, 71241475, 120529164, 71048204, 71241989, 105843992, 70327298, 71241732, 71240961, 120530192, 69077520, 71177744, 105714969, 114103834, 120530449, 120529935, 120529421, 120529678, 134217728)),
    ((17, 33, 34, 61, 62), 6, (101783064, 67244056, 101848603, 101716761, 108794394, 106828060)),
    ((34, 41, 46, 47, 82), 6, (101782040, 104864537, 73209113, 110694682, 101914395, 104795676)),
    ((33, 45, 52, 60, 63), 6, (100864792, 106829593, 107289115, 101848860, 75238939, 107746586)),
    ((22, 68, 85), 6, (72357890, 69277700, 70588416, 69408769, 69278469, 69409027, 101914136, 102042137, 101913114)),
    ((21, 67), 6, (69278212, 70588677, 69670912, 69539843, 70391809, 69540354, 101975832, 101979161)),
    ((27, 35, 51, 52, 62), 4, (100863000, 100865817, 107679770, 100800027, 104663068)),
    ((13, 101), 2, (102110488, 106695705)),
    ((24, 40, 41), 2, (102173464, 110694426, 102172185, 110694939)),
    ((9, 25, 58), 6, (110759448, 105454107, 101190169, 77204507, 102237722, 76090394, 77074970)),
    ((9, 24, 26, 107, 137, 153), 8, (101192984, 103357465, 68749849, 102172700, 102240794, 108597277, 112921883, 67701786)),
    ((27, 61, 74, 153), 11, (72751361, 81271043, 70785026, 83368708, 70785792, 79305477, 108795417, 111808539, 102241560, 107680026, 68815642, 75110170)),
    ((10, 11, 12, 26, 44, 45, 62), 10, (83433473, 71965187, 69671172, 69671936, 108728856, 82516485, 69802498, 106631705, 106762011, 102304028, 106630426, 104662813, 106632478, 104663839)),
    ((13, 29, 44, 47), 15, (70392578, 69671428, 75238657, 107745048, 69867780, 79436547, 73014277, 79436800, 103679514, 105649179, 69999643, 102501145, 71110171, 104731164, 72159513, 73144089)),
    ((1, 11, 12, 14, 15, 27, 29, 31, 36, 45, 46, 53, 59, 60, 63, 108, 317), 11, (70261248, 82647041, 70916356, 72161538, 102767897, 74256131, 121448981, 69999381, 70065173, 74256645, 106761242, 106763032, 73207321, 121448210, 121447953, 121446668, 121447439, 113972507, 121447696, 121447182, 121448724, 121449238, 121448467, 121449495, 121446925, 134217728, 33554442, 33554439, 33554441, 33554440, 33554443, 33554438)),
    ((15, 16, 28, 30, 31, 43, 46, 47, 60, 94, 318), 17, (68164097, 70064133, 73273348, 71244036, 69475843, 70064640, 121512461, 71244301, 73272834, 70064909, 70589442, 80550401, 70982913, 121512975, 70195471, 103680537, 73273091, 69409795, 106695960, 121512718, 121515031, 69077783, 73272320, 70193431, 70261765, 121513489, 105843718, 121514260, 73273862, 102500634, 70192660, 73143578, 121513232, 103681563, 121514774, 121512204, 121514517, 121513746, 121514003, 134217728, 33554442, 33554440, 33554439, 33554443, 33554441)),
    ((0, 45, 46, 47, 49, 62, 319), 10, (70392069, 70129664, 72226818, 69409284, 70130180, 70195201, 72290051, 106764056, 70130433, 121578511, 72226063, 104663577, 121579025, 72226577, 70126353, 121578768, 102565658, 121577997, 104666651, 104666908, 104662557, 121578254, 121577740, 134217728)),
    ((35, 49, 68, 79, 95), 4, (102963992, 67374872, 100799257, 105776666, 105778971, 105777180)),
    ((16, 77, 78, 86, 93, 94), 6, (108859416, 106306329, 76353049, 100996890, 106759707, 109909276, 105715229)),
    ((69, 74, 93), 3, (100930072, 111808281, 109843738)),
    ((77, 85, 93), 5, (104077592, 67440152, 109451545, 75304217, 109907994)),
    ((69,), 7, (74520577, 71309315, 69343234, 72685568, 72489221, 70457348, 100931096, 100930585, 100931354)),
    ((20, 78, 85, 86), 7, (100994840, 71440384, 77863171, 71571460, 72620033, 71571714, 71571973, 105711129, 100995866, 107681563)),
    ((74,), 1, (111807512, 111807769, 111808026)),
    ((81, 86, 119), 3, (101125656, 100996377, 105711386)),
    ((9, 77), 3, (101189144, 76026392, 105646617)),
    ((56, 92, 153), 5, (106043928, 72948760, 78320152, 101256985, 111743514)),
    ((8, 26, 44, 59, 123), 9, (71440643, 68032773, 71702528, 70916868, 106633752, 74190872, 71702785, 108661529, 71703042, 110761242, 108662811, 107613724)),
    ((76, 91, 140), 7, (73013507, 72947972, 73078789, 77270273, 83565056, 77270530, 111873817, 109775128, 106632218, 106632987)),
    ((2, 6, 10, 12, 42, 44, 60, 72, 77, 90, 91, 93, 125, 140, 332), 11, (83564803, 74324225, 83696133, 75176192, 76287490, 122430222, 72030734, 106694937, 77337881, 76288004, 122430993, 72030993, 108792600, 108859659, 106695194, 77338138, 76289803, 122431764, 122430736, 122431250, 122431507, 122429965, 122432278, 122430479, 122429708, 122432021, 122432535, 134217728, 33554438, 33554441, 33554442, 33554439, 33554440)),
    ((11, 13, 15, 29, 37, 43, 45, 47, 60, 61, 65, 69, 71, 92, 93, 94, 95, 125, 163, 229, 333), 12, (71506177, 72751106, 73209859, 71374852, 71833860, 73210624, 73014017, 72092421, 106629144, 107810329, 122495501, 73143053, 122496272, 73143824, 107681306, 122495758, 73143310, 122496015, 107812379, 107811868, 122496529, 122497043, 122496786, 122497557, 122497814, 122497300, 122495244, 122498071, 134217728, 33554443, 33554442, 33554440, 33554438, 33554441, 33554439)),
    ((32, 46, 63, 64, 79, 93, 94, 95, 110, 334), 10, (72423681, 73340931, 74322181, 73275397, 73210116, 71637248, 73341186, 74320896, 73276163, 74321924, 122561808, 73341456, 104930329, 73206041, 75370265, 106828824, 74321410, 122560780, 73341708, 106760218, 106825499, 122561294, 73208846, 122561037, 107878155, 122562836, 70125588, 122563093, 107876870, 70125845, 122563607, 122562065, 122561551, 122563350, 122562322, 134217728, 122562579, 33554442, 33554441, 33554440, 33554439)),
    ((35, 47, 62, 63, 94, 95, 335), 8, (73338370, 75372803, 73275652, 73338113, 71309824, 116333336, 75370008, 72223493, 106826009, 74387225, 73338627, 122627087, 73274639, 73339141, 107941146, 73338884, 73337856, 122626573, 73274125, 122627344, 73274896, 122626316, 122626830, 122627601, 134217728)),
    ((51, 92, 94, 95), 6, (101848088, 107026713, 72948249, 75369753, 108926746, 73272090, 110890267)),
    ((34, 78), 5, (115481368, 110959385, 71768601, 68228888, 74321177)),
    ((68, 73, 85), 4, (101978648, 103881497, 67375385, 110890010)),
    ((41, 86, 108), 3, (112924440, 110693657, 100995610)),
    ((69, 92), 3, (100930328, 113973529, 77336089)),
    ((68,), 8, (72488960, 69474308, 71636995, 71505922, 69540101, 67439873, 104012312, 67374104)),
    ((58, 65, 77, 91), 11, (71375365, 82123266, 71768323, 72555008, 69672196, 109843480, 71637505, 112857626, 111614489, 77204761, 106694683)),
    ((2, 38, 93, 103), 3, (101061144, 106632729, 106630683, 111874842)),
    ((25, 91), 3, (110629912, 68683800, 112858137)),
    ((73, 75, 80, 90, 122), 5, (110825497, 108594712, 106628636, 110825243, 108725789, 106759962)),
    ((60, 75, 77, 123, 171), 7, (106502937, 78255385, 101323544, 108794140, 76224284, 105645851, 108660762)),
    ((6, 23, 27, 29, 43, 59, 74, 75, 77, 87, 89, 92, 93, 106, 347), 12, (72751616, 83695877, 72030467, 76225028, 72882434, 82516225, 110825752, 108728089, 108729882, 123412748, 74060300, 123414290, 72092690, 123414033, 123413519, 74061071, 106761499, 123413005, 123414547, 123414804, 123415061, 123415318, 123415575, 123413776, 123413262, 134217728, 33554442, 33554441, 33554440, 33554443, 33554439, 33554438)),
    ((20, 26, 28, 45, 54, 60, 62, 76, 77, 86, 93, 109, 156, 244, 348), 13, (71899136, 72620290, 73210369, 83630083, 75372549, 72161282, 73075204, 72358657, 73210885, 123478798, 77336580, 74126350, 73074947, 110892811, 106896408, 74192664, 123479312, 123479569, 123480083, 123479826, 72158226, 123478541, 123479055, 123480854, 123481111, 123478284, 123480597, 123480340, 134217728, 33554441, 33554439, 33554442, 33554440, 33554438)),
    ((45, 49, 59, 61, 63, 65, 77, 78, 89, 91, 92, 94, 95, 109, 349), 15, (71375106, 82582016, 72096003, 73140997, 74258689, 71506436, 104995352, 105712153, 116267803, 72091163, 106371610, 72096260, 75303963, 72091928, 75306521, 123544848, 106629916, 74192400, 123546647, 72225047, 73074458, 75304728, 108860445, 123543820, 123545876, 123546133, 123544591, 123545619, 123546390, 123544334, 123545362, 123544077, 123545105, 134217728, 33554443, 33554441, 33554440, 33554438, 33554442, 33554439)),
    ((16, 47, 48, 50, 62, 78, 79, 80, 126, 350), 10, (72358145, 72227075, 72292354, 75370500, 73206533, 72227330, 75370757, 75369472, 105712408, 71375616, 107877913, 72223257, 123610384, 72162064, 107876123, 105780250, 123609870, 72162318, 123610127, 123611412, 71174164, 123609356, 108926217, 72289812, 123612183, 71174935, 123611669, 108925703, 72290583, 71174421, 123609613, 123610898, 123611155, 123610641, 123611926, 134217728, 33554443, 33554438, 33554442, 33554440)),
    ((78, 79, 92, 351), 12, (72358405, 74323972, 72292611, 72227585, 74386946, 108860696, 75371008, 72292865, 123675406, 83827470, 106765593, 71310350, 123675149, 72157209, 74322701, 74386432, 123675663, 106763802, 123676177, 106762779, 123675920, 123674892, 106762524, 134217728)),
    ((110, 111, 127), 2, (108075544, 76420888, 109972761, 109974810, 109973019)),
    ((80, 126), 2, (112006936, 109908761)),
    ((111,), 1, (109974296,)),
    ((115, 117, 120, 126), 3, (101127448, 112006425, 107808282, 112005659)),
    ((108,), 2, (111938840, 79368984)),
    ((50, 119, 124), 4, (104208408, 67571480, 113972761, 109777946)),
    ((103,), 5, (74717184, 77862917, 74913793, 67506180, 74782722, 67505923, 101062168, 101061657)),
    ((120,), 6, (75634693, 74717443, 69605377, 73799684, 72816640, 73799938, 101127192)),
    ((123, 136), 3, (108660504, 101191962, 108660249, 109712411)),
    ((25, 108, 122, 138, 154, 230), 5, (108595481, 109645082, 101259036, 77138716, 108595995, 109644312, 107677470, 108597789)),
    ((10, 36, 38, 40, 45, 74, 91, 108, 120, 122, 123, 155, 187, 230, 234, 362), 9, (108661272, 111938587, 124396045, 75043597, 106634010, 74191642, 108730908, 78385436, 124396559, 75044111, 110757401, 124397073, 75044625, 112922377, 124398358, 73076758, 124395788, 124398615, 124396816, 124397330, 124397587, 124396302, 124397844, 124398101, 134217728, 33554440, 33554439, 33554438, 33554443, 33554442)),
    ((11, 21, 43, 53, 58, 69, 77, 92, 105, 109, 122, 123, 124, 125, 135, 157, 171, 229, 239, 363), 12, (74782981, 79367168, 75175938, 70851329, 74783492, 75110659, 74979845, 75111169, 108595225, 75111428, 112989464, 75237656, 78450456, 124461581, 124463380, 75109133, 124462352, 108726810, 75109904, 124461324, 124462095, 75109647, 107809051, 124462609, 124463894, 124464151, 124461838, 124462866, 124463637, 124463123, 134217728, 33554440, 33554438, 33554441, 33554439, 33554443, 33554442)),
    ((32, 50, 60, 74, 92, 93, 106, 123, 124, 125, 140, 156, 157, 224, 226, 364), 13, (72554501, 76159492, 73668609, 74062592, 75241730, 82713091, 78384642, 74783747, 74062853, 75242243, 108791832, 74258944, 73997825, 104667929, 75172121, 124527888, 124527631, 75175183, 124528659, 124529687, 124527117, 124529430, 124527374, 124526860, 124528402, 124529173, 124528145, 124528916, 134217728, 33554439, 33554443, 33554440, 33554441, 33554438, 33554442)),
    ((35, 45, 61, 77, 93, 99, 107, 108, 111, 124, 125, 126, 127, 157, 205, 237, 365), 13, (83630337, 75307008, 77401602, 75241985, 82582788, 75307781, 77339139, 75308036, 112004120, 77401859, 75236888, 109907225, 73139993, 107677210, 124593167, 75240719, 106760731, 76355099, 124593681, 75241233, 109777693, 124592910, 75240462, 124592653, 109909788, 124595223, 75240205, 124593938, 124594195, 124594709, 124593424, 124594966, 124594452, 124592396, 134217728, 33554440, 33554442, 33554439, 33554443, 33554441, 33554438)),
    ((76, 78, 81, 94, 95, 111, 126, 127, 142, 255, 366), 11, (74651904, 77403395, 75438085, 75307522, 74390020, 76419076, 75438337, 124659217, 75438865, 76419333, 124657932, 108857626, 75439116, 108926488, 73406721, 76418819, 124658960, 73407234, 109841689, 124658446, 108989446, 76419590, 124660245, 72222997, 124660502, 124659731, 72222483, 124660759, 124658703, 109975050, 124658189, 134217728, 124659988, 124659474, 33554441, 33554443, 33554440, 33554439)),
    ((79, 95, 110, 126, 127, 367), 11, (73406469, 75435779, 73537537, 75435522, 75436036, 111023896, 108075289, 74319360, 110038555, 75368475, 75435265, 124723982, 78451481, 75371534, 107809306, 77466905, 76484888, 124724239, 124723468, 124723725, 124724496, 124724753, 134217728)),
    ((125,), 2, (112989976, 112989721, 112988442, 75237913)),
    ((68, 96, 111), 4, (103030040, 68358936, 108990746, 108857113)),
    ((125,), 3, (109517336, 75237144, 79434520)),
    ((110, 120), 4, (101126936, 107158041, 75045145, 76418073)),
    ((102, 103, 117, 124), 3, (101059608, 101061913, 112987930, 111021083)),
    ((102, 107, 108, 126), 5, (102044696, 112922905, 107158298, 74717978, 112922651, 112923932, 75302426)),
    ((119, 120), 2, (102111000, 102109721, 101127706)),
    ((102, 120), 7, (73734147, 74848261, 75962369, 71768066, 74848512, 67571716, 103160600, 68490008, 101126681)),
    ((107, 137), 8, (74651649, 69801989, 73603075, 74914048, 74848772, 73865218, 101192472, 101193241, 107612954)),
    ((7, 8, 25, 36, 41, 57, 89, 105, 106, 107, 115, 122, 151, 215, 249, 377), 4, (110693400, 125379599, 76027151, 125379342, 125380884, 110957081, 125380627, 125378828, 125380113, 125381141, 125381398, 125379856, 125379085, 125380370, 125381655, 134217728, 33554442, 33554441, 33554439, 33554440, 33554438, 33554443)),
    ((20, 24, 26, 41, 58, 74, 90, 104, 106, 107, 123, 124, 180, 246, 250, 378), 10, (72947712, 73996547, 74127618, 73997061, 113711384, 75041284, 72949016, 107612441, 125445135, 76225551, 75040513, 107682330, 107611931, 79433754, 79432728, 107612700, 125446420, 125444364, 74124820, 110760989, 125445649, 125445392, 125446163, 125444621, 125447191, 125446934, 125445906, 125444878, 125446677, 134217728, 33554441, 33554442, 33554443, 33554439, 33554438, 33554440)),
    ((36, 37, 43, 59, 76, 89, 91, 106, 107, 108, 125, 138, 157, 185, 186, 379), 11, (71964933, 73930753, 74061828, 75106563, 73013762, 73931008, 107612184, 79367704, 125510414, 73931534, 110826009, 125511442, 74189842, 125509900, 76157452, 125512727, 74191127, 125510671, 76158223, 107678490, 125511185, 76158737, 125512470, 125512213, 125510157, 125511956, 125511699, 125510928, 134217728, 33554443, 33554441, 33554439, 33554440, 33554442, 33554438)),
    ((42, 48, 50, 58, 60, 76, 90, 107, 108, 109, 112, 114, 141, 188, 380), 15, (75307269, 77207809, 75110400, 70064389, 73734404, 74193155, 79433218, 75110916, 74717699, 75308289, 116138008, 76286488, 77405186, 125575693, 74259725, 107743002, 107677721, 107677979, 112004616, 79434760, 125578006, 74256406, 125576721, 125576978, 74255378, 125577749, 125576207, 125576464, 125575950, 125578263, 125575436, 125577492, 134217728, 125577235, 33554438, 33554441, 33554443, 33554439, 33554442)),
    ((32, 65, 67, 76, 93, 95, 109, 110, 113, 117, 124, 127, 140, 147, 157, 173, 381), 11, (74586113, 74192898, 74258432, 74127363, 72095749, 74455045, 74455300, 109845272, 108010009, 75172633, 110956827, 74189595, 107808794, 77403162, 77401112, 125643285, 72157461, 108726045, 110956572, 125640972, 125642000, 76289552, 125643542, 108729374, 125641229, 110957343, 74189340, 125642257, 125641743, 125643799, 125643028, 125642771, 125642514, 125641486, 134217728, 33554441, 33554442, 33554438, 33554439, 33554440, 33554443)),
    ((78, 79, 80, 92, 94, 95, 110, 111, 142, 158, 382), 14, (74783232, 77467138, 74389761, 83761156, 74324483, 73472005, 77467395, 75438596, 125707536, 74259216, 77467909, 109779736, 107877657, 125707793, 74259473, 77336856, 125706508, 73603331, 76354060, 125708050, 73270802, 125707279, 125706765, 125707022, 125709078, 73271830, 74387478, 125709335, 74387735, 134217728, 125708564, 73271316, 125708821, 125708307, 33554440, 33554438, 33554441, 33554442, 33554443, 33554439)),
    ((110, 111, 113, 126, 383), 10, (82712833, 74389509, 76421124, 74390274, 76421376, 76421891, 125772815, 73406991, 110958360, 74320143, 76484355, 125772558, 108863257, 76420110, 125773072, 74254105, 74320400, 108857882, 125772301, 108861211, 108859932, 125772044, 125773329, 134217728)),
    ((129, 140, 141, 143), 3, (110172696, 78517528, 114036505, 114035994, 112069915)),
    ((142, 158, 159), 5, (112135193, 110434330, 80549658, 109905688, 75504408)),
    ((103, 143), 2, (101062424, 112072473)),
    ((157,), 2, (115085848, 80546840)),
    ((137, 140), 3, (101193496, 76024600, 114036761)),
    ((156, 158), 2, (114103065, 110823960)),
    ((67, 137, 154, 215), 3, (109578008, 113971994, 109843225, 109582107)),
    ((114, 119, 137, 138), 4, (101125400, 101257753, 112004378, 107678235)),
    ((36, 72, 121, 132, 134, 139, 151, 152, 153, 166, 168, 184, 185, 228, 232, 244, 248, 392), 8, (69736707, 67636738, 77010945, 69736961, 67637252, 69737728, 79108096, 73931269, 79108357, 110626584, 109709337, 110626842, 126363410, 126362896, 126363153, 126361868, 126363667, 126364181, 126364438, 126363924, 126362639, 126362382, 126362125, 126364695, 134217728, 33554440, 33554441, 33554443, 33554438, 33554439, 33554442)),
    ((41, 56, 105, 138, 139, 151, 152, 154, 155, 169, 201, 231, 233, 393), 13, (75765765, 70850563, 77076482, 78125059, 75896833, 74979329, 79173888, 77011460, 74979588, 67637760, 109517080, 77137432, 101258009, 77137689, 126429460, 126427661, 77075213, 126428432, 77075984, 126428689, 126427918, 126428946, 126429974, 126427404, 126429717, 126430231, 126428175, 126429203, 134217728, 33554441, 33554438, 33554439, 33554440, 33554443, 33554442)),
    ((40, 42, 104, 108, 123, 136, 139, 154, 155, 170, 186, 232, 236, 394), 13, (77011202, 73996292, 77273088, 76089603, 77273857, 77274117, 103357208, 77138200, 110758169, 126493454, 77141006, 110758683, 111939610, 75963162, 110757916, 79369754, 126495510, 75173910, 126493968, 111809309, 126494225, 77141777, 126493197, 126492940, 126494482, 126494739, 126493711, 126495253, 126495767, 134217728, 126494996, 33554441, 33554442, 33554439, 33554440, 33554443, 33554438)),
    ((39, 41, 75, 90, 91, 101, 109, 122, 126, 140, 141, 154, 155, 157, 171, 173, 188, 235, 249, 395), 10, (76028162, 77207556, 76155139, 77208069, 77208320, 103488536, 77137944, 114102041, 77334809, 76154625, 111874074, 126558733, 77206285, 126559504, 109647132, 111875867, 77207056, 126558476, 77206028, 126560018, 126561046, 126559761, 126560275, 126561303, 126558990, 126559247, 126560532, 126560789, 134217728, 33554443, 33554439, 33554442, 33554440, 33554441, 33554438)),
    ((66, 76, 86, 110, 124, 125, 134, 141, 142, 155, 156, 157, 170, 172, 236, 238, 253, 396), 18, (76355585, 76683266, 72030211, 77273602, 80482565, 77338880, 75766020, 76356100, 75503875, 76221189, 113055000, 110889753, 110823194, 81532697, 78515992, 126624526, 77405454, 126625040, 77405712, 107742747, 78385691, 113053706, 126626068, 72091668, 126624269, 77271821, 75304468, 126625297, 126626839, 126626582, 126626325, 126624783, 126624012, 126625554, 126625811, 134217728, 33554441, 33554440, 33554438, 33554443, 33554439)),
    ((65, 67, 97, 109, 126, 129, 140, 145, 156, 173, 189, 239, 397), 12, (75241476, 77273346, 79370240, 77404163, 77338624, 82582533, 78388225, 77404677, 109058584, 76220184, 79498497, 76286211, 110822937, 109775386, 126689805, 77337357, 113054471, 126691090, 113055499, 126690062, 77337614, 126692118, 126690576, 126691604, 126690319, 126692375, 126691861, 126690833, 126691347, 126689548, 134217728, 33554441, 33554442, 33554438, 33554440)),
    ((96, 98, 110, 115, 127, 143, 144, 158, 159, 174, 398), 11, (75569153, 76290051, 78515200, 77535236, 76617733, 79632642, 78515714, 111023640, 126756112, 77536272, 110954778, 111022617, 75367961, 126756369, 108923163, 126755855, 77468955, 112072202, 126757911, 74320663, 112071174, 111086855, 126757140, 74319892, 78516999, 126756883, 126755084, 74319635, 126756626, 126755341, 126757397, 126757654, 126755598, 134217728, 33554443, 33554440, 33554441)),
    ((111, 127, 158, 159, 399), 11, (75503619, 77532674, 77469701, 76552193, 77532160, 75634949, 76417540, 103750168, 77400600, 77533188, 113120025, 77533445, 113120538, 126821391, 78581017, 126821134, 77468686, 78581530, 126821905, 126821648, 126820620, 126820877, 134217728)),
    ((143, 159), 2, (109971224, 111019545)),
    ((128, 142, 158), 5, (111155736, 76352280, 113056537, 80548889, 111087386)),
    ((140,), 1, (114036248,)),
    ((158,), 2, (112006168, 75302936)),
    ((157,), 2, (115086360, 80547352)),
    ((129,), 1, (110955288,)),
    ((153,), 1, (110627608,)),
    ((136, 137, 138, 228), 4, (102175512, 109643801, 109578778, 108596507)),
    ((56, 88, 136, 137, 150, 153, 168, 184, 214, 408), 5, (101192728, 76023832, 102241802, 102241031, 127412500, 76090900, 127412757, 76091157, 127412243, 127413271, 127413014, 127411986, 33554438, 33554443, 33554440, 33554441)),
    ((40, 49, 55, 83, 105, 121, 137, 138, 139, 154, 185, 187, 232, 249, 409), 11, (77072900, 82385154, 76027905, 70916099, 76945413, 77071872, 80156673, 70851072, 67703045, 76028418, 71899395, 78126083, 127478036, 127475980, 127477008, 127476494, 127476237, 127476751, 127477265, 127478293, 127477522, 127477779, 127478550, 134217728, 127478807, 33554442, 33554441, 33554438, 33554440, 33554439, 33554443)),
    ((56, 74, 86, 106, 122, 124, 138, 139, 155, 156, 186, 216, 248, 410), 10, (76158979, 76093440, 76224514, 69933572, 76093697, 73997317, 77138436, 109709848, 109451801, 109710106, 79432985, 109708827, 127542030, 78189582, 127543829, 76222229, 127542287, 127542801, 127542544, 127543315, 127541516, 127544086, 127541773, 127543058, 127544343, 127543572, 134217728, 33554439, 33554441, 33554442, 33554443, 33554440, 33554438)),
    ((75, 89, 91, 123, 133, 138, 140, 141, 156, 157, 159, 187, 251, 411), 10, (74062080, 76159235, 77203201, 76159749, 76160002, 109643288, 77203972, 109643547, 113908761, 76285977, 109644572, 127607309, 76160269, 109774874, 127607566, 78255118, 79498777, 127608337, 78255889, 127608080, 78255632, 127608594, 76286994, 127609365, 127607823, 127607052, 127609108, 127608851, 134217728, 127609879, 127609622, 33554440, 33554439, 33554438, 33554443, 33554441, 33554442)),
    ((76, 80, 82, 84, 92, 109, 126, 139, 140, 141, 157, 158, 188, 220, 235, 236, 252, 412), 13, (75831300, 76290561, 76355840, 77535747, 77404421, 77268994, 112007961, 80481305, 107743514, 127673616, 109839896, 78454032, 78386458, 127673359, 127674901, 76353301, 127675415, 127673873, 76353815, 127674130, 73139730, 76352530, 110761755, 127675158, 127673102, 127674387, 127672845, 127672588, 127674644, 134217728, 33554439, 33554443, 33554441, 33554438, 33554442, 33554440)),
    ((81, 109, 110, 121, 124, 125, 127, 140, 141, 142, 143, 149, 156, 159, 172, 189, 413), 18, (76814338, 80547073, 76224771, 76290309, 77334273, 75700224, 78453252, 77469952, 113053464, 127738638, 78518798, 74188814, 127740437, 113053978, 74128149, 110824217, 108726300, 127738895, 108860187, 127739409, 78386961, 127740951, 74255127, 127740180, 110826525, 127738124, 110827038, 127739152, 127739923, 127740694, 127738381, 127739666, 134217728, 33554442, 33554441, 33554439, 33554438, 33554440, 33554443)),
    ((111, 116, 126, 142, 143, 144, 157, 159, 190, 238, 254, 414), 11, (75569669, 76486660, 77535489, 79563776, 76617986, 76421635, 79564547, 75831553, 79564290, 127804174, 76748814, 109972248, 77536000, 79564804, 127804431, 113121035, 79565061, 127804945, 110888473, 127806230, 75368982, 76484630, 127806487, 127805202, 75369239, 76483602, 127805459, 75368211, 76483859, 127804688, 127803917, 127805973, 127805716, 127803660, 134217728, 33554438, 33554440, 33554439, 33554441, 33554442)),
    ((142, 143, 145, 156, 158, 415), 11, (75569408, 78518274, 77466373, 78581764, 76486913, 76487171, 127869710, 78517262, 76552448, 127869196, 112008216, 76416524, 112073497, 127870224, 78516248, 110823706, 127870481, 77399833, 110954011, 110958108, 127869967, 127869453, 134217728)),
    ((145, 175), 3, (112269592, 80614680, 114169625, 112070938)),
    ((174,), 1, (116200216,)),
    ((165, 175), 2, (114168600, 78513944, 114167833)),
    ((31,), 1, (105715480,)),
    ((69, 102), 3, (114628888, 67506456, 100930841)),
    ((172, 174, 190), 6, (111286552, 78977560, 78449176, 116201242, 79108634, 111871513)),
    ((7, 170), 3, (101322520, 68752664, 109581337)),
    ((86, 186, 187), 3, (101387544, 79042584, 111740441, 111743770)),
    ((8, 137, 153, 171), 4, (109578520, 101323801, 78252057, 109580315, 101324058, 110627100, 78252314)),
    ((20, 73, 154, 167, 170, 185, 186, 188, 201, 217, 248, 425), 4, (101389848, 79366680, 109646617, 128527383, 128527126, 128526869, 128526612, 128526355, 128526098, 33554439, 33554441, 33554440, 33554442, 33554443, 33554438)),
    ((14, 42, 58, 66, 70, 90, 138, 155, 168, 171, 184, 186, 202, 251, 426), 12, (79239169, 79304960, 80222213, 77993987, 81336322, 79239682, 83565316, 79239940, 67767553, 78186755, 112925464, 76156184, 101324555, 109842201, 128590092, 128590863, 128592405, 128592148, 128591377, 128591120, 128591634, 128590349, 128592919, 128590606, 128592662, 128591891, 134217728, 33554439, 33554438, 33554440, 33554442, 33554441)),
    ((13, 73, 75, 87, 139, 165, 172, 173, 186, 187, 188, 203, 235, 237, 253, 427), 11, (79304704, 79173637, 73013249, 80353284, 78251777, 78125314, 78125571, 101388312, 101389337, 79366169, 128657170, 128656656, 79304208, 107680282, 128656399, 79303951, 109778203, 128657941, 128655885, 128658455, 128656913, 128655628, 128657684, 128658198, 128656142, 128657427, 134217728, 33554439, 33554443, 33554440, 33554442, 33554441, 33554438)),
    ((100, 106, 108, 138, 140, 141, 156, 157, 174, 188, 189, 204, 236, 238, 252, 428), 11, (77928704, 79436036, 79370498, 78452995, 78317313, 78318341, 112986392, 112920857, 112986650, 128721678, 112985627, 81468686, 114037532, 115149830, 76285724, 128721164, 79368716, 115150087, 128722192, 128722963, 77401363, 128721421, 128723477, 128721935, 128723734, 128722706, 128722449, 128723991, 128723220, 134217728, 33554442, 33554443, 33554441, 33554440)),
    ((97, 99, 107, 109, 111, 124, 135, 147, 156, 157, 159, 165, 172, 175, 188, 221, 237, 429), 11, (81467394, 79435776, 79501316, 81596163, 79436289, 79501573, 112920344, 114102298, 79437338, 111872281, 128786700, 79434252, 115151880, 109774363, 113055260, 76352028, 128789527, 111875613, 75303703, 128788499, 128787214, 128787471, 128789013, 128787985, 128786957, 128788756, 128788242, 128789270, 128787728, 134217728, 33554439, 33554442, 33554438, 33554441, 33554443)),
    ((128, 130, 140, 142, 157, 159, 160, 162, 190, 191, 206, 222, 430), 14, (77928452, 80613123, 78583810, 79632384, 78714881, 81730053, 78584321, 80612352, 128852236, 79499788, 111220761, 81661209, 113120280, 78649858, 80613637, 79496985, 128852750, 114169354, 79630346, 114168326, 128854292, 76417044, 128854549, 111940634, 76417301, 128853007, 113118491, 128854806, 128853264, 128855063, 128853778, 128853521, 128854035, 128852493, 134217728, 33554440, 33554439, 33554441, 33554443)),
    ((129, 143, 159, 174, 190, 191, 431), 9, (77600771, 79566852, 79629312, 81664514, 77601029, 79630597, 77731841, 79629826, 112003096, 79629569, 114301977, 112002842, 128918800, 80677913, 79566352, 128917772, 114232604, 112002587, 79565324, 128918029, 128918286, 128918543, 128919057, 134217728)),
    ((174, 191, 223), 3, (117314328, 115217945, 114167322)),
    ((160, 174), 2, (115151640, 113184537)),
    ((189, 190, 195), 2, (112986136, 115217177, 115215130)),
    ((4,), 1, (100861976,)),
    ((21,), 1, (108663320,)),
    ((165, 185, 190), 4, (113318424, 79497496, 102306585, 115152410)),
    ((167,), 1, (112854808,)),
    ((136, 165), 2, (102175256, 102176537, 113052442)),
    ((137, 171, 231), 3, (111807256, 109577753, 110630682)),
    ((23, 41, 170, 189, 224), 6, (112531736, 78186264, 111740954, 111741467, 110693913, 108729116, 116200478, 109579549)),
    ((43, 58, 86, 88, 170, 171, 182, 187, 188, 202, 216, 218, 442), 13, (103422488, 78251544, 101321753, 78059801, 101388555, 108727578, 68818699, 76157722, 111744795, 77205787, 113972252, 129640210, 78318610, 129640724, 78319124, 129641238, 129640981, 129641495, 129640467, 33554442, 33554440, 33554441, 33554439, 33554438)),
    ((57, 83, 100, 106, 107, 117, 123, 138, 141, 169, 170, 171, 172, 173, 189, 219, 251, 253, 443), 12, (78059521, 78321668, 80418819, 79301381, 81271296, 79301124, 67833346, 79300610, 80354051, 111872025, 113052696, 129704204, 74057228, 129704718, 110695195, 129705489, 129706774, 110827290, 129705232, 129706003, 129707031, 129706517, 129705746, 129704461, 129704975, 129706260, 134217728, 33554441, 33554439, 33554442, 33554443, 33554440, 33554438)),
    ((60, 107, 112, 114, 116, 122, 124, 154, 172, 173, 178, 189, 190, 220, 444), 13, (82515968, 78190596, 78387459, 78452737, 80288005, 78321922, 82516739, 111937048, 79501829, 111872537, 82517249, 111937306, 129770254, 79305742, 108793627, 78322459, 108792860, 76223004, 114102813, 110889502, 129769997, 129772567, 78450967, 129772310, 78450710, 129770768, 129771282, 129771539, 129769740, 129772053, 129771796, 129770511, 129771025, 134217728, 33554443, 33554441, 33554442, 33554438, 33554439, 33554440)),
    ((140, 141, 145, 155, 157, 173, 174, 181, 183, 187, 188, 190, 191, 445), 11, (78780418, 81533441, 78387203, 79432453, 78387716, 78387968, 115150872, 78383640, 115151129, 78383897, 112795144, 112921370, 129835533, 129836047, 80483599, 129837589, 129835276, 76351765, 80482828, 129836818, 76350994, 129836561, 129837332, 76351508, 110954523, 129835790, 129837846, 129836304, 129837075, 129838103, 134217728, 33554441, 33554439, 33554438, 33554442, 33554443)),
    ((143, 158, 174, 175, 191, 207, 208, 222, 446), 12, (78977027, 78518529, 79497218, 81660928, 77928965, 79632900, 81662213, 79633152, 112069144, 81661442, 129900812, 79437068, 112335111, 81661699, 78584839, 129901583, 80549135, 81661956, 129901326, 129901840, 129902868, 77465620, 78581268, 129902097, 129902611, 77465363, 129903639, 78582039, 129903125, 77465877, 129903382, 77466134, 129902354, 129901069, 134217728, 33554441, 33554440, 33554442, 33554438, 33554443)),
    ((142, 174, 175, 177, 190, 447), 11, (80615941, 79562497, 81663235, 78584064, 78649604, 80678402, 129966348, 78513676, 112139032, 81596952, 129967633, 129966862, 113054745, 116200986, 129966605, 113051163, 79497754, 129967376, 129967119, 134217728)),
    ((1, 222, 239), 4, (100668184, 101585945, 101455386, 82708505)),
    ((181, 206, 208), 3, (114099992, 116330265, 116200730)),
    ((3, 207, 223), 3, (100796952, 114497561, 82711833, 116265498)),
    ((206, 223), 3, (112335384, 83760920, 101520921)),
    ((), 0, ()),
    ((206, 222), 4, (114497816, 80546072, 114629401, 67965721)),
    ((), 0, ()),
    ((122, 153), 2, (101256472, 113971737)),
    ((170,), 3, (114891032, 67768600, 68753176)),
    ((24, 188, 204, 216), 4, (101390105, 113969176, 109647642, 111744283)),
    ((155, 171, 187, 205), 5, (101324312, 101454361, 80479769, 112855323, 114034714, 78252568, 114037788)),
    ((45, 61, 84, 101, 134, 186, 187, 199, 201, 204, 219, 220, 221, 459), 4, (117053976, 67833624, 111875097, 130755607, 130755350, 130754836, 130754322, 130755093, 130754579, 33554443, 33554441, 33554439, 33554442, 33554438, 33554440)),
    ((128, 132, 140, 146, 156, 172, 189, 202, 205, 219, 220, 221, 222, 236, 460), 10, (83564546, 80615424, 81533185, 81598467, 80287746, 67899653, 81467908, 67899396, 81468160, 115083288, 80415493, 130819601, 101455627, 115082777, 101454599, 111937818, 111937563, 130818316, 130820115, 130820629, 130819087, 130821143, 130818830, 130819858, 130820372, 130818573, 130820886, 130819344, 134217728, 33554441, 33554438, 33554442, 33554440)),
    ((47, 62, 129, 131, 133, 139, 145, 148, 157, 173, 188, 190, 193, 197, 207, 220, 221, 222, 223, 237, 461), 11, (81664004, 81532929, 80353536, 68950531, 80481029, 80747010, 81533699, 80353794, 101518360, 117185305, 130884109, 81402125, 67965209, 101519131, 107811610, 130884880, 130884623, 81532175, 81532432, 130886165, 130886679, 130885394, 130885651, 130885908, 130883852, 130884366, 130886422, 130885137, 134217728, 33554442, 33554443, 33554440, 33554439, 33554441, 33554438)),
    ((160, 162, 174, 176, 191, 204, 207, 221, 222, 223, 238, 462), 12, (80025603, 81729536, 81664258, 82710789, 79763457, 81729797, 80681220, 82709761, 82710532, 101452824, 113449241, 81594905, 130950159, 115218202, 80747290, 81597711, 115149595, 130949388, 116265735, 130950673, 130951701, 78514453, 116265992, 130952215, 130951444, 78514967, 130951187, 130951958, 130949902, 130950930, 130950416, 130949645, 134217728, 33554438, 33554443, 33554441, 33554442)),
    ((175, 191, 206, 222, 223, 463), 12, (79829251, 83826693, 81726464, 81795844, 81726978, 80611073, 81727492, 117314584, 114100761, 81726721, 82775576, 131015438, 79562766, 81662990, 116199962, 131014924, 81662476, 131015695, 131016209, 131015181, 131015952, 134217728)),
    ((175, 205, 206, 222, 223), 7, (114629145, 67965465, 113318168, 81660184, 80878360, 101454874, 113117979, 113116700)),
    ((1,), 1, (101779224,)),
    ((5, 19, 208, 255), 4, (100928024, 101845529, 117314843, 116266778)),
    ((194, 197), 2, (115281688, 116264729)),
    ((19, 21), 2, (101845016, 101976345)),
    ((22, 164, 197, 208), 2, (102042392, 102045465, 115148314, 115148571)),
    ((23, 25, 216), 4, (102238488, 77075736, 102107161, 102503706)),
    ((9,), 2, (109452056, 75043096)),
    ((58, 187, 221, 253), 8, (114694680, 81529112, 114956314, 67832858, 110759705, 80288537, 68817434, 112858907)),
    ((170, 200), 3, (101322264, 68752408, 111741721)),
    ((205, 216, 235), 2, (112854552, 115086105, 112857882)),
    ((172, 173, 204, 220, 221), 6, (101518873, 113969690, 114039576, 113968667, 81595928, 102437660, 112923677)),
    ((131, 140, 148, 189, 204, 205, 216, 218, 221, 250, 252, 476), 9, (114034456, 115022873, 67898649, 114034971, 80414489, 102503432, 112985882, 131869719, 80548119, 131868948, 77334548, 131868434, 131869205, 131868691, 131869462, 33554441, 33554439, 33554442, 33554438, 33554443)),
    ((172, 173, 177, 181, 189, 191, 204, 206, 213, 219, 223, 241, 253, 477), 13, (81270787, 83499012, 80549888, 80484354, 81467650, 67964161, 80550149, 80484608, 101453592, 80415000, 80550659, 68883736, 131933199, 80484879, 81528577, 131933456, 131933970, 131933713, 131934741, 78448917, 131934227, 80612627, 131932942, 131935255, 78449431, 131934484, 131932428, 131932685, 131934998, 134217728, 33554442, 33554443, 33554441, 33554438, 33554440, 33554439)),
    ((174, 175, 176, 178, 190, 191, 205, 206, 207, 208, 223, 254, 478), 15, (81860866, 80746752, 80615684, 82647299, 80025857, 80616197, 83630597, 113252888, 116264473, 131997964, 80681484, 80480792, 117315082, 131999249, 80545817, 112068634, 80614426, 131998478, 132000277, 80678677, 131998735, 79563029, 132000791, 80679191, 131998992, 131998221, 132000534, 79563286, 80678934, 132000020, 134217728, 131999763, 131999506, 33554441, 33554440, 33554439, 33554443, 33554438)),
    ((174, 206, 207, 211, 255, 479), 13, (80746499, 78649345, 81660420, 82775040, 79894533, 80680962, 116202008, 132063500, 79829516, 80610828, 82709528, 132064014, 80611342, 114101017, 132064528, 115152666, 132063757, 132064785, 80612113, 132064271, 134217728)),
    ((17, 44, 207, 239), 4, (101716505, 112794648, 74190104, 116262426, 116266523)),
    ((2, 222, 255), 4, (100730904, 100731418, 116464153, 101649947, 67965977)),
    ((3, 45, 81), 2, (100797208, 100796185, 100798747, 107745818)),
    ((2, 4), 2, (100862232, 100730393)),
    ((5, 9), 4, (100928280, 110566169, 67634969, 76026649)),
    ((6, 30, 86, 244, 255), 5, (116857112, 72159768, 100996122, 107681051, 100993049, 116197148)),
    ((7, 10, 23), 4, (107552024, 101058073, 74058776, 101058586, 102106907)),
    ((6, 25), 3, (112728600, 76091672, 100993817)),
    ((24, 42, 241), 4, (109711128, 77141272, 109579801, 116197914)),
    ((25, 26, 153, 250), 6, (116791832, 83434264, 76092440, 101256729, 116923418, 76091418, 109646363, 68748827)),
    ((10, 11), 3, (107614489, 116137752, 74061336, 107616026, 67767066, 107615003, 67766043)),
    ((59, 91, 188, 238, 255), 7, (117120024, 67834392, 110893850, 114956825, 101389595, 76222746, 101389085, 78318873, 116197404, 116198174)),
    ((42, 93, 109, 124, 141, 234, 238, 255), 12, (117311257, 101583899, 116988952, 76156952, 83696667, 116197662, 110891546, 69014814, 109841180, 101321247, 111941149, 80484124, 114038304)),
    ((61, 161, 165, 185, 191, 193, 207, 222, 223, 229, 232, 235, 236, 252, 253, 254, 493), 7, (107810072, 117251353, 67966233, 111875355, 114099738, 112006684, 132983574, 132983831, 132982546, 132982803, 132983317, 132983060, 33554441, 33554438, 33554440, 33554443, 33554442, 33554439)),
    ((14, 93, 108, 127, 192, 194, 206, 210, 211, 222, 223, 224, 239, 254, 255, 494), 13, (82909444, 83826945, 82582272, 68029954, 82844165, 83827205, 82583043, 68029697, 117311512, 133047825, 82516994, 68030211, 133046797, 83696386, 111022873, 133047568, 101585671, 83823879, 111939354, 133047054, 101585414, 109842971, 83823622, 133048853, 133046540, 80611605, 133048339, 117379082, 133049110, 80611862, 133048596, 133048082, 133047311, 133049367, 134217728, 33554443, 33554440, 33554441)),
    ((13, 14, 79, 193, 207, 223, 254, 255, 495), 12, (81795584, 79698178, 69081093, 83824387, 83761412, 82708225, 83824130, 101650201, 83171845, 133112076, 101517080, 83759628, 101649690, 109909019, 107680540, 133112590, 133112847, 133113104, 133112333, 133113361, 134217728)),
    ((1, 238, 255), 3, (117311000, 100668441, 101585178)),
    ((18, 225, 238), 5, (101779480, 115874329, 68030489, 69015065, 115148826)),
    ((19,), 1, (101844760, 101845785)),
    ((4, 20), 2, (100861464, 101910809, 101910042)),
    ((6, 8, 21, 28), 6, (116988440, 82123544, 73142040, 100993562, 109580057, 101976603)),
    ((22, 239), 2, (102041112, 102041625, 117379354)),
    ((23, 27, 233), 3, (108663832, 68814872, 102107673, 108662298)),
    ((24, 229), 2, (102172440, 102565401)),
    ((8, 9, 58, 233, 255), 5, (109580568, 109581850, 117311769, 110759963, 78190107, 102238748)),
    ((9, 59, 233, 236, 244), 5, (109776152, 108596249, 102303771, 102435098, 110695964)),
    ((26, 203, 221), 5, (115940121, 75107353, 102503960, 81529368, 102372634)),
    ((75, 76, 170, 204, 235), 6, (102437912, 111810841, 77272345, 101322779, 68752923, 111809050, 77270042, 112920092)),
    ((92, 109, 205, 222), 6, (116202264, 77336344, 111940377, 101521178, 102504219, 81529627)),
    ((15, 76, 91, 236, 237, 238), 8, (114826009, 112925210, 102699288, 76288282, 102568987, 78319897, 102568476, 82642460, 115149085)),
    ((30, 126, 176, 195, 207, 210, 222, 236, 238, 239, 240, 248, 255, 510), 8, (102635275, 101586457, 82709017, 116202520, 77467672, 102634504, 134097686, 82776086, 102634247, 134097172, 81659924, 134096915, 82775315, 102633990, 134096658, 81659667, 134097943, 81659410, 82776343, 134097429, 33554441, 33554442)),
    ((95, 207, 238, 239, 245, 511), 16, (82843648, 82581761, 68096004, 83757829, 82712578, 81861378, 83368195, 68094976, 82778371, 82778625, 115678233, 69014297, 114432536, 134161423, 116071962, 68031759, 81727768, 69015322, 134161166, 107877403, 134160909, 134161937, 134160652, 134161680, 134217728)),
)

LEFT, RIGHT0, RIGHT1 = CHUNKS, 2 * CHUNKS, 3 * CHUNKS
SIZE = 384 // CHUNKS
MAX_SENDS = max(len(p[2]) for p in PLAN)
MAX_FROM = max(1, max(len(p[0]) for p in PLAN))
MESH = pl.DeviceIdType.MESH


def nt_dot(left, right):
    return lax.dot_general(left, right, (((1,), (1,)), ((), ())), preferred_element_type=jnp.float32)


def choose(index, low, high, leaf):
    if all(PLAN[i] == PLAN[low] for i in range(low, high)):
        leaf(PLAN[low])
        return
    middle = (low + high) // 2

    @pl.when(index < middle)
    def _():
        choose(index, low, middle, leaf)

    @pl.when(index >= middle)
    def _():
        choose(index, middle, high, leaf)


def kernel(upper_ref, mask_hbm, out_ref, buf, acc, mask_ref, table, origin, count, in_sem, send_sem, recv_sem):
    brow, column = lax.axis_index("brow"), lax.axis_index("bcol")
    row, half = brow // 2, brow % 2
    own = buf.at[pl.ds(0, 384)]
    load = pltpu.make_async_copy(upper_ref, own, in_sem.at[0])
    load.start()
    load_mask = pltpu.make_async_copy(mask_hbm, mask_ref, in_sem.at[1])
    load_mask.start()

    def leaf(plan):
        origins, targets, sends = plan
        count[0] = len(origins)
        count[1] = targets
        count[2] = len(sends)
        for i, v in enumerate(origins):
            origin[i] = v
        for i, v in enumerate(sends):
            table[i] = v

    choose(row * 16 + column, 0, 256, leaf)
    sends = count[2]
    barrier = pltpu.get_barrier_semaphore()

    @pl.loop(0, count[0])
    def _(i):
        v = origin[i]
        there = ((v >> 4) & 15) * 2 + (half ^ (v >> 8))
        pl.semaphore_signal(barrier, inc=1, device_id=(there, v & 15), device_id_type=MESH)

    load_mask.wait()
    load.wait()
    for i in range(3):
        for j in range(6):
            keep = mask_ref[i, j].astype(jnp.float32)
            at = (pl.ds(i * 128, 128), pl.ds(j * 128, 128))
            buf[at] = (buf[at].astype(jnp.float32) * keep).astype(jnp.bfloat16)

    @pl.when(count[1] > 0)
    def _():
        pl.semaphore_wait(barrier, count[1])

    def slot(index):
        return buf.at[pl.ds(pl.multiple_of(index * SIZE, SIZE), SIZE)]

    def copy(v, i):
        there = ((v >> 20) & 15) * 2 + (half ^ ((v >> 24) & 1))
        return pltpu.make_async_remote_copy(
            src_ref=slot(v & 255),
            dst_ref=slot((v >> 8) & 255),
            send_sem=send_sem.at[i],
            recv_sem=recv_sem.at[(v >> 8) & 255],
            device_id=(there, (v >> 16) & 15),
            device_id_type=MESH,
        )

    def arrived(index):
        pltpu.make_async_copy(slot(index), slot(index), recv_sem.at[index]).wait()

    has0 = (row == 0) | ((column >= row) & (row + column >= 16))
    has1 = (column < 15) & ((row <= 1) | ((column + 1 >= row) & (row + column >= 16)))
    here = pl.ds(pl.multiple_of(half * 384, 128), 384)
    other = pl.ds(pl.multiple_of(384 - half * 384, 128), 384)

    def rows(index):
        return buf[pl.ds(pl.multiple_of(index * SIZE, SIZE), 384), :]

    def first_term():
        right = jnp.where(row + column == 0, 0, RIGHT0)
        acc[:, here] = nt_dot(rows(0), rows(right))

        @pl.loop(0, CHUNKS)
        def _(j):
            arrived(SIB + j)

        acc[:, other] = nt_dot(rows(0), rows(SIB))

    @pl.loop(0, sends)
    def _(i):
        v = table[i]

        @pl.when((v & (1 << 25)) != 0)
        def _():
            arrived(v & 255)

        @pl.when((v & (1 << 26)) != 0)
        def _():
            copy(v, i).start()

        @pl.when((v & (1 << 27)) != 0)
        def _():
            first_term()

    @pl.when(has1)
    def _():
        left = jnp.where(column == 0, RIGHT1, LEFT)
        for columns, right in ((here, RIGHT1), (other, SIB + CHUNKS)):
            if right != RIGHT1:

                @pl.loop(0, CHUNKS)
                def _(j):
                    arrived(SIB + CHUNKS + j)

            term = nt_dot(rows(left), rows(right))

            @pl.when(has0)
            def _():
                out_ref[:, columns] = (acc[:, columns] + term).astype(jnp.bfloat16)

            @pl.when(jnp.logical_not(has0))
            def _():
                out_ref[:, columns] = term.astype(jnp.bfloat16)

    @pl.when(has0 & jnp.logical_not(has1))
    def _():
        out_ref[...] = acc[...].astype(jnp.bfloat16)

    @pl.when(jnp.logical_not(has0 | has1))
    def _():
        out_ref[...] = jnp.zeros_like(out_ref)

    @pl.loop(0, sends)
    def _(i):
        v = table[i]

        @pl.when((v & (1 << 26)) != 0)
        def _():
            copy(v, i).wait_send()


def per_device(upper_store, block_mask):
    return pl.pallas_call(
        kernel,
        out_shape=jax.ShapeDtypeStruct((384, 768), jnp.bfloat16),
        in_specs=[pl.BlockSpec(memory_space=pl.ANY)] * 2,
        out_specs=pl.BlockSpec(memory_space=pltpu.VMEM),
        scratch_shapes=[
            pltpu.VMEM((SLOTS * SIZE, 768), jnp.bfloat16),
            pltpu.VMEM((384, 768), jnp.float32),
            pltpu.SMEM((3, 6), jnp.int32),
            pltpu.SMEM((MAX_SENDS,), jnp.int32),
            pltpu.SMEM((MAX_FROM,), jnp.int32),
            pltpu.SMEM((3,), jnp.int32),
            pltpu.SemaphoreType.DMA((2,)),
            pltpu.SemaphoreType.DMA((MAX_SENDS,)),
            pltpu.SemaphoreType.DMA((SLOTS,)),
        ],
        compiler_params=pltpu.CompilerParams(
            collective_id=0, has_side_effects=True, vmem_limit_bytes=60 * 2**20
        ),
        name="cannon_steps",
    )(upper_store, block_mask)


def solution(mesh):
    spec = P("brow", "bcol")
    return jax.shard_map(per_device, mesh=mesh, in_specs=(spec, spec), out_specs=spec, check_vma=False)
```
